32 devices in a mesh: ctx: 8 (over z, y), fsdp: 4 (over x, core).
Axes of the slice: x: 2, y: 2, z: 4, core: 2. Of those that a mesh axis runs over, the one named last changes fastest.
Arguments:
- tokens: bfloat16 [8192, 1152], P(('ctx', 'fsdp')), may hold values from -6 to 6
- cotangent: bfloat16 [8192, 1152], P(('ctx', 'fsdp')), may hold values from -6 to 6
- qkv_weight: bfloat16 [1152, 1536], P(('ctx', 'fsdp')), may hold values from -0.21875 to 0.21875
- output_weight: bfloat16 [1024, 1152], P(('ctx', 'fsdp')), may hold values from -1 to 1
- expand_weight: bfloat16 [1152, 13824], P(('ctx', 'fsdp')), may hold values from -0.1875 to 0.1875
- contract_weight: bfloat16 [6912, 1152], P(('ctx', 'fsdp')), may hold values from -0.078125 to 0.078125
- norm_gains: bfloat16 [2, 1152], P(None, ('ctx', 'fsdp')), may hold values from 0.5 to 1.5
- first_qkv: float32 [1152, 1536], P(('ctx', 'fsdp')), may hold values from -160 to 160
- first_output: float32 [1024, 1152], P(('ctx', 'fsdp')), may hold values from -10 to 10
- first_expand: float32 [1152, 13824], P(('ctx', 'fsdp')), may hold values from -16 to 16
- first_contract: float32 [6912, 1152], P(('ctx', 'fsdp')), may hold values from -40 to 40
- first_gains: float32 [2, 1152], P(None, ('ctx', 'fsdp')), may hold values from -128 to 128
- second_qkv: float32 [1152, 1536], P(('ctx', 'fsdp')), may hold values from 51.2 to 204.8
- second_output: float32 [1024, 1152], P(('ctx', 'fsdp')), may hold values from 0.18432 to 0.73728
- second_expand: float32 [1152, 13824], P(('ctx', 'fsdp')), may hold values from 0.73728 to 2.94912
- second_contract: float32 [6912, 1152], P(('ctx', 'fsdp')), may hold values from 3.44064 to 13.9264
- second_gains: float32 [2, 1152], P(None, ('ctx', 'fsdp')), may hold values from 32.768 to 131.072
Outputs:
- block_out: bfloat16 [8192, 1152], P(('ctx', 'fsdp'))
- input_grad: float32 [8192, 1152], P(('ctx', 'fsdp'))
- new_qkv: float32 [1152, 1536], P(('ctx', 'fsdp'))
- new_output: float32 [1024, 1152], P(('ctx', 'fsdp'))
- new_expand: float32 [1152, 13824], P(('ctx', 'fsdp'))
- new_contract: float32 [6912, 1152], P(('ctx', 'fsdp'))
- new_gains: float32 [2, 1152], P(None, ('ctx', 'fsdp'))
- mean_qkv: float32 [1152, 1536], P(('ctx', 'fsdp'))
- mean_output: float32 [1024, 1152], P(('ctx', 'fsdp'))
- mean_expand: float32 [1152, 13824], P(('ctx', 'fsdp'))
- mean_contract: float32 [6912, 1152], P(('ctx', 'fsdp'))
- mean_gains: float32 [2, 1152], P(None, ('ctx', 'fsdp'))
- square_qkv: float32 [1152, 1536], P(('ctx', 'fsdp'))
- square_output: float32 [1024, 1152], P(('ctx', 'fsdp'))
- square_expand: float32 [1152, 13824], P(('ctx', 'fsdp'))
- square_contract: float32 [6912, 1152], P(('ctx', 'fsdp'))
- square_gains: float32 [2, 1152], P(None, ('ctx', 'fsdp'))
The draws below stay inside these ranges and needn't reach their ends.
All inputs are finite; a program needn't handle non-finite values.
Results may differ from the reference program's by a relative error of at most 0.024.
Values may be sent and summed in bfloat16 or wider, within the bound.
A program may use at most 192 MiB of HBM per device.

```python
import math
import jax
import jax.numpy as jnp
from jax import lax

D = 1152
HQ = 4
HD = 256
FF = 6912
WINDOW = 512
TOK_DEV = 256
STEP = 10
TOKENS = 8192
N_CTX = 8
N_FSDP = 4


def spiked(entries, own_key, source, target, parts, factor):
    owner, partner = [(jnp.arange(entries.shape[axis_at]) // (entries.shape[axis_at] // parts)).reshape([-1 if axis == axis_at else 1 for axis in range(entries.ndim)]) for axis_at in (source, target)]
    chosen = jax.random.permutation(own_key, parts)[partner]
    strong = (owner == chosen) | (owner == (partner + parts // 2) % parts)
    return jnp.where(strong, factor * entries, entries)


def levels(stream_key, shape, cuts, smallest, largest):
    gain, own = 1.0, jax.random.fold_in(stream_key, 6)
    for position, parts in cuts:
        heights = jnp.exp(jax.random.uniform(jax.random.fold_in(own, position), (parts,), jnp.float32, smallest / len(cuts), largest / len(cuts)))
        gain = gain * jnp.repeat(heights, shape[position] // parts).reshape([-1 if axis == position else 1 for axis in range(len(shape))])
    return gain


def scatter_about(key, shape, spread, bound, shards=(), kind=jnp.bfloat16):
    values = spread * jax.random.normal(key, shape, jnp.float32)
    if shards:
        values = values * levels(key, shape, shards, -0.22, 0.18)
    return jnp.clip(values, -bound, bound).astype(kind)


def bell_draw_with(rng, extent, width, limit, shards, heavy, kind=jnp.bfloat16):
    values = width * jax.random.normal(rng, extent, jnp.float32)
    if shards:
        values = values * levels(rng, extent, shards, -0.22, 0.18)
    return jnp.clip(spiked(values, jax.random.fold_in(rng, 3), *heavy), -limit, limit).astype(kind)


def setup_inputs(seed: int = 0) -> dict:
    arg_keys = jax.random.split(jax.random.key(seed), 18)
    return {
        "tokens": bell_draw_with(arg_keys[0], (TOKENS, D), 1.0, 6.0, ((0, 32),), (0, 1, 32, 2.75)),
        "cotangent": scatter_about(arg_keys[1], (TOKENS, D), 1.0, 6.0, ((0, 32),)),
        "qkv_weight": scatter_about(arg_keys[2], (D, HQ * HD + 2 * HD), (2 * D // 3) ** -0.5, 0.21875, ((0, 32),)),
        "output_weight": scatter_about(arg_keys[3], (HQ * HD, D), (HQ * HD // 32) ** -0.5, 1.0, ((0, 32),)),
        "expand_weight": scatter_about(arg_keys[4], (D, 2 * FF), D ** -0.5, 0.1875, ((0, 32),)),
        "contract_weight": scatter_about(arg_keys[5], (FF, D), FF ** -0.5, 0.078125, ((0, 32),)),
        "norm_gains": jnp.clip(1.0 + 0.1 * jax.random.normal(arg_keys[6], (2, D), jnp.float32), 0.5, 1.5).astype(jnp.bfloat16),
        "first_qkv": scatter_about(arg_keys[7], (D, HQ * HD + 2 * HD), (0.28 * TOKENS ** 0.5), 160.0, ((0, 32),), jnp.float32),
        "first_output": scatter_about(arg_keys[8], (HQ * HD, D), (0.017 * TOKENS ** 0.5), 10.0, ((0, 32),), jnp.float32),
        "first_expand": scatter_about(arg_keys[9], (D, 2 * FF), (0.033 * TOKENS ** 0.5), 16.0, ((0, 32),), jnp.float32),
        "first_contract": scatter_about(arg_keys[10], (FF, D), (0.072 * TOKENS ** 0.5), 40.0, ((0, 32),), jnp.float32),
        "first_gains": scatter_about(arg_keys[11], (2, D), (0.22 * TOKENS ** 0.5), 128.0, ((1, 32),), jnp.float32),
        "second_qkv": jnp.clip(jnp.exp(math.log(204.8) - 1.3862944 * jax.random.uniform(arg_keys[12], (D, HQ * HD + 2 * HD), jnp.float32) ** levels(arg_keys[12], (D, HQ * HD + 2 * HD), ((0, 32),), -0.2, 0.2)), 51.2, 204.8),
        "second_output": jnp.clip(jnp.exp(math.log(0.73728) - 1.3862944 * jax.random.uniform(arg_keys[13], (HQ * HD, D), jnp.float32) ** levels(arg_keys[13], (HQ * HD, D), ((0, 32),), -0.2, 0.2)), 0.18432, 0.73728),
        "second_expand": jnp.clip(jnp.exp(math.log(2.94912) - 1.3862944 * jax.random.uniform(arg_keys[14], (D, 2 * FF), jnp.float32) ** levels(arg_keys[14], (D, 2 * FF), ((0, 32),), -0.2, 0.2)), 0.73728, 2.94912),
        "second_contract": jnp.clip(jnp.exp(math.log(13.9264) - 1.39812884 * jax.random.uniform(arg_keys[15], (FF, D), jnp.float32) ** levels(arg_keys[15], (FF, D), ((0, 32),), -0.2, 0.2)), 3.44064, 13.9264),
        "second_gains": jnp.clip(jnp.exp(math.log(131.072) - 1.3862944 * jax.random.uniform(arg_keys[16], (2, D), jnp.float32) ** levels(arg_keys[16], (2, D), ((1, 32),), -0.2, 0.2)), 32.768, 131.072),
    }


NORM_EPSILON = 1e-06
BETA_FIRST = 0.9
BETA_SECOND = 0.999
RATE_MATRIX = 0.1
RATE_GAINS = 0.5
WEIGHT_DECAY = 0.1
ADAM_EPSILON = 1e-08
MASKED_SCORE = -1e+30
HIGHEST = lax.Precision.HIGHEST

@jax.custom_vjp
def low(v):
    return lax.optimization_barrier(v.astype(jnp.bfloat16)).astype(jnp.float32)

@jax.custom_vjp
def low_back(v):
    return v

def low_keep(v):
    return (low(v), None)

def low_pass(kept, grad):
    return (grad,)

def back_keep(v):
    return (v, None)

def back_low(kept, grad):
    return (low(grad),)
low.defvjp(low_keep, low_pass)
low_back.defvjp(back_keep, back_low)

def rms_normed(values, gain_row):
    norm_scale = lax.rsqrt(lax.optimization_barrier(jnp.mean(values * values, axis=-1, keepdims=True)) + NORM_EPSILON)
    return values * norm_scale * gain_row

def block_attention(block_index, queries, key_padded, value_padded):
    block_len = TOK_DEV * N_FSDP
    score_scale = 1.0 / math.sqrt(HD)
    offset = block_index * block_len
    row_index = lax.broadcasted_iota(jnp.int32, (block_len, WINDOW + block_len), 0)
    col_index = lax.broadcasted_iota(jnp.int32, (block_len, WINDOW + block_len), 1)
    query_block = lax.dynamic_slice_in_dim(queries, offset, block_len, 0)
    key_block = lax.dynamic_slice_in_dim(key_padded, offset, WINDOW + block_len, 0)
    value_block = lax.dynamic_slice_in_dim(value_padded, offset, WINDOW + block_len, 0)
    raw_scores = low_back(jnp.einsum('qhd,kd->hqk', query_block, key_block, precision=HIGHEST) * score_scale)
    visible = (col_index > row_index) & (col_index <= row_index + WINDOW) & (col_index + offset >= WINDOW)
    masked = jnp.where(visible[None], raw_scores, MASKED_SCORE)
    log_total = jax.nn.logsumexp(masked, axis=-1, keepdims=True)
    attn_probs = low(jnp.exp(masked - log_total))
    mixture = jnp.einsum('hqk,kd->qhd', attn_probs, value_block, precision=HIGHEST)
    return mixture.reshape(block_len, HQ * HD)

def attention(queries, key_rows, value_rows):
    padding = jnp.zeros((WINDOW, HD), jnp.float32)
    key_padded = jnp.concatenate([padding, key_rows], axis=0)
    value_padded = jnp.concatenate([padding, value_rows], axis=0)
    checked = jax.checkpoint(block_attention)

    def one_block(block_index):
        return checked(block_index, queries, key_padded, value_padded)
    blocks = lax.map(one_block, jnp.arange(N_CTX, dtype=jnp.int32))
    return blocks.reshape(TOKENS, HQ * HD)

def forward(inputs, qkv_matrix, output_matrix, expand_matrix, contract_matrix, gain_rows):
    normed = low(rms_normed(inputs, gain_rows[0]))
    projected = low_back(low(jnp.dot(normed, qkv_matrix, precision=HIGHEST)))
    queries = projected[:, :HQ * HD].reshape(TOKENS, HQ, HD)
    key_rows = projected[:, HQ * HD:HQ * HD + HD]
    value_rows = projected[:, HQ * HD + HD:]
    mixture = low_back(low(attention(queries, key_rows, value_rows)))
    branch = low_back(jnp.dot(mixture, output_matrix, precision=HIGHEST))
    middle = inputs + branch
    normed_two = low(rms_normed(middle, gain_rows[1]))
    gate_up = low_back(jnp.dot(normed_two, expand_matrix, precision=HIGHEST))
    hidden = low(jax.nn.gelu(gate_up[:, :FF], approximate=True) * gate_up[:, FF:])
    return middle + jnp.dot(hidden, contract_matrix, precision=HIGHEST)

def adamw_update(weight, gradient, first, second, rate, decay_rate):
    mean_new = BETA_FIRST * first + (1.0 - BETA_FIRST) * gradient
    square_new = BETA_SECOND * second + (1.0 - BETA_SECOND) * gradient * gradient
    mean_hat = mean_new / (1.0 - BETA_FIRST ** STEP)
    square_hat = square_new / (1.0 - BETA_SECOND ** STEP)
    updated = weight - rate * (mean_hat / (jnp.sqrt(square_hat) + ADAM_EPSILON) + decay_rate * weight)
    return (updated, mean_new, square_new)

def reference(tokens, cotangent, qkv_weight, output_weight, expand_weight, contract_weight, norm_gains, first_qkv, first_output, first_expand, first_contract, first_gains, second_qkv, second_output, second_expand, second_contract, second_gains):
    weights = (qkv_weight.astype(jnp.float32), output_weight.astype(jnp.float32), expand_weight.astype(jnp.float32), contract_weight.astype(jnp.float32), norm_gains.astype(jnp.float32))
    result, pullback = jax.vjp(forward, tokens.astype(jnp.float32), *weights)
    grads = pullback(cotangent.astype(jnp.float32))
    firsts = (first_qkv, first_output, first_expand, first_contract, first_gains)
    seconds = (second_qkv, second_output, second_expand, second_contract, second_gains)
    rates = (RATE_MATRIX, RATE_MATRIX, RATE_MATRIX, RATE_MATRIX, RATE_GAINS)
    decays = (WEIGHT_DECAY, WEIGHT_DECAY, WEIGHT_DECAY, WEIGHT_DECAY, 0.0)
    updates = [adamw_update(weights[which], grads[which + 1], firsts[which], seconds[which], rates[which], decays[which]) for which in range(5)]
    return (result.astype(jnp.bfloat16), grads[0], updates[0][0], updates[1][0], updates[2][0], updates[3][0], updates[4][0], updates[0][1], updates[1][1], updates[2][1], updates[3][1], updates[4][1], updates[0][2], updates[1][2], updates[2][2], updates[3][2], updates[4][2])
```

```python
import functools
import math

import jax
import jax.numpy as jnp
from jax import lax
from jax.experimental import pallas as pl
from jax.experimental.pallas import tpu as pltpu
from jax.sharding import PartitionSpec as P

HQ = 4
HD = 256
FF = 6912
WINDOW = 512
STEP = 10

NORM_EPSILON = 1e-06
BETA_FIRST = 0.9
BETA_SECOND = 0.999
RATE_MATRIX = 0.1
RATE_GAINS = 0.5
WEIGHT_DECAY = 0.1
ADAM_EPSILON = 1e-08
MASKED_SCORE = -1e30

F32 = jnp.float32
BF16 = jnp.bfloat16
MESH = pl.DeviceIdType.MESH
VMEM_LIMIT = 62 * 1024 * 1024


def position():
    ctx, fsdp = lax.axis_index("ctx"), lax.axis_index("fsdp")
    return ctx // 2, lax.rem(ctx, 2), fsdp // 2, lax.rem(fsdp, 2)


def device(q, y, x, c):
    return (q * 2 + y, x * 2 + c)


class Wires:
    def __init__(self, send_sems, recv_sems):
        self.send_sems, self.recv_sems = send_sems, recv_sems
        self.count = 0
        self.sent = []

    def take(self, number=1):
        first = self.count
        self.count += number
        assert self.count <= WIRES, self.count
        return first

    def copy(self, src, dst, target, index):
        return pltpu.make_async_remote_copy(
            src_ref=src,
            dst_ref=dst,
            send_sem=self.send_sems.at[index],
            recv_sem=self.recv_sems.at[index],
            device_id=target,
            device_id_type=MESH,
        )

    def send(self, src, dst, target, index, when=None):
        copy = self.copy(src, dst, target, index)
        if when is None:
            copy.start()
        else:
            pl.when(when)(copy.start)
        self.sent.append((copy, when))

    def wait(self, dst, target, index, when=None):
        copy = self.copy(dst, dst, target, index)
        if when is None:
            copy.wait_recv()
        else:
            pl.when(when)(copy.wait_recv)

    def drain(self):
        for copy, when in self.sent:
            if when is None:
                copy.wait_send()
            else:
                pl.when(when)(copy.wait_send)
        self.sent = []


WIRES = 160


def greet(n_dp, plane=True):
    q, y, x, c = position()
    barrier = pltpu.get_barrier_semaphore()
    expected = 0
    for dy in range(2):
        for dx in range(2):
            for dc in range(2):
                if dy + dx + dc == 0:
                    continue
                target = device(q, (y + dy) % 2, (x + dx) % 2, (c + dc) % 2)
                pl.semaphore_signal(barrier, inc=1, device_id=target, device_id_type=MESH)
                expected += 1

    @pl.when(q > 0)
    def _():
        pl.semaphore_signal(
            barrier, inc=1, device_id=device(q - 1, y, x, c), device_id_type=MESH
        )

    @pl.when(q < n_dp - 1)
    def _():
        pl.semaphore_signal(
            barrier, inc=1, device_id=device(q + 1, y, x, c), device_id_type=MESH
        )

    chained = (q > 0).astype(jnp.int32) + (q < n_dp - 1).astype(jnp.int32)
    pl.semaphore_wait(barrier, expected + chained)


class Chain:
    def __init__(self, wires, n_dp, own, place):
        self.wires, self.n_dp, self.own, self.place = wires, n_dp, own, place
        self.first = {way: wires.take(n_dp - 1) for way in (1, -1)}

    def valid(self, way, step):
        q = position()[0]
        return (q - 1 - step >= 0) if way == 1 else (q + 1 + step <= self.n_dp - 1)

    def send(self, way, step):
        q, y, x, c = position()
        block = q - way * step
        here = (block >= 0) & (block <= self.n_dp - 1) & (q + way >= 0) & (q + way <= self.n_dp - 1)
        inside = jnp.clip(block, 0, self.n_dp - 1)
        src = self.own if step == 0 else self.place(inside)
        self.wires.send(
            src,
            self.place(inside),
            device(jnp.clip(q + way, 0, self.n_dp - 1), y, x, c),
            self.first[way] + step,
            here,
        )

    def wait(self, way, step):
        q, y, x, c = position()
        block = jnp.clip(q - way * (step + 1), 0, self.n_dp - 1)
        self.wires.wait(
            self.place(block),
            device(jnp.clip(q + way, 0, self.n_dp - 1), y, x, c),
            self.first[way] + step,
            self.valid(way, step),
        )
        if step + 1 < self.n_dp - 1:
            self.send(way, step + 1)

    def start(self):
        self.send(1, 0)
        self.send(-1, 0)


class PlaneGather:
    def __init__(self, wires, own, buf, rows):
        self.wires, self.own, self.buf, self.rows = wires, own, buf, rows
        self.half = rows // 2
        (self.xa, self.xb, self.ya, self.yb, self.co, self.da, self.db) = (
            wires.take() for _ in range(7)
        )
        self.cx, self.cy, self.cd = (wires.take() for _ in range(3))
        q, y, x, c = position()
        self.to_x, self.to_y = device(q, y, 1 - x, c), device(q, 1 - y, x, c)
        self.to_c = device(q, y, x, 1 - c)
        self.chip = y * 2 + x
        self.chip_x, self.chip_y = y * 2 + 1 - x, (1 - y) * 2 + x
        self.chip_d = (1 - y) * 2 + 1 - x
        self.c = c

    def part(self, chip, c, which=None):
        first = pl.multiple_of((chip * 2 + c) * self.rows, self.rows)
        if which is None:
            return self.buf.at[pl.ds(first, self.rows)]
        return self.buf.at[pl.ds(first + which * self.half, self.half)]

    def start(self):
        c, half = self.c, self.half
        low, high = self.own.at[pl.ds(0, half)], self.own.at[pl.ds(half, half)]
        send = self.wires.send
        send(low, self.part(self.chip, c, 0), self.to_x, self.xa)
        send(high, self.part(self.chip, c, 1), self.to_y, self.yb)
        send(high, self.part(self.chip, c, 1), self.to_x, self.xb)
        send(low, self.part(self.chip, c, 0), self.to_y, self.ya)
        send(self.own, self.part(self.chip, c), self.to_c, self.co)

    def relay(self):
        c, wires = self.c, self.wires
        wires.wait(self.part(self.chip_x, c, 0), self.to_x, self.xa)
        wires.send(self.part(self.chip_x, c, 0), self.part(self.chip_x, c, 0), self.to_y, self.da)
        wires.wait(self.part(self.chip_y, c, 1), self.to_y, self.yb)
        wires.send(self.part(self.chip_y, c, 1), self.part(self.chip_y, c, 1), self.to_x, self.db)

    def relay_core(self):
        c, wires = self.c, self.wires
        wires.wait(self.part(self.chip_x, c, 1), self.to_x, self.xb)
        wires.send(self.part(self.chip_x, c), self.part(self.chip_x, c), self.to_c, self.cx)
        wires.wait(self.part(self.chip_y, c, 0), self.to_y, self.ya)
        wires.send(self.part(self.chip_y, c), self.part(self.chip_y, c), self.to_c, self.cy)

    def relay_last(self):
        c, wires = self.c, self.wires
        wires.wait(self.part(self.chip_d, c, 0), self.to_y, self.da)
        wires.wait(self.part(self.chip_d, c, 1), self.to_x, self.db)
        wires.send(self.part(self.chip_d, c), self.part(self.chip_d, c), self.to_c, self.cd)

    def wait_core(self):
        self.wires.wait(self.part(self.chip, 1 - self.c), self.to_c, self.co)

    def wait_core_xy(self):
        self.wires.wait(self.part(self.chip_x, 1 - self.c), self.to_c, self.cx)
        self.wires.wait(self.part(self.chip_y, 1 - self.c), self.to_c, self.cy)

    def wait_last(self):
        self.wires.wait(self.part(self.chip_d, 1 - self.c), self.to_c, self.cd)


class SlotGather:
    def __init__(self, wires, n_dp, own, buf):
        self.wires, self.n_dp, self.own, self.buf = wires, n_dp, own, buf
        q, y, x, c = position()
        self.q, self.c = q, c
        self.chip = y * 2 + x
        self.chip_x, self.chip_y = y * 2 + 1 - x, (1 - y) * 2 + x
        self.chip_d = (1 - y) * 2 + 1 - x
        self.to_x, self.to_y = device(q, y, 1 - x, c), device(q, 1 - y, x, c)
        self.to_c = device(q, y, x, 1 - c)
        self.order = [(0, -1)] + [(way, s) for s in range(n_dp - 1) for way in (1, -1)]
        self.chain = Chain(wires, n_dp, own, lambda j: self.slot(c, j, self.chip))
        self.kx, self.ky, self.kd, self.kc = (wires.take(len(self.order)) for _ in range(4))

    def slot(self, c, j, chip):
        return self.buf.at[(c * self.n_dp + j) * 4 + chip]

    def each(self):
        for rank, (way, step) in enumerate(self.order):
            if way == 0:
                yield rank, way, step, self.q, None
            else:
                block = jnp.clip(self.q - way * (step + 1), 0, self.n_dp - 1)
                yield rank, way, step, block, self.chain.valid(way, step)

    def start(self):
        self.chain.start()

    def spread(self, ranks=None):
        for rank, way, step, j, ok in self.each():
            if ranks is not None and rank not in ranks:
                continue
            if way:
                self.chain.wait(way, step)
            src = self.slot(self.c, j, self.chip) if way else self.own
            dst = self.slot(self.c, j, self.chip)
            self.wires.send(src, dst, self.to_x, self.kx + rank, ok)
            self.wires.send(src, dst, self.to_y, self.ky + rank, ok)

    def relay(self, ranks=None):
        for rank, way, step, j, ok in self.each():
            if ranks is not None and rank not in ranks:
                continue
            even = lax.rem(j, 2) == 0
            sx, sy = self.slot(self.c, j, self.chip_x), self.slot(self.c, j, self.chip_y)
            self.wires.wait(sx, self.to_x, self.kx + rank, ok)
            self.wires.send(sx, sx, self.to_y, self.kd + rank, even if ok is None else ok & even)
            self.wires.wait(sy, self.to_y, self.ky + rank, ok)
            odd = jnp.logical_not(even)
            self.wires.send(sy, sy, self.to_x, self.kd + rank, odd if ok is None else ok & odd)

    def core(self, ranks=None):
        for rank, way, step, j, ok in self.each():
            if ranks is not None and rank not in ranks:
                continue
            self.wires.wait(self.slot(self.c, j, self.chip_d), self.to_x, self.kd + rank, ok)
            four = self.buf.at[pl.ds((self.c * self.n_dp + j) * 4, 4)]
            self.wires.send(four, four, self.to_c, self.kc + rank, ok)

    def finish(self):
        for rank, way, step, j, ok in self.each():
            four = self.buf.at[pl.ds(((1 - self.c) * self.n_dp + j) * 4, 4)]
            self.wires.wait(four, self.to_c, self.kc + rank, ok)


def group_pieces(n_dp, ff_block):
    padded = -(-ff_block // 16) * 16
    width = n_dp * padded
    first = (width // 128 + 1) // 2 * 128
    pieces = []
    for group in range(8):
        for part in range(2):
            for q in range(n_dp):
                source = part * FF + ff_block * (q * 8 + group)
                begin, end = padded * q, padded * q + ff_block
                for lo, hi in ((begin, min(end, first)), (max(begin, first), end)):
                    if hi <= lo:
                        continue
                    if lo < first:
                        place = part * first + lo
                    else:
                        place = 2 * first + part * (width - first) + lo - first
                    pieces.append((group, part, source + lo - begin, hi - lo, place))
    return padded, width, first, pieces


def gather_kernel(
    n_dp,
    gains_ref,
    qkv_ref,
    output_ref,
    expand_ref,
    contract_ref,
    cotangent_ref,
    gains_all,
    qkv_all,
    output_all,
    expand_use,
    contract_use,
    cotangent_all,
    pieces_out,
    pieces_in,
    rows_own,
    contract_own,
    local_sems,
    send_sems,
    recv_sems,
):
    wires = Wires(send_sems, recv_sems)
    q, y, x, c = position()
    chip = y * 2 + x
    me = chip * 2 + c
    shard = expand_ref.shape[0]
    ff_block = contract_ref.shape[0]
    padded, width, first, pieces = group_pieces(n_dp, ff_block)
    plane_rows = 8 * shard
    greet(n_dp)
    gathers = [
        SlotGather(wires, n_dp, gains_ref, gains_all),
        SlotGather(wires, n_dp, qkv_ref, qkv_all),
        SlotGather(wires, n_dp, output_ref, output_all),
    ]
    for gather in gathers:
        gather.start()
    local = []
    for index, gather in enumerate(gathers):
        copy = pltpu.make_async_copy(
            gather.own, gather.slot(c, q, chip), local_sems.at[index]
        )
        copy.start()
        local.append(copy)
    for gather in gathers:
        gather.spread((0,))
    contract_own[0:ff_block, :] = contract_ref[...]
    if padded > ff_block:
        contract_own[ff_block:, :] = jnp.zeros((padded - ff_block, contract_ref.shape[1]), BF16)

    def contract_place(j):
        return contract_use.at[pl.ds(pl.multiple_of(j * padded, 16), padded)]

    def expand_place(j):
        return expand_use.at[pl.ds(pl.multiple_of(j * plane_rows, 16), plane_rows)]

    contract_chain = Chain(wires, n_dp, contract_own, contract_place)
    contract_chain.start()
    copy = pltpu.make_async_copy(contract_own, contract_place(q), local_sems.at[3])
    copy.start()
    local.append(copy)
    pieces_out[...] = jnp.zeros_like(pieces_out)
    for group, part, source, size, place in pieces:
        pieces_out[group, :, place : place + size] = expand_ref[:, source : source + size]
    index = wires.take(7)
    number = 0
    arrivals = []
    for dy in range(2):
        for dx in range(2):
            for dc in range(2):
                if dy + dx + dc == 0:
                    continue
                ty, tx, tc = (y + dy) % 2, (x + dx) % 2, (c + dc) % 2
                other = (ty * 2 + tx) * 2 + tc
                target = device(q, ty, tx, tc)
                wires.send(pieces_out.at[other], pieces_in.at[me], target, index + number)
                arrivals.append((pieces_in.at[other], target, index + number))
                number += 1
    copy = pltpu.make_async_copy(pieces_out.at[me], pieces_in.at[me], local_sems.at[4])
    copy.start()
    cotangent = PlaneGather(wires, cotangent_ref, cotangent_all, cotangent_ref.shape[0])
    ranks = len(gathers[0].order)
    for gather in gathers:
        gather.spread((1, 2))
    for gather in gathers:
        gather.relay((0,))
    for arrival in arrivals:
        wires.wait(*arrival)
    copy.wait()
    for group in range(8):
        rows_own[shard * group : shard * (group + 1), :] = pieces_in[group]
    expand_chain = Chain(wires, n_dp, rows_own, expand_place)
    expand_chain.start()
    copy = pltpu.make_async_copy(rows_own, expand_place(q), local_sems.at[5])
    copy.start()
    local.append(copy)
    cotangent.start()
    mine = pltpu.make_async_copy(
        cotangent_ref, cotangent.part(chip, c), local_sems.at[6]
    )
    mine.start()
    local.append(mine)
    for gather in gathers:
        gather.spread(range(3, ranks))
    for gather in gathers:
        gather.relay(range(1, ranks))
    for copy in local:
        copy.wait()
    for gather in gathers:
        gather.core()
    cotangent.relay()
    for step in range(n_dp - 1):
        for way in (1, -1):
            contract_chain.wait(way, step)
    cotangent.relay_core()
    cotangent.relay_last()
    for step in range(n_dp - 1):
        for way in (1, -1):
            expand_chain.wait(way, step)
    for gather in gathers:
        gather.finish()
    cotangent.wait_core()
    cotangent.wait_core_xy()
    cotangent.wait_last()
    wires.drain()


def gather_weights(n_dp, gains, qkv, output, expand, contract, cotangent):
    n_all = 8 * n_dp
    shard, ff_block = expand.shape[0], contract.shape[0]
    padded, width, first, pieces = group_pieces(n_dp, ff_block)
    features = qkv.shape[0] * n_all
    hbm, vmem = pl.BlockSpec(memory_space=pl.ANY), pl.BlockSpec(memory_space=pltpu.VMEM)
    shapes = (
        ((n_all, *gains.shape), F32),
        ((n_all, *qkv.shape), BF16),
        ((n_all, *output.shape), BF16),
        ((features, 2 * width), BF16),
        ((width, features), BF16),
        ((8 * cotangent.shape[0], features), BF16),
    )
    return pl.pallas_call(
        functools.partial(gather_kernel, n_dp),
        out_shape=[jax.ShapeDtypeStruct(*s) for s in shapes],
        in_specs=[hbm, hbm, hbm, vmem, vmem, hbm],
        out_specs=[hbm] * 6,
        scratch_shapes=[
            pltpu.VMEM((8, shard, 2 * width), BF16),
            pltpu.VMEM((8, shard, 2 * width), BF16),
            pltpu.VMEM((8 * shard, 2 * width), BF16),
            pltpu.VMEM((padded, features), BF16),
            pltpu.SemaphoreType.DMA((8,)),
            pltpu.SemaphoreType.DMA((WIRES,)),
            pltpu.SemaphoreType.DMA((WIRES,)),
        ],
        compiler_params=pltpu.CompilerParams(
            collective_id=0, has_side_effects=True, vmem_limit_bytes=VMEM_LIMIT
        ),
        name="gather_weights",
    )(gains, qkv, output, expand, contract, cotangent)


def gelu_parts(u):
    k = math.sqrt(2.0 / math.pi)
    square = u * u
    t = jnp.tanh(k * u * (1.0 + 0.044715 * square))
    half = 0.5 * (1.0 + t)
    slope = half + 0.5 * u * (1.0 - t * t) * (k * (1.0 + (3.0 * 0.044715) * square))
    return u * half, slope


def dot_nt(a, b):
    return lax.dot_general(a, b, (((1,), (1,)), ((), ())), preferred_element_type=F32)


def dot_tn(a, b):
    return lax.dot_general(a, b, (((0,), (0,)), ((), ())), preferred_element_type=F32)


def dot_nn(a, b):
    return jnp.dot(a, b, preferred_element_type=F32)


class ChainSum:
    def __init__(self, wires, n_dp, own, landing, stage, local_sem):
        self.wires, self.n_dp, self.own, self.landing = wires, n_dp, own, landing
        self.stage, self.local_sem = stage, local_sem
        self.first = {way: wires.take(n_dp) for way in (1, -1)}

    def slot(self, way, j):
        q = position()[0]
        return self.landing.at[jnp.where(j == q, self.n_dp, j)] if way == -1 else self.landing.at[j]

    def add(self, way, j, when):
        q, y, x, c = position()
        target = device(jnp.clip(q - way, 0, self.n_dp - 1), y, x, c)
        self.wires.wait(self.slot(way, j), target, self.first[way] + j, when)

        @pl.when(when)
        def _():
            copy = pltpu.make_async_copy(self.slot(way, j), self.stage, self.local_sem)
            copy.start()
            copy.wait()
            own = self.own(j)
            own[...] = (own[...].astype(F32) + self.stage[...].astype(F32)).astype(BF16)

    def step(self, way, j, when=None):
        q, y, x, c = position()
        last = self.n_dp - 1
        ahead = (j > q) if way == 1 else (j < q)
        behind = (q > 0) if way == 1 else (q < last)
        if when is not None:
            ahead = ahead & when
        self.add(way, j, ahead & behind)
        nearer = jnp.clip(q + way, 0, last)
        if way == 1:
            dst = self.landing.at[j]
        else:
            dst = self.landing.at[jnp.where(nearer == j, self.n_dp, j)]
        self.wires.send(self.own(j), dst, device(nearer, y, x, c), self.first[way] + j, ahead)

    def pass_on(self, way):
        order = range(self.n_dp - 1, -1, -1) if way == 1 else range(self.n_dp)
        for j in order:
            self.step(way, j)

    def forward(self):
        q = position()[0]
        near_left = q < self.n_dp // 2
        near_right = jnp.logical_not(near_left)
        for j in range(self.n_dp - 1, -1, -1):
            self.step(1, j, near_left)
        for j in range(self.n_dp):
            self.step(-1, j, near_right)
        for j in range(self.n_dp):
            self.step(-1, j, near_left)
        for j in range(self.n_dp - 1, -1, -1):
            self.step(1, j, near_right)

    def collect(self):
        q = position()[0]
        for way in (1, -1):
            behind = (q > 0) if way == 1 else (q < self.n_dp - 1)
            y, x, c = position()[1:]
            target = device(jnp.clip(q - way, 0, self.n_dp - 1), y, x, c)
            slot = self.landing.at[q] if way == 1 else self.landing.at[self.n_dp]
            self.wires.wait(slot, target, self.first[way] + q, behind)

            @pl.when(behind)
            def _(slot=slot):
                copy = pltpu.make_async_copy(slot, self.stage, self.local_sem)
                copy.start()
                copy.wait()
                own = self.own(q)
                own[...] = (own[...].astype(F32) + self.stage[...].astype(F32)).astype(BF16)


class PlaneSum:
    def __init__(self, wires, buf, rows, cores, diag, sides):
        self.wires, self.buf, self.rows = wires, buf, rows
        self.half = rows // 2
        self.cores, self.diag, self.sides = cores, diag, sides
        self.kc = wires.take(4)
        self.kdx, self.kdy = wires.take(), wires.take()
        self.kxa, self.kxb, self.kya, self.kyb = (wires.take() for _ in range(4))
        q, y, x, c = position()
        self.to_x, self.to_y = device(q, y, 1 - x, c), device(q, 1 - y, x, c)
        self.to_c = device(q, y, x, 1 - c)
        self.c = c
        self.chips = [
            y * 2 + x,
            y * 2 + 1 - x,
            (1 - y) * 2 + x,
            (1 - y) * 2 + 1 - x,
        ]

    def part(self, chip, c, which=None):
        first = pl.multiple_of((chip * 2 + c) * self.rows, self.rows)
        if which is None:
            return self.buf.at[pl.ds(first, self.rows)]
        return self.buf.at[pl.ds(first + which * self.half, self.half)]

    def send_core(self, k):
        self.wires.send(
            self.part(self.chips[k], 1 - self.c), self.cores.at[k], self.to_c, self.kc + k
        )

    def add_core(self, k):
        self.wires.wait(self.cores.at[k], self.to_c, self.kc + k)
        mine = self.part(self.chips[k], self.c)
        mine[...] = (mine[...].astype(F32) + self.cores[k].astype(F32)).astype(BF16)

    def send_first(self):
        wires, half = self.wires, self.half
        wires.send(self.part(self.chips[3], self.c, 0), self.diag.at[0], self.to_x, self.kdx)
        wires.send(self.part(self.chips[3], self.c, 1), self.diag.at[1], self.to_y, self.kdy)
        wires.send(
            self.part(self.chips[1], self.c, 0),
            self.sides.at[0, pl.ds(0, half)],
            self.to_x,
            self.kxa,
        )
        wires.send(
            self.part(self.chips[2], self.c, 1),
            self.sides.at[1, pl.ds(half, half)],
            self.to_y,
            self.kyb,
        )

    def send_second(self):
        wires, half = self.wires, self.half
        wires.wait(self.diag.at[0], self.to_x, self.kdx)
        mine = self.part(self.chips[2], self.c, 0)
        mine[...] = (mine[...].astype(F32) + self.diag[0].astype(F32)).astype(BF16)
        wires.send(mine, self.sides.at[1, pl.ds(0, half)], self.to_y, self.kya)
        wires.wait(self.diag.at[1], self.to_y, self.kdy)
        mine = self.part(self.chips[1], self.c, 1)
        mine[...] = (mine[...].astype(F32) + self.diag[1].astype(F32)).astype(BF16)
        wires.send(mine, self.sides.at[0, pl.ds(half, half)], self.to_x, self.kxb)

    def collect(self, out):
        wires, half = self.wires, self.half
        wires.wait(self.sides.at[0, pl.ds(0, half)], self.to_x, self.kxa)
        wires.wait(self.sides.at[1, pl.ds(half, half)], self.to_y, self.kyb)
        wires.wait(self.sides.at[1, pl.ds(0, half)], self.to_y, self.kya)
        wires.wait(self.sides.at[0, pl.ds(half, half)], self.to_x, self.kxb)
        mine = self.part(self.chips[0], self.c)
        out[...] = (
            mine[...].astype(F32) + self.sides[0].astype(F32) + self.sides[1].astype(F32)
        )


def ffn_kernel(
    n_dp,
    ff_block,
    normed_ref,
    cotangent_all,
    expand_use,
    contract_use,
    branch_out,
    grad_normed_out,
    grad_contract_out,
    grad_expand_out,
    land_a,
    land_b,
    land_c,
    tokens,
    cotangent,
    expand_a,
    expand_b,
    contract,
    hidden,
    grad_gate_up,
    branch,
    grad_normed,
    sum_a,
    sum_b,
    sum_c,
    stage_a,
    stage_b,
    stage_c,
    cores,
    diag,
    sides,
    pieces_out,
    pieces_in,
    local_sems,
    send_sems,
    recv_sems,
):
    wires = Wires(send_sems, recv_sems)
    q, y, x, c = position()
    chip = y * 2 + x
    me = chip * 2 + c
    rows = normed_ref.shape[0]
    features = normed_ref.shape[1]
    shard = features // (8 * n_dp)
    plane_rows = 8 * shard
    padded, width, first, pieces = group_pieces(n_dp, ff_block)
    rest = width - first
    loads = [
        (expand_use.at[:, pl.ds(0, 2 * first)], expand_a),
        (contract_use, contract),
        (cotangent_all, cotangent),
        (expand_use.at[:, pl.ds(2 * first, 2 * rest)], expand_b),
    ]
    local = []
    for index, (src, dst) in enumerate(loads):
        copy = pltpu.make_async_copy(src, dst, local_sems.at[index])
        copy.start()
        local.append(copy)
    greet(n_dp)
    gather = PlaneGather(wires, normed_ref, tokens, rows)
    gather.start()
    mine = pltpu.make_async_copy(normed_ref, gather.part(chip, c), local_sems.at[4])
    mine.start()
    gather.relay()
    gather.relay_core()
    gather.relay_last()
    gather.wait_core()
    gather.wait_core_xy()
    gather.wait_last()
    mine.wait()
    for copy in local:
        copy.wait()

    def chunk(expand, begin, size, fresh):
        inner = contract.at[pl.ds(begin, size)]

        def tile(index, carry):
            here = pl.ds(pl.multiple_of(index * rows, rows), rows)
            gate_up = dot_nn(tokens[here, :], expand[...])
            grad_hidden = dot_nt(cotangent[here, :], inner[...])
            gate, up = gate_up[:, :size], gate_up[:, size:]
            activated, slope = gelu_parts(gate)
            low = (activated * up).astype(BF16)
            hidden[here, :size] = low
            grad_gate_up[here, :size] = (grad_hidden * up * slope).astype(BF16)
            grad_gate_up[here, size : 2 * size] = (grad_hidden * activated).astype(BF16)
            out = dot_nn(low, inner[...])
            back = dot_nt(grad_gate_up[here, : 2 * size], expand[...])
            if not fresh:
                out = out + branch[here, :].astype(F32)
                back = back + grad_normed[here, :].astype(F32)
            branch[here, :] = out.astype(BF16)
            grad_normed[here, :] = back.astype(BF16)
            return carry

        lax.fori_loop(0, 8, tile, 0)

    third = features // 3

    def weight_grads(begin, size, sum_rows):
        def contract_tile(index, carry):
            here = pl.ds(pl.multiple_of(index * 128, 128), 128)
            there = pl.ds(pl.multiple_of(begin + index * 128, 128), 128)
            sum_c[there, :] = dot_tn(hidden[:, here], cotangent[...]).astype(BF16)
            return carry

        lax.fori_loop(0, size // 128, contract_tile, 0)

        def expand_tile(index, carry):
            here = pl.ds(pl.multiple_of(index * third, third), third)
            sum_rows[here, :] = dot_tn(tokens[:, here], grad_gate_up[:, : 2 * size]).astype(BF16)
            return carry

        lax.fori_loop(0, 3, expand_tile, 0)

    chain_a = ChainSum(
        wires,
        n_dp,
        lambda j: sum_a.at[pl.ds(pl.multiple_of(j * plane_rows, 16), plane_rows)],
        land_a,
        stage_a,
        local_sems.at[5],
    )
    chain_b = ChainSum(
        wires,
        n_dp,
        lambda j: sum_b.at[pl.ds(pl.multiple_of(j * plane_rows, 16), plane_rows)],
        land_b,
        stage_b,
        local_sems.at[6],
    )
    chain_c = ChainSum(
        wires,
        n_dp,
        lambda j: sum_c.at[pl.ds(pl.multiple_of(j * padded, 16), padded)],
        land_c,
        stage_c,
        local_sems.at[7],
    )
    chunk(expand_a, 0, first, True)
    weight_grads(0, first, sum_a)
    chain_a.forward()
    chunk(expand_b, first, rest, False)
    sums = [
        PlaneSum(wires, buf, rows, cores.at[i], diag.at[i], sides.at[i])
        for i, buf in enumerate((branch, grad_normed))
    ]
    for k in (3, 1, 2, 0):
        for one in sums:
            one.send_core(k)
    weight_grads(first, rest, sum_b)
    chain_b.forward()
    chain_c.forward()
    for k in (3, 1, 2, 0):
        for one in sums:
            one.add_core(k)
    for one in sums:
        one.send_first()
    for one in sums:
        one.send_second()
    chain_a.collect()
    chain_b.collect()
    chain_c.collect()
    grad_contract_out[...] = chain_c.own(q)[0:ff_block, :].astype(F32)
    for begin, size, chain, stage in (
        (0, 2 * first, chain_a, stage_a),
        (2 * first, 2 * rest, chain_b, stage_b),
    ):
        stage[...] = chain.own(q)[...]
        for group in range(8):
            pieces_out[group, :, begin : begin + size] = stage[
                shard * group : shard * (group + 1), :
            ]
    index = wires.take(7)
    number = 0
    arrivals = []
    for dy in range(2):
        for dx in range(2):
            for dc in range(2):
                if dy + dx + dc == 0:
                    continue
                ty, tx, tc = (y + dy) % 2, (x + dx) % 2, (c + dc) % 2
                other = (ty * 2 + tx) * 2 + tc
                target = device(q, ty, tx, tc)
                wires.send(pieces_out.at[other], pieces_in.at[me], target, index + number)
                arrivals.append((pieces_in.at[other], target, index + number))
                number += 1
    copy = pltpu.make_async_copy(pieces_out.at[me], pieces_in.at[me], local_sems.at[4])
    copy.start()
    sums[0].collect(branch_out)
    sums[1].collect(grad_normed_out)
    for arrival in arrivals:
        wires.wait(*arrival)
    copy.wait()
    for group, part, source, size, place in pieces:
        grad_expand_out[:, source : source + size] = pieces_in[group, :, place : place + size]
    wires.drain()


def feed_forward(n_dp, ff_block, normed, cotangent_all, expand_use, contract_use):
    rows, features = normed.shape
    shard = features // (8 * n_dp)
    plane_rows = 8 * shard
    padded, width, first, pieces = group_pieces(n_dp, ff_block)
    rest = width - first
    hbm, vmem = pl.BlockSpec(memory_space=pl.ANY), pl.BlockSpec(memory_space=pltpu.VMEM)
    outs = [
        ((rows, features), F32),
        ((rows, features), F32),
        ((ff_block, features), F32),
        ((shard, 2 * FF), BF16),
        ((n_dp + 1, plane_rows, 2 * first), BF16),
        ((n_dp + 1, plane_rows, 2 * rest), BF16),
        ((n_dp + 1, padded, features), BF16),
    ]
    results = pl.pallas_call(
        functools.partial(ffn_kernel, n_dp, ff_block),
        out_shape=[jax.ShapeDtypeStruct(*s) for s in outs],
        in_specs=[hbm] * 4,
        out_specs=[vmem] * 4 + [hbm] * 3,
        scratch_shapes=[
            pltpu.VMEM((8 * rows, features), BF16),
            pltpu.VMEM((8 * rows, features), BF16),
            pltpu.VMEM((features, 2 * first), BF16),
            pltpu.VMEM((features, 2 * rest), BF16),
            pltpu.VMEM((width, features), BF16),
            pltpu.VMEM((8 * rows, first), BF16),
            pltpu.VMEM((8 * rows, 2 * first), BF16),
            pltpu.VMEM((8 * rows, features), BF16),
            pltpu.VMEM((8 * rows, features), BF16),
            pltpu.VMEM((features, 2 * first), BF16),
            pltpu.VMEM((features, 2 * rest), BF16),
            pltpu.VMEM((width, features), BF16),
            pltpu.VMEM((plane_rows, 2 * first), BF16),
            pltpu.VMEM((plane_rows, 2 * rest), BF16),
            pltpu.VMEM((padded, features), BF16),
            pltpu.VMEM((2, 4, rows, features), BF16),
            pltpu.VMEM((2, 2, rows // 2, features), BF16),
            pltpu.VMEM((2, 2, rows, features), BF16),
            pltpu.VMEM((8, shard, 2 * width), BF16),
            pltpu.VMEM((8, shard, 2 * width), BF16),
            pltpu.SemaphoreType.DMA((8,)),
            pltpu.SemaphoreType.DMA((WIRES,)),
            pltpu.SemaphoreType.DMA((WIRES,)),
        ],
        compiler_params=pltpu.CompilerParams(
            collective_id=1, has_side_effects=True, vmem_limit_bytes=VMEM_LIMIT
        ),
        name="feed_forward",
    )(normed, cotangent_all, expand_use, contract_use)
    return results[:4]


class SlotSum:
    def __init__(self, wires, n_dp, buf, cores, diag, sides, landing):
        self.wires, self.n_dp, self.buf = wires, n_dp, buf
        self.cores, self.diag, self.sides, self.landing = cores, diag, sides, landing
        self.low = n_dp // 2
        q, y, x, c = position()
        self.q, self.c = q, c
        self.chips = [y * 2 + x, y * 2 + 1 - x, (1 - y) * 2 + x, (1 - y) * 2 + 1 - x]
        self.to_x, self.to_y = device(q, y, 1 - x, c), device(q, 1 - y, x, c)
        self.to_c = device(q, y, x, 1 - c)
        self.kc = wires.take(4)
        self.kdx, self.kdy, self.kx0, self.kx1, self.ky0, self.ky1 = (
            wires.take() for _ in range(6)
        )
        self.first = {way: wires.take(n_dp) for way in (1, -1)}

    def at(self, c, chip, j, count):
        return self.buf.at[pl.ds((c * 4 + chip) * self.n_dp + j, count)]

    def accumulate(self, mine, other):
        mine[...] = (mine[...].astype(F32) + other[...].astype(F32)).astype(mine.dtype)

    def send_core(self):
        for k in (3, 1, 2, 0):
            src = self.at(1 - self.c, self.chips[k], 0, self.n_dp)
            self.wires.send(src, self.cores.at[k], self.to_c, self.kc + k)

    def add_core(self, k):
        self.wires.wait(self.cores.at[k], self.to_c, self.kc + k)
        self.accumulate(self.at(self.c, self.chips[k], 0, self.n_dp), self.cores.at[k])

    def send_first(self):
        low, high, c, wires = self.low, self.n_dp - self.low, self.c, self.wires
        self.add_core(3)
        wires.send(self.at(c, self.chips[3], 0, low), self.diag.at[pl.ds(0, low)], self.to_x, self.kdx)
        wires.send(self.at(c, self.chips[3], low, high), self.diag.at[pl.ds(low, high)], self.to_y, self.kdy)
        self.add_core(1)
        wires.send(self.at(c, self.chips[1], 0, low), self.sides.at[0, pl.ds(0, low)], self.to_x, self.kx0)
        self.add_core(2)
        wires.send(self.at(c, self.chips[2], low, high), self.sides.at[1, pl.ds(low, high)], self.to_y, self.ky1)
        self.add_core(0)

    def send_second(self):
        low, high, c, wires = self.low, self.n_dp - self.low, self.c, self.wires
        wires.wait(self.diag.at[pl.ds(0, low)], self.to_x, self.kdx)
        mine = self.at(c, self.chips[2], 0, low)
        self.accumulate(mine, self.diag.at[pl.ds(0, low)])
        wires.send(mine, self.sides.at[1, pl.ds(0, low)], self.to_y, self.ky0)
        wires.wait(self.diag.at[pl.ds(low, high)], self.to_y, self.kdy)
        mine = self.at(c, self.chips[1], low, high)
        self.accumulate(mine, self.diag.at[pl.ds(low, high)])
        wires.send(mine, self.sides.at[0, pl.ds(low, high)], self.to_x, self.kx1)

    def gather_sides(self):
        low, high, wires = self.low, self.n_dp - self.low, self.wires
        wires.wait(self.sides.at[0, pl.ds(0, low)], self.to_x, self.kx0)
        wires.wait(self.sides.at[1, pl.ds(low, high)], self.to_y, self.ky1)
        wires.wait(self.sides.at[1, pl.ds(0, low)], self.to_y, self.ky0)
        wires.wait(self.sides.at[0, pl.ds(low, high)], self.to_x, self.kx1)
        mine = self.at(self.c, self.chips[0], 0, self.n_dp)
        mine[...] = (
            mine[...].astype(F32) + self.sides[0].astype(F32) + self.sides[1].astype(F32)
        ).astype(mine.dtype)

    def own(self, j):
        return self.buf.at[(self.c * 4 + self.chips[0]) * self.n_dp + j]

    def step(self, way, j, when):
        q, y, x, c = position()
        last = self.n_dp - 1
        ahead = ((j > q) if way == 1 else (j < q)) & when
        behind = (q > 0) if way == 1 else (q < last)
        target = device(jnp.clip(q - way, 0, last), y, x, c)
        self.wires.wait(self.landing.at[j], target, self.first[way] + j, ahead & behind)

        @pl.when(ahead & behind)
        def _():
            self.accumulate(self.own(j), self.landing.at[j])

        nearer = jnp.clip(q + way, 0, last)
        dst = self.landing.at[j if way == 1 else jnp.where(nearer == j, self.n_dp, j)]
        self.wires.send(self.own(j), dst, device(nearer, y, x, c), self.first[way] + j, ahead)

    def forward(self):
        near_left = self.q < self.n_dp // 2
        near_right = jnp.logical_not(near_left)
        for j in range(self.n_dp - 1, -1, -1):
            self.step(1, j, near_left)
        for j in range(self.n_dp):
            self.step(-1, j, near_right)
        for j in range(self.n_dp):
            self.step(-1, j, near_left)
        for j in range(self.n_dp - 1, -1, -1):
            self.step(1, j, near_right)

    def collect(self, out):
        q, y, x, c = position()
        total = self.own(q)[...].astype(F32)
        out[...] = total
        for way in (1, -1):
            behind = (q > 0) if way == 1 else (q < self.n_dp - 1)
            target = device(jnp.clip(q - way, 0, self.n_dp - 1), y, x, c)
            slot = self.landing.at[q] if way == 1 else self.landing.at[self.n_dp]
            self.wires.wait(slot, target, self.first[way] + q, behind)

            @pl.when(behind)
            def _(slot=slot):
                out[...] = out[...] + slot[...].astype(F32)


def slot_sum_scratch(n_dp, block, dtype):
    low, high = n_dp // 2, n_dp - n_dp // 2
    return [
        pltpu.VMEM((8 * n_dp, *block), dtype),
        pltpu.VMEM((4, n_dp, *block), dtype),
        pltpu.VMEM((n_dp, *block), dtype),
        pltpu.VMEM((2, n_dp, *block), dtype),
        pltpu.VMEM((n_dp + 1, *block), dtype),
    ]


def sums_kernel(n_dp, qkv_ref, output_ref, gains_ref, qkv_out, output_out, gains_out, *scratch):
    send_sems, recv_sems = scratch[-2:]
    wires = Wires(send_sems, recv_sems)
    greet(n_dp)
    sums = [SlotSum(wires, n_dp, *scratch[5 * i : 5 * i + 5]) for i in range(3)]
    refs, outs = (output_ref, gains_ref, qkv_ref), (output_out, gains_out, qkv_out)
    for one, ref in zip(sums, refs):
        block = ref.shape[0] // (8 * n_dp)
        for j in range(n_dp):
            for chip in range(4):
                for c in range(2):
                    d = (j * 4 + chip) * 2 + c
                    one.buf[(c * 4 + chip) * n_dp + j] = ref[block * d : block * (d + 1), :].astype(
                        one.buf.dtype
                    )
        one.send_core()
    for one in sums:
        one.send_first()
    for one in sums:
        one.send_second()
    for one in sums:
        one.gather_sides()
        one.forward()
    for one, out in zip(sums, outs):
        one.collect(out)
    wires.drain()


def attention_sums(n_dp, grad_qkv, grad_output, grad_gains):
    n_all = 8 * n_dp
    features = grad_qkv.shape[0]
    share = features // n_all
    gains = grad_gains.reshape(2, n_all, share).transpose(1, 0, 2)
    gains = jnp.pad(gains, ((0, 0), (0, 6), (0, 128 - share))).reshape(n_all * 8, 128)
    blocks = [
        ((grad_output.shape[0] // n_all, features), BF16),
        ((8, 128), F32),
        ((share, grad_qkv.shape[1]), BF16),
    ]
    scratch = [entry for block in blocks for entry in slot_sum_scratch(n_dp, *block)]
    vmem = pl.BlockSpec(memory_space=pltpu.VMEM)
    qkv, output, gains = pl.pallas_call(
        functools.partial(sums_kernel, n_dp),
        out_shape=[jax.ShapeDtypeStruct(blocks[i][0], F32) for i in (2, 0, 1)],
        in_specs=[vmem] * 3,
        out_specs=[vmem] * 3,
        scratch_shapes=scratch
        + [pltpu.SemaphoreType.DMA((WIRES,)), pltpu.SemaphoreType.DMA((WIRES,))],
        compiler_params=pltpu.CompilerParams(
            collective_id=2, has_side_effects=True, vmem_limit_bytes=VMEM_LIMIT
        ),
        name="attention_sums",
    )(grad_qkv, grad_output, gains)
    return qkv, output, gains[:2, :share]


def passed_along(block, axis, distance):
    devices = range(lax.axis_size(axis))
    route = [(i - distance, i) for i in devices if i - distance in devices]
    return lax.ppermute(block, axis, route)


def norm_forward(values, gain_row):
    norm_scale = lax.rsqrt(jnp.mean(values * values, axis=-1, keepdims=True) + NORM_EPSILON)
    return (values * norm_scale * gain_row, norm_scale)


def norm_backward(values, norm_scale, gain_row, grad_normed):
    gain_grad = jnp.sum(grad_normed * values * norm_scale, axis=0)
    scaled = grad_normed * gain_row
    cubed = norm_scale * norm_scale * norm_scale
    grad_values = norm_scale * scaled - values * cubed * jnp.mean(
        scaled * values, axis=-1, keepdims=True
    )
    return (grad_values, gain_grad)


def adamw_update(weight, gradient, first, second, rate, decay_rate):
    mean_new = BETA_FIRST * first + (1.0 - BETA_FIRST) * gradient
    square_new = BETA_SECOND * second + (1.0 - BETA_SECOND) * gradient * gradient
    mean_hat = mean_new / (1.0 - BETA_FIRST**STEP)
    square_hat = square_new / (1.0 - BETA_SECOND**STEP)
    updated = weight - rate * (
        mean_hat / (jnp.sqrt(square_hat) + ADAM_EPSILON) + decay_rate * weight
    )
    return (updated, mean_new, square_new)


def in_order(slots, n_dp):
    return slots.reshape(2, n_dp, 4, *slots.shape[1:]).transpose(
        1, 2, 0, *range(3, slots.ndim + 2)
    )


def shards_kernels(
    tokens,
    cotangent,
    qkv_weight,
    output_weight,
    expand_weight,
    contract_weight,
    norm_gains,
    first_qkv,
    first_output,
    first_expand,
    first_contract,
    first_gains,
    second_qkv,
    second_output,
    second_expand,
    second_contract,
    second_gains,
):
    tok_dev, features = tokens.shape
    n_fsdp = lax.axis_size("fsdp")
    n_ctx = lax.axis_size("ctx")
    n_dp = n_ctx // 2
    ff_block = contract_weight.shape[0]
    score_scale = 1.0 / math.sqrt(HD)
    fsdp_index = lax.axis_index("fsdp")
    ctx_index = lax.axis_index("ctx")
    share = norm_gains.shape[1]
    gains_tile = jnp.pad(norm_gains.astype(F32), ((0, 6), (0, 128 - share)))
    gains_all, qkv_all, output_all, expand_use, contract_use, cotangent_all = gather_weights(
        n_dp, gains_tile, qkv_weight, output_weight, expand_weight, contract_weight, cotangent
    )
    qkv_full = in_order(qkv_all, n_dp).reshape(features, qkv_weight.shape[1])
    output_full = in_order(output_all, n_dp).reshape(HQ * HD, features)
    gains_float = (
        in_order(gains_all, n_dp)[..., :2, :share].transpose(3, 0, 1, 2, 4).reshape(2, features)
    )
    inputs = tokens.astype(jnp.float32)
    normed, scale_one = norm_forward(inputs, gains_float[0])
    normed_low = normed.astype(jnp.bfloat16)
    projected = jnp.dot(normed_low, qkv_full, preferred_element_type=jnp.float32).astype(
        jnp.bfloat16
    )
    queries = projected[:, : HQ * HD].reshape(tok_dev, HQ, HD)
    key_value = projected[:, HQ * HD :]
    reach = (WINDOW + tok_dev - 1) // tok_dev
    earlier_pieces = []
    for distance in range(reach, 0, -1):
        earlier_pieces.append(passed_along(key_value, ("ctx", "fsdp"), distance))
    earlier = jnp.concatenate(earlier_pieces, axis=0)
    window_kv = jnp.concatenate([earlier, key_value], axis=0)
    key_rows = window_kv[:, :HD]
    value_rows = window_kv[:, HD:]
    offset = (ctx_index * n_fsdp + fsdp_index) * tok_dev
    row_index = lax.broadcasted_iota(jnp.int32, (tok_dev, WINDOW + tok_dev), 0)
    col_index = lax.broadcasted_iota(jnp.int32, (tok_dev, WINDOW + tok_dev), 1)
    visible = (
        (col_index > row_index) & (col_index <= row_index + WINDOW) & (col_index + offset >= WINDOW)
    )

    def masked_scores():
        raw_scores = (
            jnp.einsum("qhd,kd->hqk", queries, key_rows, preferred_element_type=jnp.float32)
            * score_scale
        )
        return jnp.where(visible[None], raw_scores, MASKED_SCORE)

    scores = masked_scores()
    log_total = jax.nn.logsumexp(scores, axis=-1, keepdims=True)
    probs_low = jnp.exp(scores - log_total).astype(jnp.bfloat16)
    mixture = jnp.einsum("hqk,kd->qhd", probs_low, value_rows, preferred_element_type=jnp.float32)
    mixture_low = mixture.reshape(tok_dev, HQ * HD).astype(jnp.bfloat16)
    middle = inputs + jnp.dot(mixture_low, output_full, preferred_element_type=jnp.float32)
    normed_two, scale_two = norm_forward(middle, gains_float[1])
    normed_two_low = normed_two.astype(jnp.bfloat16)
    branch_two, grad_normed_two, sum_contract, sum_expand = feed_forward(
        n_dp, ff_block, normed_two_low, cotangent_all, expand_use, contract_use
    )
    sum_expand = sum_expand.astype(F32)
    result = middle + branch_two
    block_out = result.astype(jnp.bfloat16)
    grad_result = cotangent.astype(jnp.float32)
    grad_norm_two, gain_grad_two = norm_backward(middle, scale_two, gains_float[1], grad_normed_two)
    grad_middle = grad_result + grad_norm_two
    grad_branch = grad_middle.astype(jnp.bfloat16)
    grad_output = jnp.einsum(
        "tc,td->cd", mixture_low, grad_branch, preferred_element_type=jnp.float32
    )
    grad_mixture = jnp.einsum(
        "td,cd->tc", grad_branch, output_full, preferred_element_type=jnp.float32
    )
    grad_mixture = grad_mixture.astype(jnp.bfloat16).reshape(tok_dev, HQ, HD)
    again_scores = masked_scores()
    again_probs = jnp.exp(again_scores - log_total)
    again_low = again_probs.astype(jnp.bfloat16)
    grad_probs = jnp.einsum(
        "qhd,kd->hqk", grad_mixture, value_rows, preferred_element_type=jnp.float32
    )
    row_dot = jnp.sum(again_probs * grad_probs, axis=-1, keepdims=True)
    grad_scores = (again_probs * (grad_probs - row_dot)).astype(jnp.bfloat16)
    grad_queries = (
        jnp.einsum("hqk,kd->qhd", grad_scores, key_rows, preferred_element_type=jnp.float32)
        * score_scale
    )
    grad_keys = (
        jnp.einsum("hqk,qhd->kd", grad_scores, queries, preferred_element_type=jnp.float32)
        * score_scale
    )
    grad_values = jnp.einsum(
        "hqk,qhd->kd", again_low, grad_mixture, preferred_element_type=jnp.float32
    )
    grad_window = jnp.concatenate([grad_keys, grad_values], axis=1)
    grad_key_value = grad_window[WINDOW:]
    grad_earlier = jnp.concatenate(
        [jnp.zeros((reach * tok_dev - WINDOW, 2 * HD), jnp.float32), grad_window[:WINDOW]], axis=0
    )
    for position in range(reach):
        piece = grad_earlier[position * tok_dev : (position + 1) * tok_dev]
        grad_key_value = grad_key_value + passed_along(
            piece.astype(jnp.bfloat16), ("ctx", "fsdp"), position - reach
        ).astype(piece.dtype)
    grad_projected = jnp.concatenate(
        [grad_queries.reshape(tok_dev, HQ * HD), grad_key_value], axis=1
    ).astype(jnp.bfloat16)
    grad_qkv = jnp.einsum(
        "td,tc->dc", normed_low, grad_projected, preferred_element_type=jnp.float32
    )
    grad_normed = jnp.einsum(
        "tc,dc->td", grad_projected, qkv_full, preferred_element_type=jnp.float32
    )
    grad_norm_one, gain_grad_one = norm_backward(inputs, scale_one, gains_float[0], grad_normed)
    input_grad = grad_middle + grad_norm_one
    grad_gains = jnp.stack([gain_grad_one, gain_grad_two], axis=0)
    sum_qkv, sum_output, sum_gains = attention_sums(n_dp, grad_qkv, grad_output, grad_gains)
    updates = [
        adamw_update(
            weight.astype(F32), gradient, first, second, rate, decay
        )
        for weight, gradient, first, second, rate, decay in (
            (qkv_weight, sum_qkv, first_qkv, second_qkv, RATE_MATRIX, WEIGHT_DECAY),
            (output_weight, sum_output, first_output, second_output, RATE_MATRIX, WEIGHT_DECAY),
            (expand_weight, sum_expand, first_expand, second_expand, RATE_MATRIX, WEIGHT_DECAY),
            (contract_weight, sum_contract, first_contract, second_contract, RATE_MATRIX, WEIGHT_DECAY),
            (norm_gains, sum_gains, first_gains, second_gains, RATE_GAINS, 0.0),
        )
    ]
    return (
        block_out,
        input_grad,
        *(new for new, _, _ in updates),
        *(mean for _, mean, _ in updates),
        *(square for _, _, square in updates),
    )


def shards_plain(
    tokens,
    cotangent,
    qkv_weight,
    output_weight,
    expand_weight,
    contract_weight,
    norm_gains,
    first_qkv,
    first_output,
    first_expand,
    first_contract,
    first_gains,
    second_qkv,
    second_output,
    second_expand,
    second_contract,
    second_gains,
):
    tok_dev = tokens.shape[0]
    n_fsdp = lax.axis_size("fsdp")
    n_ctx = lax.axis_size("ctx")
    ff_block = FF // (n_ctx * n_fsdp)
    score_scale = 1.0 / math.sqrt(HD)
    fsdp_index = lax.axis_index("fsdp")
    ctx_index = lax.axis_index("ctx")
    qkv_full, output_full, gains_full = (
        lax.all_gather(qkv_weight, ("ctx", "fsdp"), axis=0, tiled=True),
        lax.all_gather(output_weight, ("ctx", "fsdp"), axis=0, tiled=True),
        lax.all_gather(norm_gains, ("ctx", "fsdp"), axis=1, tiled=True),
    )
    arranged = expand_weight.reshape(expand_weight.shape[0], 2, n_ctx, n_fsdp, ff_block)
    arranged = lax.all_to_all(arranged, "fsdp", split_axis=3, concat_axis=0, tiled=True)
    arranged = arranged.reshape(arranged.shape[0], 2 * n_ctx * ff_block)
    expand_use, contract_use = (
        lax.all_gather(arranged, "ctx", axis=0, tiled=True),
        lax.all_gather(contract_weight, "ctx", axis=0, tiled=True),
    )
    width = n_ctx * ff_block
    gains_float = gains_full.astype(jnp.float32)
    inputs = tokens.astype(jnp.float32)
    normed, scale_one = norm_forward(inputs, gains_float[0])
    normed_low = normed.astype(jnp.bfloat16)
    projected = jnp.dot(normed_low, qkv_full, preferred_element_type=jnp.float32).astype(
        jnp.bfloat16
    )
    queries = projected[:, : HQ * HD].reshape(tok_dev, HQ, HD)
    key_value = projected[:, HQ * HD :]
    reach = (WINDOW + tok_dev - 1) // tok_dev
    earlier_pieces = []
    for distance in range(reach, 0, -1):
        earlier_pieces.append(passed_along(key_value, ("ctx", "fsdp"), distance))
    earlier = jnp.concatenate(earlier_pieces, axis=0)
    window_kv = jnp.concatenate([earlier, key_value], axis=0)
    key_rows = window_kv[:, :HD]
    value_rows = window_kv[:, HD:]
    offset = (ctx_index * n_fsdp + fsdp_index) * tok_dev
    row_index = lax.broadcasted_iota(jnp.int32, (tok_dev, WINDOW + tok_dev), 0)
    col_index = lax.broadcasted_iota(jnp.int32, (tok_dev, WINDOW + tok_dev), 1)
    visible = (
        (col_index > row_index) & (col_index <= row_index + WINDOW) & (col_index + offset >= WINDOW)
    )

    def masked_scores():
        raw_scores = (
            jnp.einsum("qhd,kd->hqk", queries, key_rows, preferred_element_type=jnp.float32)
            * score_scale
        )
        return jnp.where(visible[None], raw_scores, MASKED_SCORE)

    scores = masked_scores()
    log_total = jax.nn.logsumexp(scores, axis=-1, keepdims=True)
    probs_low = jnp.exp(scores - log_total).astype(jnp.bfloat16)
    mixture = jnp.einsum("hqk,kd->qhd", probs_low, value_rows, preferred_element_type=jnp.float32)
    mixture_low = mixture.reshape(tok_dev, HQ * HD).astype(jnp.bfloat16)
    middle = inputs + jnp.dot(mixture_low, output_full, preferred_element_type=jnp.float32)
    normed_two, scale_two = norm_forward(middle, gains_float[1])
    normed_two_low = normed_two.astype(jnp.bfloat16)
    ffn_input, ffn_cotangent = (
        lax.all_gather(normed_two_low, "fsdp", axis=0, tiled=True),
        lax.all_gather(cotangent, "fsdp", axis=0, tiled=True),
    )
    gate_up = jnp.dot(ffn_input, expand_use, preferred_element_type=jnp.float32)
    gate_part = gate_up[:, :width]
    up_part = gate_up[:, width:]
    activated, gelu_back = jax.vjp(functools.partial(jax.nn.gelu, approximate=True), gate_part)
    hidden_low = (activated * up_part).astype(jnp.bfloat16)
    branch_two = jnp.dot(hidden_low, contract_use, preferred_element_type=jnp.float32)
    branch_two = lax.psum_scatter(
        branch_two.astype(jnp.bfloat16), "fsdp", scatter_dimension=0, tiled=True
    ).astype(jnp.float32)
    result = middle + branch_two
    block_out = result.astype(jnp.bfloat16)
    grad_result = cotangent.astype(jnp.float32)
    grad_contract = jnp.einsum(
        "tf,td->fd", hidden_low, ffn_cotangent, preferred_element_type=jnp.float32
    )
    grad_hidden = jnp.einsum(
        "td,fd->tf", ffn_cotangent, contract_use, preferred_element_type=jnp.float32
    )
    (grad_gate,) = gelu_back(grad_hidden * up_part)
    grad_gate_up = jnp.concatenate([grad_gate, grad_hidden * activated], axis=1).astype(
        jnp.bfloat16
    )
    grad_expand = jnp.einsum(
        "td,tf->df", ffn_input, grad_gate_up, preferred_element_type=jnp.float32
    )
    grad_normed_two = jnp.einsum(
        "tf,df->td", grad_gate_up, expand_use, preferred_element_type=jnp.float32
    )
    grad_normed_two = lax.psum_scatter(grad_normed_two, "fsdp", scatter_dimension=0, tiled=True)
    part_expand, sum_contract = (
        lax.psum_scatter(
            grad_expand.astype(jnp.bfloat16), "ctx", scatter_dimension=0, tiled=True
        ).astype(jnp.float32),
        lax.psum_scatter(
            grad_contract.astype(jnp.bfloat16), "ctx", scatter_dimension=0, tiled=True
        ).astype(jnp.float32),
    )
    part_expand = part_expand.reshape(part_expand.shape[0], 2, n_ctx, 1, ff_block)
    sum_expand = lax.all_to_all(part_expand, "fsdp", split_axis=0, concat_axis=3, tiled=True)
    sum_expand = sum_expand.reshape(sum_expand.shape[0], 2 * FF)
    grad_norm_two, gain_grad_two = norm_backward(middle, scale_two, gains_float[1], grad_normed_two)
    grad_middle = grad_result + grad_norm_two
    grad_branch = grad_middle.astype(jnp.bfloat16)
    grad_output = jnp.einsum(
        "tc,td->cd", mixture_low, grad_branch, preferred_element_type=jnp.float32
    )
    grad_mixture = jnp.einsum(
        "td,cd->tc", grad_branch, output_full, preferred_element_type=jnp.float32
    )
    grad_mixture = grad_mixture.astype(jnp.bfloat16).reshape(tok_dev, HQ, HD)
    again_scores = masked_scores()
    again_probs = jnp.exp(again_scores - log_total)
    again_low = again_probs.astype(jnp.bfloat16)
    grad_probs = jnp.einsum(
        "qhd,kd->hqk", grad_mixture, value_rows, preferred_element_type=jnp.float32
    )
    row_dot = jnp.sum(again_probs * grad_probs, axis=-1, keepdims=True)
    grad_scores = (again_probs * (grad_probs - row_dot)).astype(jnp.bfloat16)
    grad_queries = (
        jnp.einsum("hqk,kd->qhd", grad_scores, key_rows, preferred_element_type=jnp.float32)
        * score_scale
    )
    grad_keys = (
        jnp.einsum("hqk,qhd->kd", grad_scores, queries, preferred_element_type=jnp.float32)
        * score_scale
    )
    grad_values = jnp.einsum(
        "hqk,qhd->kd", again_low, grad_mixture, preferred_element_type=jnp.float32
    )
    grad_window = jnp.concatenate([grad_keys, grad_values], axis=1)
    grad_key_value = grad_window[WINDOW:]
    grad_earlier = jnp.concatenate(
        [jnp.zeros((reach * tok_dev - WINDOW, 2 * HD), jnp.float32), grad_window[:WINDOW]], axis=0
    )
    for position in range(reach):
        piece = grad_earlier[position * tok_dev : (position + 1) * tok_dev]
        grad_key_value = grad_key_value + passed_along(
            piece.astype(jnp.bfloat16), ("ctx", "fsdp"), position - reach
        ).astype(piece.dtype)
    grad_projected = jnp.concatenate(
        [grad_queries.reshape(tok_dev, HQ * HD), grad_key_value], axis=1
    ).astype(jnp.bfloat16)
    grad_qkv = jnp.einsum(
        "td,tc->dc", normed_low, grad_projected, preferred_element_type=jnp.float32
    )
    grad_normed = jnp.einsum(
        "tc,dc->td", grad_projected, qkv_full, preferred_element_type=jnp.float32
    )
    grad_norm_one, gain_grad_one = norm_backward(inputs, scale_one, gains_float[0], grad_normed)
    input_grad = grad_middle + grad_norm_one
    grad_gains = jnp.stack([gain_grad_one, gain_grad_two], axis=0)
    sum_qkv, sum_output, sum_gains = (
        lax.psum_scatter(grad_qkv, ("ctx", "fsdp"), scatter_dimension=0, tiled=True),
        lax.psum_scatter(grad_output, ("ctx", "fsdp"), scatter_dimension=0, tiled=True),
        lax.psum_scatter(grad_gains, ("ctx", "fsdp"), scatter_dimension=1, tiled=True),
    )
    new_qkv, mean_qkv, square_qkv = adamw_update(
        qkv_weight.astype(jnp.float32), sum_qkv, first_qkv, second_qkv, RATE_MATRIX, WEIGHT_DECAY
    )
    new_output, mean_output, square_output = adamw_update(
        output_weight.astype(jnp.float32),
        sum_output,
        first_output,
        second_output,
        RATE_MATRIX,
        WEIGHT_DECAY,
    )
    new_expand, mean_expand, square_expand = adamw_update(
        expand_weight.astype(jnp.float32),
        sum_expand,
        first_expand,
        second_expand,
        RATE_MATRIX,
        WEIGHT_DECAY,
    )
    new_contract, mean_contract, square_contract = adamw_update(
        contract_weight.astype(jnp.float32),
        sum_contract,
        first_contract,
        second_contract,
        RATE_MATRIX,
        WEIGHT_DECAY,
    )
    new_gains, mean_gains, square_gains = adamw_update(
        norm_gains.astype(jnp.float32), sum_gains, first_gains, second_gains, RATE_GAINS, 0.0
    )
    return (
        block_out,
        input_grad,
        new_qkv,
        new_output,
        new_expand,
        new_contract,
        new_gains,
        mean_qkv,
        mean_output,
        mean_expand,
        mean_contract,
        mean_gains,
        square_qkv,
        square_output,
        square_expand,
        square_contract,
        square_gains,
    )


def shards(*arguments):
    plane_rows = 8 * arguments[4].shape[0]
    return (shards_kernels if plane_rows % 16 == 0 else shards_plain)(*arguments)


def solution(mesh):
    rows, columns = P(("ctx", "fsdp"), None), P(None, ("ctx", "fsdp"))
    in_specs = (rows,) * 6 + (columns,) + ((rows,) * 4 + (columns,)) * 2
    out_specs = (rows,) * 2 + ((rows,) * 4 + (columns,)) * 3
    return jax.shard_map(shards, mesh=mesh, in_specs=in_specs, out_specs=out_specs, check_vma=False)
```

```python
import functools
import math
import types

import jax
import jax.numpy as jnp
from jax import lax
from jax.experimental import pallas as pl
from jax.experimental.pallas import tpu as pltpu
from jax.sharding import PartitionSpec as P

HQ = 4
HD = 256
FF = 6912
WINDOW = 512
STEP = 10

NORM_EPSILON = 1e-06
BETA_FIRST = 0.9
BETA_SECOND = 0.999
RATE_MATRIX = 0.1
RATE_GAINS = 0.5
WEIGHT_DECAY = 0.1
ADAM_EPSILON = 1e-08
MASKED_SCORE = -1e30

F32 = jnp.float32
BF16 = jnp.bfloat16
MESH = pl.DeviceIdType.MESH
VMEM_LIMIT = 65400 * 1024
WIRES = 320
QD = HQ * HD


def position():
    ctx, fsdp = lax.axis_index("ctx"), lax.axis_index("fsdp")
    return ctx // 2, lax.rem(ctx, 2), fsdp // 2, lax.rem(fsdp, 2)


def device(q, y, x, c):
    return (q * 2 + y, x * 2 + c)


def device_at(index):
    return (index // 4, lax.rem(index, 4))


def rows_of(ref, first, count):
    if not isinstance(first, int):
        first = pl.multiple_of(first, 16 if ref.dtype == BF16 else 8)
    return ref.at[pl.ds(first, count)]


def gelu_parts(u):
    k = math.sqrt(2.0 / math.pi)
    square = u * u
    t = jnp.tanh(k * u * (1.0 + 0.044715 * square))
    half = 0.5 * (1.0 + t)
    slope = half + 0.5 * u * (1.0 - t * t) * (k * (1.0 + (3.0 * 0.044715) * square))
    return u * half, slope


def dot_nt(a, b):
    return lax.dot_general(a, b, (((1,), (1,)), ((), ())), preferred_element_type=F32)


def dot_tn(a, b):
    return lax.dot_general(a, b, (((0,), (0,)), ((), ())), preferred_element_type=F32)


def dot_nn(a, b):
    return jnp.dot(a, b, preferred_element_type=F32)


def norm_scale(values):
    return lax.rsqrt(jnp.mean(values * values, axis=-1, keepdims=True) + NORM_EPSILON)


def norm_backward(values, scale, gain_row, grad_normed):
    gain_grad = jnp.sum(grad_normed * values * scale, axis=0, keepdims=True)
    scaled = grad_normed * gain_row
    cubed = scale * scale * scale
    grad_values = scale * scaled - values * cubed * jnp.mean(
        scaled * values, axis=-1, keepdims=True
    )
    return grad_values, gain_grad


class Wires:
    def __init__(self, send_sems, recv_sems):
        self.send_sems, self.recv_sems = send_sems, recv_sems
        self.count = 0
        self.sent = {}
        self.tag = None

    def take(self, number=1):
        first = self.count
        self.count += number
        assert self.count <= WIRES, self.count
        return first

    def copy(self, src, dst, target, index):
        return pltpu.make_async_remote_copy(
            src_ref=src,
            dst_ref=dst,
            send_sem=self.send_sems.at[index],
            recv_sem=self.recv_sems.at[index],
            device_id=target,
            device_id_type=MESH,
        )

    def send(self, src, dst, target, index, when=None, tag=None):
        def make():
            here, there = (ref() if callable(ref) else ref for ref in (src, dst))
            return self.copy(here, there, target, index)

        if when is None:
            make().start()
        else:
            pl.when(when)(make().start)
        self.sent.setdefault(tag, []).append((make, when))

    def wait(self, dst, target, index, when=None):
        copy = self.copy(dst, dst, target, index)
        if when is None:
            copy.wait_recv()
        else:
            pl.when(when)(copy.wait_recv)

    def drain(self, *tags):
        for tag in tags or list(self.sent):
            for make, when in self.sent.pop(tag, ()):
                if when is None:
                    make().wait_send()
                else:
                    pl.when(when)(make().wait_send)


def greet(n_dp, reach):
    q, y, x, c = position()
    barrier = pltpu.get_barrier_semaphore()
    expected = 0

    def signal(target):
        pl.semaphore_signal(barrier, inc=1, device_id=target, device_id_type=MESH)

    for dy in range(2):
        for dx in range(2):
            for dc in range(2):
                if dy + dx + dc:
                    signal(device(q, (y + dy) % 2, (x + dx) % 2, (c + dc) % 2))
                    expected += 1
    me = (q * 2 + y) * 4 + x * 2 + c
    last = 8 * n_dp - 1
    for distance in range(1, reach + 1):
        for other in (me - distance, me + distance):
            here = (other >= 0) & (other <= last)
            pl.when(here)(functools.partial(signal, device_at(jnp.clip(other, 0, last))))
            expected = expected + here.astype(jnp.int32)
    for other in (q - 1, q + 1):
        here = (other >= 0) & (other <= n_dp - 1)
        pl.when(here)(functools.partial(signal, device(jnp.clip(other, 0, n_dp - 1), y, x, c)))
        expected = expected + here.astype(jnp.int32)
    pl.semaphore_wait(barrier, expected)


class Plane:
    def __init__(self):
        self.q, self.y, self.x, self.c = q, y, x, c = position()
        self.chips = [y * 2 + x, y * 2 + 1 - x, (1 - y) * 2 + x, (1 - y) * 2 + 1 - x]
        self.chip, self.chip_x, self.chip_y, self.chip_d = self.chips
        self.to_x, self.to_y = device(q, y, 1 - x, c), device(q, 1 - y, x, c)
        self.to_c = device(q, y, x, 1 - c)


class Chain:
    def __init__(self, wires, n_dp, own, place, tag):
        self.wires, self.n_dp, self.own, self.place, self.tag = wires, n_dp, own, place, tag
        self.first = {way: wires.take(n_dp - 1) for way in (1, -1)}

    def valid(self, way, step):
        q = position()[0]
        return (q - 1 - step >= 0) if way == 1 else (q + 1 + step <= self.n_dp - 1)

    def send(self, way, step):
        q, y, x, c = position()
        block = q - way * step
        here = (block >= 0) & (block <= self.n_dp - 1) & (q + way >= 0) & (q + way <= self.n_dp - 1)
        inside = jnp.clip(block, 0, self.n_dp - 1)
        src = self.own if step == 0 else self.place(inside)
        self.wires.send(
            src,
            self.place(inside),
            device(jnp.clip(q + way, 0, self.n_dp - 1), y, x, c),
            self.first[way] + step,
            here,
            self.tag,
        )

    def wait(self, way, step):
        q, y, x, c = position()
        block = jnp.clip(q - way * (step + 1), 0, self.n_dp - 1)
        self.wires.wait(
            self.place(block),
            device(jnp.clip(q + way, 0, self.n_dp - 1), y, x, c),
            self.first[way] + step,
            self.valid(way, step),
        )
        if step + 1 < self.n_dp - 1:
            self.send(way, step + 1)

    def start(self):
        self.send(1, 0)
        self.send(-1, 0)

    def hop(self, step):
        self.wait(1, step)
        self.wait(-1, step)


class PlaneGather(Plane):
    def __init__(self, wires, own, buf, base, rows, tag):
        super().__init__()
        self.wires, self.own, self.buf, self.base, self.rows = wires, own, buf, base, rows
        self.half = rows // 2
        self.tag = tag
        (self.xa, self.xb, self.ya, self.yb, self.co, self.da, self.db) = (
            wires.take() for _ in range(7)
        )
        self.cx, self.cy, self.cd = (wires.take() for _ in range(3))

    def part(self, chip, c, which=None):
        first = self.base + (chip * 2 + c) * self.rows
        if which is None:
            return rows_of(self.buf, first, self.rows)
        return rows_of(self.buf, first + which * self.half, self.half)

    def send(self, src, dst, target, index):
        self.wires.send(src, dst, target, index, None, self.tag)

    def start(self):
        c, half = self.c, self.half
        low, high = self.own.at[pl.ds(0, half)], self.own.at[pl.ds(half, half)]
        self.send(low, self.part(self.chip, c, 0), self.to_x, self.xa)
        self.send(high, self.part(self.chip, c, 1), self.to_y, self.yb)
        self.send(high, self.part(self.chip, c, 1), self.to_x, self.xb)
        self.send(low, self.part(self.chip, c, 0), self.to_y, self.ya)
        self.send(self.own, self.part(self.chip, c), self.to_c, self.co)

    def forward(self, target, index, chip, which=None):
        def part():
            return self.part(chip, self.c, which)

        self.send(part, part, target, index)

    def relay(self):
        c, wires = self.c, self.wires
        wires.wait(self.part(self.chip_x, c, 0), self.to_x, self.xa)
        self.forward(self.to_y, self.da, self.chip_x, 0)
        wires.wait(self.part(self.chip_y, c, 1), self.to_y, self.yb)
        self.forward(self.to_x, self.db, self.chip_y, 1)

    def relay_core(self):
        c, wires = self.c, self.wires
        wires.wait(self.part(self.chip_x, c, 1), self.to_x, self.xb)
        self.forward(self.to_c, self.cx, self.chip_x)
        wires.wait(self.part(self.chip_y, c, 0), self.to_y, self.ya)
        self.forward(self.to_c, self.cy, self.chip_y)

    def relay_last(self):
        c, wires = self.c, self.wires
        wires.wait(self.part(self.chip_d, c, 0), self.to_y, self.da)
        wires.wait(self.part(self.chip_d, c, 1), self.to_x, self.db)
        self.forward(self.to_c, self.cd, self.chip_d)

    def wait_core(self):
        self.wires.wait(self.part(self.chip, 1 - self.c), self.to_c, self.co)

    def wait_core_x(self):
        self.wires.wait(self.part(self.chip_x, 1 - self.c), self.to_c, self.cx)

    def wait_core_y(self):
        self.wires.wait(self.part(self.chip_y, 1 - self.c), self.to_c, self.cy)

    def wait_last(self):
        self.wires.wait(self.part(self.chip_d, 1 - self.c), self.to_c, self.cd)


class SlotGather(Plane):
    def __init__(self, wires, n_dp, own, buf, base, rows, tag):
        super().__init__()
        self.wires, self.n_dp, self.own, self.tag = wires, n_dp, own, tag
        self.buf, self.base, self.rows = buf, base, rows
        self.order = [(0, -1)] + [(way, s) for s in range(n_dp - 1) for way in (1, -1)]
        self.chain = Chain(wires, n_dp, own, lambda j: self.slot(self.c, j, self.chip), tag)
        self.kx, self.ky, self.kd, self.kc = (wires.take(len(self.order)) for _ in range(4))

    def slot(self, c, j, chip, count=1):
        return rows_of(
            self.buf, self.base + ((c * self.n_dp + j) * 4 + chip) * self.rows, count * self.rows
        )

    def each(self, ranks):
        for rank, (way, step) in enumerate(self.order):
            if ranks is not None and rank not in ranks:
                continue
            if way == 0:
                yield rank, way, step, self.q, None
            else:
                block = jnp.clip(self.q - way * (step + 1), 0, self.n_dp - 1)
                yield rank, way, step, block, self.chain.valid(way, step)

    def start(self):
        self.chain.start()

    def spread(self, ranks=None):
        for rank, way, step, j, ok in self.each(ranks):
            if way:
                self.chain.wait(way, step)
            src = self.slot(self.c, j, self.chip) if way else self.own
            dst = self.slot(self.c, j, self.chip)
            self.wires.send(src, dst, self.to_x, self.kx + rank, ok, self.tag)
            self.wires.send(src, dst, self.to_y, self.ky + rank, ok, self.tag)

    def relay(self, ranks=None):
        for rank, way, step, j, ok in self.each(ranks):
            even = lax.rem(j, 2) == 0
            odd = jnp.logical_not(even)
            sx, sy = self.slot(self.c, j, self.chip_x), self.slot(self.c, j, self.chip_y)
            self.wires.wait(sx, self.to_x, self.kx + rank, ok)
            to_y = even if ok is None else ok & even
            self.wires.send(sx, sx, self.to_y, self.kd + rank, to_y, self.tag)
            self.wires.wait(sy, self.to_y, self.ky + rank, ok)
            to_x = odd if ok is None else ok & odd
            self.wires.send(sy, sy, self.to_x, self.kd + rank, to_x, self.tag)

    def core(self, ranks=None):
        for rank, way, step, j, ok in self.each(ranks):
            self.wires.wait(self.slot(self.c, j, self.chip_d), self.to_x, self.kd + rank, ok)
            four = self.slot(self.c, j, 0, 4)
            self.wires.send(four, four, self.to_c, self.kc + rank, ok, self.tag)

    def finish(self, ranks=None):
        for rank, way, step, j, ok in self.each(ranks):
            four = self.slot(1 - self.c, j, 0, 4)
            self.wires.wait(four, self.to_c, self.kc + rank, ok)


def add_into(mine, other):
    mine[...] = (mine[...].astype(F32) + other[...].astype(F32)).astype(mine.dtype)


class ChainSum:
    def __init__(self, wires, n_dp, own, land, tag, stage=None, stage_sem=None):
        self.wires, self.n_dp, self.own, self.land, self.tag = wires, n_dp, own, land, tag
        self.stage, self.stage_sem = stage, stage_sem
        self.first = {way: wires.take(n_dp) for way in (1, -1)}

    def add(self, own, slot):
        if self.stage is None:
            add_into(own, slot)
        else:
            copy = pltpu.make_async_copy(slot, self.stage, self.stage_sem)
            copy.start()
            copy.wait()
            add_into(own, self.stage)

    def step(self, way, j, when):
        q, y, x, c = position()
        last = self.n_dp - 1
        ahead = ((j > q) if way == 1 else (j < q)) & when
        behind = (q > 0) if way == 1 else (q < last)
        target = device(jnp.clip(q - way, 0, last), y, x, c)
        self.wires.wait(self.land(j), target, self.first[way] + j, ahead & behind)

        @pl.when(ahead & behind)
        def _():
            self.add(self.own(j), self.land(j))

        nearer = jnp.clip(q + way, 0, last)
        slot = j if way == 1 else jnp.where(nearer == j, self.n_dp, j)
        self.wires.send(
            self.own(j),
            self.land(slot),
            device(nearer, y, x, c),
            self.first[way] + j,
            ahead,
            self.tag,
        )

    def level(self, number, blocks=None):
        q = position()[0]
        blocks = range(self.n_dp) if blocks is None else blocks
        for j in sorted(blocks, reverse=True):
            self.step(1, j, q == number)
        for j in sorted(blocks):
            self.step(-1, j, q == self.n_dp - 1 - number)

    def collect(self):
        q, y, x, c = position()
        for way in (1, -1):
            behind = (q > 0) if way == 1 else (q < self.n_dp - 1)
            target = device(jnp.clip(q - way, 0, self.n_dp - 1), y, x, c)
            slot = self.land(q) if way == 1 else self.land(self.n_dp)
            self.wires.wait(slot, target, self.first[way] + q, behind)
            pl.when(behind)(functools.partial(self.add, self.own(q), slot))


class PlaneSum(Plane):
    def __init__(self, wires, buf, base, rows, cores, diag, sides, tag):
        super().__init__()
        self.wires, self.buf, self.base, self.rows, self.tag = wires, buf, base, rows, tag
        self.half = rows // 2
        self.cores, self.diag, self.sides = cores, diag, sides
        self.kc = wires.take(4)
        self.kdx, self.kdy = wires.take(), wires.take()
        self.kxa, self.kxb, self.kya, self.kyb = (wires.take() for _ in range(4))

    part = PlaneGather.part
    send = PlaneGather.send

    def send_core(self, k):
        self.send(self.part(self.chips[k], 1 - self.c), self.cores.at[k], self.to_c, self.kc + k)

    def fetch_core(self, k, stage, sem):
        self.wires.wait(self.cores.at[k], self.to_c, self.kc + k)
        copy = pltpu.make_async_copy(self.cores.at[k], stage, sem)
        copy.start()
        return copy

    def add_core(self, k, stage):
        add_into(self.part(self.chips[k], self.c), stage)

    def side(self, which, half):
        return self.sides.at[which, pl.ds(half * self.half, self.half)]

    def send_diag(self):
        self.send(self.part(self.chip_d, self.c, 0), self.diag.at[0], self.to_x, self.kdx)
        self.send(self.part(self.chip_d, self.c, 1), self.diag.at[1], self.to_y, self.kdy)

    def send_x(self):
        self.send(self.part(self.chip_x, self.c, 0), self.side(0, 0), self.to_x, self.kxa)

    def send_y(self):
        self.send(self.part(self.chip_y, self.c, 1), self.side(1, 1), self.to_y, self.kyb)

    def send_second(self):
        self.wires.wait(self.diag.at[0], self.to_x, self.kdx)
        mine = self.part(self.chip_y, self.c, 0)
        add_into(mine, self.diag.at[0])
        self.send(mine, self.side(1, 0), self.to_y, self.kya)
        self.wires.wait(self.diag.at[1], self.to_y, self.kdy)
        mine = self.part(self.chip_x, self.c, 1)
        add_into(mine, self.diag.at[1])
        self.send(mine, self.side(0, 1), self.to_x, self.kxb)

    def total(self):
        self.wires.wait(self.side(0, 0), self.to_x, self.kxa)
        self.wires.wait(self.side(1, 1), self.to_y, self.kyb)
        self.wires.wait(self.side(1, 0), self.to_y, self.kya)
        self.wires.wait(self.side(0, 1), self.to_x, self.kxb)
        mine = self.part(self.chip, self.c)
        return mine[...].astype(F32) + self.sides[0].astype(F32) + self.sides[1].astype(F32)


class SlotSum(Plane):
    def __init__(
        self, wires, n_dp, buf, base, rows, cores, diag, sides, landing, tag, stage=None, sem=None
    ):
        super().__init__()
        self.wires, self.n_dp, self.tag = wires, n_dp, tag
        self.buf, self.base, self.rows = buf, base, rows
        self.cores, self.diag, self.sides = cores, diag, sides
        self.stage, self.sem = stage, sem
        self.low = n_dp // 2
        self.high = n_dp - self.low
        self.kc = wires.take(4)
        self.kdx, self.kdy, self.kx0, self.kx1, self.ky0, self.ky1 = (
            wires.take() for _ in range(6)
        )
        self.chain = ChainSum(
            wires,
            n_dp,
            lambda j: self.at(self.c, self.chip, j, 1),
            lambda j: rows_of(landing, j * rows, rows),
            tag,
        )

    def at(self, c, chip, j, count):
        first = self.base + ((c * 4 + chip) * self.n_dp + j) * self.rows
        return rows_of(self.buf, first, count * self.rows)

    def four(self, ref, k):
        return ref.at[pl.ds(k * self.n_dp * self.rows, self.n_dp * self.rows)]

    def lows(self, ref, which=0):
        return ref.at[pl.ds(which * self.n_dp * self.rows, self.low * self.rows)]

    def highs(self, ref, which=0):
        first = (which * self.n_dp + self.low) * self.rows
        return ref.at[pl.ds(first, self.high * self.rows)]

    def send(self, src, dst, target, index):
        self.wires.send(src, dst, target, index, None, self.tag)

    def send_core(self):
        for k in (3, 1, 2, 0):
            src = self.at(1 - self.c, self.chips[k], 0, self.n_dp)
            self.send(src, self.four(self.cores, k), self.to_c, self.kc + k)

    def add_core(self, k):
        other = self.four(self.cores, k)
        self.wires.wait(other, self.to_c, self.kc + k)
        if self.stage is not None:
            copy = pltpu.make_async_copy(other, self.stage, self.sem)
            copy.start()
            copy.wait()
            other = self.stage
        add_into(self.at(self.c, self.chips[k], 0, self.n_dp), other)

    def send_first(self):
        low, c = self.low, self.c
        self.add_core(3)
        self.send(self.at(c, self.chip_d, 0, low), self.lows(self.diag), self.to_x, self.kdx)
        self.send(self.at(c, self.chip_d, low, self.high), self.highs(self.diag), self.to_y, self.kdy)
        self.add_core(1)
        self.send(self.at(c, self.chip_x, 0, low), self.lows(self.sides), self.to_x, self.kx0)
        self.add_core(2)
        self.send(self.at(c, self.chip_y, low, self.high), self.highs(self.sides, 1), self.to_y, self.ky1)
        self.add_core(0)

    def send_second(self):
        low, c, wires = self.low, self.c, self.wires
        wires.wait(self.lows(self.diag), self.to_x, self.kdx)
        mine = self.at(c, self.chip_y, 0, low)
        add_into(mine, self.lows(self.diag))
        self.send(mine, self.lows(self.sides, 1), self.to_y, self.ky0)
        wires.wait(self.highs(self.diag), self.to_y, self.kdy)
        mine = self.at(c, self.chip_x, low, self.high)
        add_into(mine, self.highs(self.diag))
        self.send(mine, self.highs(self.sides), self.to_x, self.kx1)

    def add_sides(self):
        wires = self.wires
        wires.wait(self.lows(self.sides), self.to_x, self.kx0)
        wires.wait(self.highs(self.sides, 1), self.to_y, self.ky1)
        wires.wait(self.lows(self.sides, 1), self.to_y, self.ky0)
        wires.wait(self.highs(self.sides), self.to_x, self.kx1)
        mine = self.at(self.c, self.chip, 0, self.n_dp)
        mine[...] = (
            mine[...].astype(F32)
            + self.four(self.sides, 0)[...].astype(F32)
            + self.four(self.sides, 1)[...].astype(F32)
        ).astype(mine.dtype)


class Exchange(Plane):
    def __init__(self, wires, pieces_out, pieces_in, local_sem, tag):
        super().__init__()
        self.wires, self.out, self.into, self.tag = wires, pieces_out, pieces_in, tag
        self.index = wires.take(7)
        self.me = self.chip * 2 + self.c
        self.copy = pltpu.make_async_copy(
            pieces_out.at[self.me], pieces_in.at[self.me], local_sem
        )

    def others(self):
        number = 0
        for dc in (0, 1):
            for dy, dx in ((1, 1), (0, 1), (1, 0), (0, 0)):
                if dy + dx + dc == 0:
                    continue
                ty, tx, tc = (self.y + dy) % 2, (self.x + dx) % 2, (self.c + dc) % 2
                yield (ty * 2 + tx) * 2 + tc, device(self.q, ty, tx, tc), self.index + number
                number += 1

    def start(self):
        for other, target, index in self.others():
            self.wires.send(
                self.out.at[other], self.into.at[self.me], target, index, None, self.tag
            )
        self.copy.start()

    def finish(self):
        for other, target, index in self.others():
            self.wires.wait(self.into.at[other], target, index)
        self.copy.wait()


def hidden_layout(n_dp, ff_block):
    padded = -(-ff_block // 16) * 16
    width = -(-n_dp * padded // 128) * 128
    tiles = width // 128
    cuts = [0, tiles * 2 // 7, tiles * 4 // 7, tiles]
    chunks = [(128 * a, 128 * (b - a)) for a, b in zip(cuts, cuts[1:])]
    pieces = []
    for group in range(8):
        for part in range(2):
            for q in range(n_dp):
                source = part * FF + ff_block * (q * 8 + group)
                begin, end = padded * q, padded * q + ff_block
                for number, (first, size) in enumerate(chunks):
                    lo, hi = max(begin, first), min(end, first + size)
                    if lo < hi:
                        place = part * size + lo - first
                        pieces.append((group, source + lo - begin, hi - lo, number, place))
    return padded, width, chunks, pieces


INPUTS = ("tokens", "cotangent", "qkv", "output", "gains", "expand", "contract")
OUTPUTS = (
    "block_out",
    "input_grad",
    "sum_qkv",
    "sum_output",
    "sum_gains",
    "sum_expand",
    "sum_contract",
)


def fold(dst, first, src, row, share):
    wide, features = src.shape[1], dst.shape[1]
    third = share // 3
    extra = wide - features
    dst[first : first + share, :] = src[row : row + share, :features]
    for k in range(3):
        dst[first + share : first + share + third, k * extra : (k + 1) * extra] = src[
            row + third * k : row + third * (k + 1), features:
        ]


def unfold(dst, row, share, src, first):
    wide, features = dst.shape[1], src.shape[1]
    third = share // 3
    extra = wide - features
    dst[row : row + share, :features] = src[first : first + share, :].astype(dst.dtype)
    for k in range(3):
        dst[row + third * k : row + third * (k + 1), features:] = src[
            first + share : first + share + third, k * extra : (k + 1) * extra
        ].astype(dst.dtype)


def block_kernel(n_dp, names, *refs):
    r = types.SimpleNamespace(**dict(zip(names, refs, strict=True)))
    wires = Wires(r.send_sems, r.recv_sems)
    plane = Plane()
    q, y, x, c, chip = plane.q, plane.y, plane.x, plane.c, plane.chip
    me = (q * 4 + chip) * 2 + c
    n_all = 8 * n_dp
    rows, features = r.tokens.shape
    share, wide = r.qkv.shape
    share_out = r.output.shape[0]
    ff_block = r.contract.shape[0]
    plane_rows = 8 * share
    folded = share + share // 3
    padded, width, chunks, pieces = hidden_layout(n_dp, ff_block)
    experts = [r.expand_0, r.expand_1, r.expand_2]
    all_rows = 8 * rows
    x_base, cot_base, branch_base, back_base = (all_rows * i for i in range(4))
    qkv_base, output_base = branch_base, branch_base + n_all * folded
    output_full, output_again = output_base + n_all * share_out, n_all * (share_out + folded)
    reach = WINDOW // rows
    scale = 1.0 / math.sqrt(HD)
    arena = r.arena

    def load(src, dst, number):
        copy = pltpu.make_async_copy(src, dst, r.local_sems.at[number])
        copy.start()
        return copy

    get_expand = load(r.expand, r.sum_expand, 0)
    get_contract = load(r.contract, r.sum_contract, 5)
    greet(n_dp, reach)
    fold(r.own_qkv, 0, r.qkv, 0, share)
    gains_gather = SlotGather(wires, n_dp, r.gains, r.gain_slots, 0, 8, "weights")
    qkv_gather = SlotGather(wires, n_dp, r.own_qkv, arena, qkv_base, folded, "weights")
    output_gather = SlotGather(wires, n_dp, r.output, arena, output_base, share_out, "weights")
    gathers = (gains_gather, qkv_gather, output_gather)
    for gather in gathers:
        gather.start()
    own_slots = [
        load(g.own, g.slot(c, q, chip), 1 + i) for i, g in enumerate(gathers)
    ]
    gains_gather.spread((0,))
    qkv_gather.spread((0,))

    def contract_place(j):
        return rows_of(r.contract_all, j * padded, padded)

    get_contract.wait()
    r.stage[0:ff_block, :] = r.sum_contract[...]
    if padded > ff_block:
        r.stage[ff_block:padded, :] = jnp.zeros((padded - ff_block, features), BF16)
    contract_place(q)[...] = r.stage[0:padded, :]
    contract_chain = Chain(wires, n_dp, contract_place(q), contract_place, "contract")
    contract_chain.start()
    starts = [2 * begin for begin, _ in chunks]
    r.pieces_out[...] = jnp.zeros_like(r.pieces_out)
    get_expand.wait()
    for group, source, size, number, place in pieces:
        at = starts[number] + place
        r.pieces_out[group, :, at : at + size] = r.sum_expand[:, source : source + size]
    exchange = Exchange(wires, r.pieces_out, r.pieces_in, r.local_sems.at[4], "pieces")
    exchange.start()
    ranks = len(gains_gather.order)
    for gather in (gains_gather, qkv_gather):
        gather.spread((1, 2))
    output_gather.spread((0,))
    for gather in (gains_gather, qkv_gather):
        gather.relay((0,))
        gather.spread(range(3, ranks))
    exchange.finish()

    def expand_place(number):
        return lambda j: rows_of(experts[number], j * plane_rows, plane_rows)

    expand_chains = []
    for number, (begin, size) in enumerate(chunks):
        for group in range(8):
            r.stage[share * group : share * (group + 1), 0 : 2 * size] = r.pieces_in[
                group, :, starts[number] : starts[number] + 2 * size
            ]
        place = expand_place(number)
        place(q)[...] = r.stage[0:plane_rows, 0 : 2 * size]
        chain = Chain(wires, n_dp, place(q), place, "expand_%d" % number)
        chain.start()
        expand_chains.append(chain)
    for copy in own_slots:
        copy.wait()
    for gather in (gains_gather, qkv_gather):
        gather.relay(range(1, ranks))
        gather.core((0,))
    output_gather.spread(range(1, ranks))
    for gather in (gains_gather, qkv_gather):
        gather.core(range(1, ranks))
    output_gather.relay()
    cotangent_gather = PlaneGather(wires, r.cotangent, arena, cot_base, rows, "cotangent")
    cotangent_gather.start()
    own_cotangent = load(r.cotangent, cotangent_gather.part(chip, c), 1)
    for gather in (gains_gather, qkv_gather):
        gather.finish()
    contract_chain.hop(0)
    for j in range(n_dp):
        for k in range(4):
            for e in range(2):
                d = (j * 4 + k) * 2 + e
                slot = (e * n_dp + j) * 4 + k
                unfold(r.qkv_full, share * d, share, arena, qkv_base + slot * folded)
                r.gains_full[0:2, share * d : share * (d + 1)] = r.gain_slots[
                    8 * slot : 8 * slot + 2, 0:share
                ]
    inputs = r.tokens[...].astype(F32)
    r.normed[...] = (inputs * norm_scale(inputs) * r.gains_full[0:1, :]).astype(BF16)
    for first in range(0, wide, 512):
        part = dot_nn(r.normed[...], r.qkv_full[:, first : first + 512]).astype(BF16)
        if first < QD:
            r.queries[:, first : first + 512] = part
        else:
            r.window[WINDOW : WINDOW + rows, first - QD : first - QD + 512] = part
    mine = r.window.at[pl.ds(WINDOW, rows)]
    kv_index = wires.take(2 * reach)
    earlier = []
    for distance in range(1, reach + 1):
        place = r.window.at[pl.ds(WINDOW - distance * rows, rows)]
        after, before = me + distance, me - distance
        wires.send(
            mine,
            place,
            device_at(jnp.clip(after, 0, n_all - 1)),
            kv_index + distance - 1,
            after <= n_all - 1,
            "window",
        )

        @pl.when(before < 0)
        def _(place=place):
            place[...] = jnp.zeros_like(place)

        earlier.append(
            (place, device_at(jnp.clip(before, 0, n_all - 1)), kv_index + distance - 1, before >= 0)
        )
    output_gather.core()
    contract_chain.hop(1)
    expand_chains[0].hop(0)
    output_gather.finish()
    for j in range(n_dp):
        for k in range(4):
            for e in range(2):
                d = (j * 4 + k) * 2 + e
                first = output_base + ((e * n_dp + j) * 4 + k) * share_out
                there = output_full + share_out * d
                arena[there : there + share_out, :] = arena[first : first + share_out, :]
    put_output = load(arena.at[pl.ds(output_full, QD)], r.output_kept, 2)
    for arrival in earlier:
        wires.wait(*arrival)
    keys = WINDOW + rows

    def visible():
        row = lax.broadcasted_iota(jnp.int32, (rows, keys), 0)
        col = lax.broadcasted_iota(jnp.int32, (rows, keys), 1)
        return (col > row) & (col <= row + WINDOW) & (col + me * rows >= WINDOW)

    def scores_of(h):
        mine = pl.ds(pl.multiple_of(h * HD, HD), HD)
        raw = dot_nt(r.queries[:, mine], r.window[:, 0:HD]) * scale
        return jnp.where(visible(), raw, MASKED_SCORE)

    def head(h, carry):
        scores = scores_of(h)
        top = jnp.max(scores, axis=-1, keepdims=True)
        log_total = top + jnp.log(jnp.sum(jnp.exp(scores - top), axis=-1, keepdims=True))
        r.log_totals[h] = log_total
        low = jnp.exp(scores - log_total).astype(BF16)
        mine = pl.ds(pl.multiple_of(h * HD, HD), HD)
        r.mixture[:, mine] = dot_nn(low, r.window[:, HD : 2 * HD]).astype(BF16)
        return carry

    lax.fori_loop(0, HQ, head, 0)
    middle = r.tokens[...].astype(F32) + dot_nn(
        r.mixture[...], arena[output_full : output_full + QD, :]
    )
    r.middle[...] = middle
    tokens_gather = PlaneGather(wires, None, arena, x_base, rows, "tokens")
    own = tokens_gather.part(chip, c)
    tokens_gather.own = own
    own[...] = (middle * norm_scale(middle) * r.gains_full[1:2, :]).astype(BF16)
    tokens_gather.start()
    wires.drain("weights", "pieces")
    own_cotangent.wait()
    put_output.wait()
    cotangent_gather.relay()
    expand_chains[0].hop(1)
    cotangent_gather.wait_core()
    for step in range(2, n_dp - 1):
        contract_chain.hop(step)
        expand_chains[0].hop(step)
    expand_chains[1].hop(0)
    tokens_gather.wait_core()
    chips = plane.chips

    def chunk(number, events):
        begin, size = chunks[number]
        expand = experts[number]
        inner = r.contract_all.at[pl.ds(begin, size)]

        def tile(index, carry):
            for when, event in events.items():
                pl.when(index == when)(event)
            pair = index // 2
            place = jnp.where(
                pair == 0, chips[0], jnp.where(pair == 1, chips[1], jnp.where(pair == 2, chips[2], chips[3]))
            )
            offset = (place * 2 + lax.rem(index, 2)) * rows
            here = pl.ds(pl.multiple_of(offset, rows), rows)

            def at(base):
                return pl.ds(pl.multiple_of(base + offset, rows), rows)

            gate_up = dot_nn(arena[at(x_base), :], expand[...])
            grad_hidden = dot_nt(arena[at(cot_base), :], inner[...])
            gate, up = gate_up[:, :size], gate_up[:, size:]
            activated, slope = gelu_parts(gate)
            low = (activated * up).astype(BF16)
            r.hidden[here, :size] = low
            r.grad_gate_up[here, :size] = (grad_hidden * up * slope).astype(BF16)
            r.grad_gate_up[here, size : 2 * size] = (grad_hidden * activated).astype(BF16)
            out = dot_nn(low, inner[...])
            if number:
                out = out + arena[at(branch_base), :].astype(F32)
            arena[at(branch_base), :] = out.astype(BF16)
            back = dot_nt(r.grad_gate_up[here, : 2 * size], expand[...])
            if number:
                back = back + arena[at(back_base), :].astype(F32)
            arena[at(back_base), :] = back.astype(BF16)
            return carry

        lax.fori_loop(0, 8, tile, 0)

    third = features // 3

    def weight_grads(number):
        begin, size = chunks[number]

        def contract_tile(index, carry):
            here = pl.ds(pl.multiple_of(index * 128, 128), 128)
            there = pl.ds(pl.multiple_of(begin + index * 128, 128), 128)
            for first in range(0, features, third):
                cot = arena[cot_base : cot_base + all_rows, first : first + third]
                out = dot_tn(r.hidden[:, here], cot).astype(BF16)
                r.contract_all[there, first : first + third] = out
            return carry

        lax.fori_loop(0, size // 128, contract_tile, 0)

        def expand_tile(index, carry):
            here = pl.ds(pl.multiple_of(index * third, third), third)
            lhs = arena[x_base : x_base + all_rows, here]
            experts[number][here, :] = dot_tn(lhs, r.grad_gate_up[:, : 2 * size]).astype(BF16)
            return carry

        lax.fori_loop(0, 3, expand_tile, 0)

    expand_sums = [
        ChainSum(
            wires,
            n_dp,
            expand_place(number),
            functools.partial(lambda ref, j: ref.at[j], land),
            "sum_expand",
            r.stage.at[pl.ds(0, plane_rows), pl.ds(0, 2 * chunks[number][1])],
            r.local_sems.at[5],
        )
        for number, land in enumerate((r.land_0, r.land_1, r.land_2))
    ]
    contract_sum = ChainSum(
        wires,
        n_dp,
        contract_place,
        lambda j: r.land_c.at[j],
        "sum_contract",
        r.stage.at[pl.ds(0, padded)],
        r.local_sems.at[5],
    )
    complete = [
        [
            j
            for j in range(n_dp)
            if begin < (j + 1) * padded <= begin + size
        ]
        for begin, size in chunks
    ]

    def near_x():
        tokens_gather.relay()
        tokens_gather.relay_core()
        cotangent_gather.relay_core()
        tokens_gather.wait_core_x()
        cotangent_gather.wait_core_x()

    def near_y():
        tokens_gather.wait_core_y()
        cotangent_gather.wait_core_y()

    def diagonal():
        tokens_gather.relay_last()
        cotangent_gather.relay_last()
        tokens_gather.wait_last()
        cotangent_gather.wait_last()

    chunk(0, {2: near_x, 4: near_y, 6: diagonal})
    expand_chains[1].hop(1)
    expand_chains[2].hop(0)
    wires.drain("expand_0", "contract")
    weight_grads(0)
    for step in range(2, n_dp - 1):
        expand_chains[1].hop(step)
    expand_sums[0].level(0)
    contract_sum.level(0, complete[0])
    expand_chains[2].hop(1)
    chunk(1, {})
    for step in range(2, n_dp - 1):
        expand_chains[2].hop(step)
    wires.drain("expand_1")
    expand_sums[0].level(1)
    contract_sum.level(1, complete[0])
    weight_grads(1)
    expand_sums[1].level(0)
    contract_sum.level(0, complete[1])
    chunk(2, {})
    wires.drain("expand_2", "tokens", "cotangent")
    plane_sums = [
        PlaneSum(wires, arena, base, rows, r.cores.at[i], r.diag.at[i], r.sides.at[i], "plane")
        for i, base in enumerate((branch_base, back_base))
    ]
    for k in (3, 1, 2, 0):
        for one in reversed(plane_sums):
            one.send_core(k)
    for level in range(2, n_dp - 1):
        expand_sums[0].level(level)
        contract_sum.level(level, complete[0])
    expand_sums[1].level(1)
    contract_sum.level(1, complete[1])
    weight_grads(2)
    get_output = load(r.output_kept, arena.at[pl.ds(output_again, QD)], 2)
    get_cotangent = load(r.cotangent, r.branch_low, 3)
    expand_sums[2].level(0)
    contract_sum.level(0, complete[2])

    def add_core(k):
        copies = [one.fetch_core(k, r.core_stage.at[i, pl.ds(0, rows)], r.local_sems.at[6 + i]) for i, one in enumerate(plane_sums)]
        for i, one in enumerate(plane_sums):
            copies[i].wait()
            one.add_core(k, r.core_stage.at[i, pl.ds(0, rows)])

    add_core(3)
    for one in reversed(plane_sums):
        one.send_diag()
    add_core(1)
    for one in reversed(plane_sums):
        one.send_x()
    add_core(2)
    for one in reversed(plane_sums):
        one.send_y()
    add_core(0)
    for level in range(2, n_dp - 1):
        expand_sums[1].level(level)
        contract_sum.level(level, complete[1])
    for one in reversed(plane_sums):
        one.send_second()
    expand_sums[2].level(1)
    contract_sum.level(1, complete[2])
    grad_normed = plane_sums[1].total()
    middle = r.middle[...]
    grad_middle, gain_two = norm_backward(
        middle, norm_scale(middle), r.gains_full[1:2, :], grad_normed
    )
    get_cotangent.wait()
    grad_middle = grad_middle + r.branch_low[...].astype(F32)
    r.block_out[...] = (middle + plane_sums[0].total()).astype(BF16)
    r.middle[...] = grad_middle
    r.branch_low[...] = grad_middle.astype(BF16)
    output_sum, qkv_sum = (
        SlotSum(
            wires,
            n_dp,
            arena,
            base,
            size,
            cores,
            diag,
            sides,
            land,
            tag,
            r.core_stage.at[number, pl.ds(0, n_dp * size)],
            r.local_sems.at[6 + number],
        )
        for base, size, cores, diag, sides, land, tag, number in (
            (0, share_out, r.output_cores, r.output_diag, r.output_sides, r.output_land, "output", 0),
            (n_all * share_out, folded, r.qkv_cores, r.qkv_diag, r.qkv_sides, r.qkv_land, "qkv", 1),
        )
    )
    gains_sum = SlotSum(
        wires, n_dp, r.gain_slots, 0, 8, r.gain_cores, r.gain_diag, r.gain_sides, r.gain_land, "gains"
    )
    for j in range(n_dp):
        first = 8 * share_out * j
        part = dot_tn(r.mixture[:, first : first + 8 * share_out], r.branch_low[...]).astype(BF16)
        for k in range(4):
            for e in range(2):
                slot = ((e * 4 + k) * n_dp + j) * share_out
                inner = (k * 2 + e) * share_out
                arena[slot : slot + share_out, :] = part[inner : inner + share_out, :]
    output_sum.send_core()
    get_output.wait()
    r.grad_mixture[...] = dot_nt(
        r.branch_low[...], arena[output_again : output_again + QD, :]
    ).astype(BF16)
    r.grad_window[...] = jnp.zeros_like(r.grad_window)

    def head_back(h, carry):
        mine = pl.ds(pl.multiple_of(h * HD, HD), HD)
        probs = jnp.exp(scores_of(h) - r.log_totals[h])
        grad_mixture = r.grad_mixture[:, mine]
        grad_probs = dot_nt(grad_mixture, r.window[:, HD : 2 * HD])
        row_dot = jnp.sum(probs * grad_probs, axis=-1, keepdims=True)
        grad_scores = (probs * (grad_probs - row_dot)).astype(BF16)
        grad_queries = dot_nn(grad_scores, r.window[:, 0:HD]) * scale
        r.grad_projected[:, mine] = grad_queries.astype(BF16)
        r.grad_window[:, 0:HD] += dot_tn(grad_scores, r.queries[:, mine]) * scale
        r.grad_window[:, HD : 2 * HD] += dot_tn(probs.astype(BF16), grad_mixture)
        return carry

    lax.fori_loop(0, HQ, head_back, 0)
    r.window_out[...] = r.grad_window[0:WINDOW, :].astype(BF16)
    later = []
    for distance in range(1, reach + 1):
        after, before = me + distance, me - distance
        index = kv_index + reach + distance - 1
        first = WINDOW - distance * rows
        wires.send(
            r.window_out.at[pl.ds(first, rows)],
            r.window_in.at[distance - 1],
            device_at(jnp.clip(before, 0, n_all - 1)),
            index,
            before >= 0,
            "window",
        )
        later.append(
            (r.window_in.at[distance - 1], device_at(jnp.clip(after, 0, n_all - 1)), index, after <= n_all - 1)
        )
    output_sum.send_first()
    for level in range(2, n_dp - 1):
        expand_sums[2].level(level)
        contract_sum.level(level, complete[2])
    for arrival in later:
        wires.wait(*arrival)

        @pl.when(arrival[3])
        def _(arrival=arrival):
            r.grad_window[WINDOW:, :] += arrival[0][...].astype(F32)

    r.grad_projected[:, QD:] = r.grad_window[WINDOW:, :].astype(BF16)
    output_sum.send_second()
    grad_normed = dot_nt(r.grad_projected[...], r.qkv_full[...])

    def qkv_tile(index, carry):
        here = pl.ds(pl.multiple_of(index * 128, 128), 128)
        r.qkv_full[here, :] = dot_tn(r.normed[:, here], r.grad_projected[...]).astype(BF16)
        return carry

    lax.fori_loop(0, features // 128, qkv_tile, 0)
    for j in range(n_dp):
        for k in range(4):
            for e in range(2):
                d = (j * 4 + k) * 2 + e
                slot = n_all * share_out + ((e * 4 + k) * n_dp + j) * folded
                fold(arena, slot, r.qkv_full, share * d, share)
    qkv_sum.send_core()
    inputs = r.tokens[...].astype(F32)
    grad_inputs, gain_one = norm_backward(
        inputs, norm_scale(inputs), r.gains_full[0:1, :], grad_normed
    )
    r.middle[...] = r.middle[...] + grad_inputs
    put_input_grad = load(r.middle, r.input_grad, 0)
    r.gain_slots[...] = jnp.zeros_like(r.gain_slots)
    for j in range(n_dp):
        for k in range(4):
            for e in range(2):
                d = (j * 4 + k) * 2 + e
                slot = ((e * 4 + k) * n_dp + j) * 8
                for row, gain in enumerate((gain_one, gain_two)):
                    r.gain_slots[slot + row : slot + row + 1, 0:share] = gain[
                        :, share * d : share * (d + 1)
                    ]
    gains_sum.send_core()
    output_sum.add_sides()
    output_sum.chain.level(0)
    for number, one in enumerate(expand_sums):
        one.collect()
        size = 2 * chunks[number][1]
        r.stage[0:plane_rows, 0:size] = expand_place(number)(q)[...]
        for group in range(8):
            r.pieces_out[group, :, starts[number] : starts[number] + size] = r.stage[
                share * group : share * (group + 1), 0:size
            ]
    give_back = Exchange(wires, r.pieces_out, r.pieces_in, r.local_sems.at[4], "give_back")
    give_back.start()
    qkv_sum.send_first()
    gains_sum.send_first()
    contract_sum.collect()
    r.sum_contract[...] = contract_place(q)[...][0:ff_block, :]
    output_sum.chain.level(1)
    qkv_sum.send_second()
    gains_sum.send_second()
    for level in range(2, n_dp - 1):
        output_sum.chain.level(level)
    give_back.finish()
    for group, source, size, number, place in pieces:
        at = starts[number] + place
        r.sum_expand[:, source : source + size] = r.pieces_in[group, :, at : at + size]
    for one in (qkv_sum, gains_sum):
        one.add_sides()
    for level in range(n_dp - 1):
        qkv_sum.chain.level(level)
        gains_sum.chain.level(level)
    for one in (output_sum, qkv_sum, gains_sum):
        one.chain.collect()
    r.sum_output[...] = output_sum.chain.own(q)[...].astype(F32)
    r.own_qkv[...] = qkv_sum.chain.own(q)[...]
    unfold(r.sum_qkv, 0, share, r.own_qkv, 0)
    r.sum_gains[...] = gains_sum.chain.own(q)[...]
    put_input_grad.wait()
    wires.drain()


def run_block(n_dp, tokens, cotangent, qkv, output, gains, expand, contract):
    n_all = 8 * n_dp
    rows, features = tokens.shape
    share, wide = qkv.shape
    share_out = output.shape[0]
    ff_block = contract.shape[0]
    plane_rows = 8 * share
    folded = share + share // 3
    padded, width, chunks, pieces = hidden_layout(n_dp, ff_block)
    largest = max(size for _, size in chunks)
    hbm, vmem = pl.BlockSpec(memory_space=pl.ANY), pl.BlockSpec(memory_space=pltpu.VMEM)
    outs = {
        "block_out": ((rows, features), BF16),
        "input_grad": ((rows, features), F32),
        "sum_qkv": ((share, wide), F32),
        "sum_output": ((share_out, features), F32),
        "sum_gains": ((8, 128), F32),
        "sum_expand": (expand.shape, BF16),
        "sum_contract": ((ff_block, features), BF16),
    }
    lands = {
        "land_%d" % i: ((n_dp + 1, plane_rows, 2 * size), BF16) for i, (_, size) in enumerate(chunks)
    }
    lands["land_c"] = ((n_dp + 1, padded, features), BF16)
    lands["cores"] = ((2, 4, rows, features), BF16)
    lands["output_kept"] = ((QD, features), BF16)
    lands["output_cores"] = ((4 * n_dp * share_out, features), BF16)
    lands["qkv_cores"] = ((4 * n_dp * folded, features), BF16)

    def sums(name, size, columns, dtype):
        return {
            name + "_diag": ((n_dp * size, columns), dtype),
            name + "_sides": ((2 * n_dp * size, columns), dtype),
            name + "_land": (((n_dp + 1) * size, columns), dtype),
        }

    scratch = {
        "arena": ((32 * rows, features), BF16),
        "expand_0": ((features, 2 * chunks[0][1]), BF16),
        "expand_1": ((features, 2 * chunks[1][1]), BF16),
        "expand_2": ((features, 2 * chunks[2][1]), BF16),
        "contract_all": ((width, features), BF16),
        "hidden": ((8 * rows, largest), BF16),
        "grad_gate_up": ((8 * rows, 2 * largest), BF16),
        "stage": ((max(plane_rows, padded), max(features, 2 * largest)), BF16),
        "core_stage": ((2, max(rows, n_dp * folded), features), BF16),
        "diag": ((2, 2, rows // 2, features), BF16),
        "sides": ((2, 2, rows, features), BF16),
        "pieces_out": ((8, share, 2 * width), BF16),
        "pieces_in": ((8, share, 2 * width), BF16),
        "own_qkv": ((folded, features), BF16),
        "gain_slots": ((n_all * 8, 128), F32),
        "gains_full": ((8, features), F32),
        "qkv_full": ((features, wide), BF16),
        "normed": ((rows, features), BF16),
        "queries": ((rows, QD), BF16),
        "window": ((WINDOW + rows, 2 * HD), BF16),
        "log_totals": ((HQ, rows, 1), F32),
        "mixture": ((rows, QD), BF16),
        "middle": ((rows, features), F32),
        "branch_low": ((rows, features), BF16),
        "grad_mixture": ((rows, QD), BF16),
        "grad_window": ((WINDOW + rows, 2 * HD), F32),
        "window_out": ((WINDOW, 2 * HD), BF16),
        "window_in": ((WINDOW // rows, rows, 2 * HD), BF16),
        "grad_projected": ((rows, wide), BF16),
        **sums("output", share_out, features, BF16),
        **sums("qkv", folded, features, BF16),
        **sums("gain", 8, 128, F32),
        "gain_cores": ((4 * n_dp * 8, 128), F32),
    }
    names = (*INPUTS, *outs, *lands, *scratch, "local_sems", "send_sems", "recv_sems")
    results = pl.pallas_call(
        functools.partial(block_kernel, n_dp, names),
        out_shape=[jax.ShapeDtypeStruct(*s) for s in (*outs.values(), *lands.values())],
        in_specs=[vmem, hbm, vmem, vmem, vmem, hbm, hbm],
        out_specs=[hbm if name == "input_grad" else vmem for name in outs] + [hbm] * len(lands),
        scratch_shapes=[pltpu.VMEM(*s) for s in scratch.values()]
        + [
            pltpu.SemaphoreType.DMA((8,)),
            pltpu.SemaphoreType.DMA((WIRES,)),
            pltpu.SemaphoreType.DMA((WIRES,)),
        ],
        compiler_params=pltpu.CompilerParams(
            collective_id=0, has_side_effects=True, vmem_limit_bytes=VMEM_LIMIT
        ),
        name="transformer_block",
    )(tokens, cotangent, qkv, output, gains, expand, contract)
    return results[: len(outs)]


def adamw_update(weight, gradient, first, second, rate, decay_rate):
    mean_new = BETA_FIRST * first + (1.0 - BETA_FIRST) * gradient
    square_new = BETA_SECOND * second + (1.0 - BETA_SECOND) * gradient * gradient
    mean_hat = mean_new / (1.0 - BETA_FIRST**STEP)
    square_hat = square_new / (1.0 - BETA_SECOND**STEP)
    updated = weight - rate * (
        mean_hat / (jnp.sqrt(square_hat) + ADAM_EPSILON) + decay_rate * weight
    )
    return (updated, mean_new, square_new)


def shards_kernel(tokens, cotangent, *arguments):
    weights, firsts, seconds = arguments[:5], arguments[5:10], arguments[10:15]
    qkv, output, expand, contract, gains = weights
    share = gains.shape[1]
    gains_tile = jnp.pad(gains.astype(F32), ((0, 6), (0, 128 - share)))
    block_out, input_grad, *sums = run_block(
        lax.axis_size("ctx") // 2, tokens, cotangent, qkv, output, gains_tile, expand, contract
    )
    sum_qkv, sum_output, sum_gains, sum_expand, sum_contract = sums
    gradients = (sum_qkv, sum_output, sum_expand, sum_contract, sum_gains[:2, :share])
    rates = (RATE_MATRIX,) * 4 + (RATE_GAINS,)
    decays = (WEIGHT_DECAY,) * 4 + (0.0,)
    updates = [
        adamw_update(weight.astype(F32), gradient.astype(F32), first, second, rate, decay)
        for weight, gradient, first, second, rate, decay in zip(
            weights, gradients, firsts, seconds, rates, decays
        )
    ]
    return (
        block_out,
        input_grad,
        *(new for new, _, _ in updates),
        *(mean for _, mean, _ in updates),
        *(square for _, _, square in updates),
    )


def passed_along(block, axis, distance):
    devices = range(lax.axis_size(axis))
    route = [(i - distance, i) for i in devices if i - distance in devices]
    return lax.ppermute(block, axis, route)


def norm_forward(values, gain_row):
    scale = norm_scale(values)
    return (values * scale * gain_row, scale)


def shards_plain(
    tokens,
    cotangent,
    qkv_weight,
    output_weight,
    expand_weight,
    contract_weight,
    norm_gains,
    first_qkv,
    first_output,
    first_expand,
    first_contract,
    first_gains,
    second_qkv,
    second_output,
    second_expand,
    second_contract,
    second_gains,
):
    tok_dev = tokens.shape[0]
    n_fsdp = lax.axis_size("fsdp")
    n_ctx = lax.axis_size("ctx")
    ff_block = FF // (n_ctx * n_fsdp)
    score_scale = 1.0 / math.sqrt(HD)
    fsdp_index = lax.axis_index("fsdp")
    ctx_index = lax.axis_index("ctx")
    qkv_full, output_full, gains_full = (
        lax.all_gather(qkv_weight, ("ctx", "fsdp"), axis=0, tiled=True),
        lax.all_gather(output_weight, ("ctx", "fsdp"), axis=0, tiled=True),
        lax.all_gather(norm_gains, ("ctx", "fsdp"), axis=1, tiled=True),
    )
    arranged = expand_weight.reshape(expand_weight.shape[0], 2, n_ctx, n_fsdp, ff_block)
    arranged = lax.all_to_all(arranged, "fsdp", split_axis=3, concat_axis=0, tiled=True)
    arranged = arranged.reshape(arranged.shape[0], 2 * n_ctx * ff_block)
    expand_use, contract_use = (
        lax.all_gather(arranged, "ctx", axis=0, tiled=True),
        lax.all_gather(contract_weight, "ctx", axis=0, tiled=True),
    )
    width = n_ctx * ff_block
    gains_float = gains_full.astype(jnp.float32)
    inputs = tokens.astype(jnp.float32)
    normed, scale_one = norm_forward(inputs, gains_float[0])
    normed_low = normed.astype(jnp.bfloat16)
    projected = jnp.dot(normed_low, qkv_full, preferred_element_type=jnp.float32).astype(
        jnp.bfloat16
    )
    queries = projected[:, : HQ * HD].reshape(tok_dev, HQ, HD)
    key_value = projected[:, HQ * HD :]
    reach = (WINDOW + tok_dev - 1) // tok_dev
    earlier_pieces = []
    for distance in range(reach, 0, -1):
        earlier_pieces.append(passed_along(key_value, ("ctx", "fsdp"), distance))
    earlier = jnp.concatenate(earlier_pieces, axis=0)
    window_kv = jnp.concatenate([earlier, key_value], axis=0)
    key_rows = window_kv[:, :HD]
    value_rows = window_kv[:, HD:]
    offset = (ctx_index * n_fsdp + fsdp_index) * tok_dev
    row_index = lax.broadcasted_iota(jnp.int32, (tok_dev, WINDOW + tok_dev), 0)
    col_index = lax.broadcasted_iota(jnp.int32, (tok_dev, WINDOW + tok_dev), 1)
    visible = (
        (col_index > row_index) & (col_index <= row_index + WINDOW) & (col_index + offset >= WINDOW)
    )

    def masked_scores():
        raw_scores = (
            jnp.einsum("qhd,kd->hqk", queries, key_rows, preferred_element_type=jnp.float32)
            * score_scale
        )
        return jnp.where(visible[None], raw_scores, MASKED_SCORE)

    scores = masked_scores()
    log_total = jax.nn.logsumexp(scores, axis=-1, keepdims=True)
    probs_low = jnp.exp(scores - log_total).astype(jnp.bfloat16)
    mixture = jnp.einsum("hqk,kd->qhd", probs_low, value_rows, preferred_element_type=jnp.float32)
    mixture_low = mixture.reshape(tok_dev, HQ * HD).astype(jnp.bfloat16)
    middle = inputs + jnp.dot(mixture_low, output_full, preferred_element_type=jnp.float32)
    normed_two, scale_two = norm_forward(middle, gains_float[1])
    normed_two_low = normed_two.astype(jnp.bfloat16)
    ffn_input, ffn_cotangent = (
        lax.all_gather(normed_two_low, "fsdp", axis=0, tiled=True),
        lax.all_gather(cotangent, "fsdp", axis=0, tiled=True),
    )
    gate_up = jnp.dot(ffn_input, expand_use, preferred_element_type=jnp.float32)
    gate_part = gate_up[:, :width]
    up_part = gate_up[:, width:]
    activated, gelu_back = jax.vjp(functools.partial(jax.nn.gelu, approximate=True), gate_part)
    hidden_low = (activated * up_part).astype(jnp.bfloat16)
    branch_two = jnp.dot(hidden_low, contract_use, preferred_element_type=jnp.float32)
    branch_two = lax.psum_scatter(
        branch_two.astype(jnp.bfloat16), "fsdp", scatter_dimension=0, tiled=True
    ).astype(jnp.float32)
    result = middle + branch_two
    block_out = result.astype(jnp.bfloat16)
    grad_result = cotangent.astype(jnp.float32)
    grad_contract = jnp.einsum(
        "tf,td->fd", hidden_low, ffn_cotangent, preferred_element_type=jnp.float32
    )
    grad_hidden = jnp.einsum(
        "td,fd->tf", ffn_cotangent, contract_use, preferred_element_type=jnp.float32
    )
    (grad_gate,) = gelu_back(grad_hidden * up_part)
    grad_gate_up = jnp.concatenate([grad_gate, grad_hidden * activated], axis=1).astype(
        jnp.bfloat16
    )
    grad_expand = jnp.einsum(
        "td,tf->df", ffn_input, grad_gate_up, preferred_element_type=jnp.float32
    )
    grad_normed_two = jnp.einsum(
        "tf,df->td", grad_gate_up, expand_use, preferred_element_type=jnp.float32
    )
    grad_normed_two = lax.psum_scatter(grad_normed_two, "fsdp", scatter_dimension=0, tiled=True)
    part_expand, sum_contract = (
        lax.psum_scatter(
            grad_expand.astype(jnp.bfloat16), "ctx", scatter_dimension=0, tiled=True
        ).astype(jnp.float32),
        lax.psum_scatter(
            grad_contract.astype(jnp.bfloat16), "ctx", scatter_dimension=0, tiled=True
        ).astype(jnp.float32),
    )
    part_expand = part_expand.reshape(part_expand.shape[0], 2, n_ctx, 1, ff_block)
    sum_expand = lax.all_to_all(part_expand, "fsdp", split_axis=0, concat_axis=3, tiled=True)
    sum_expand = sum_expand.reshape(sum_expand.shape[0], 2 * FF)
    grad_norm_two, gain_grad_two = norm_backward(middle, scale_two, gains_float[1], grad_normed_two)
    grad_middle = grad_result + grad_norm_two
    grad_branch = grad_middle.astype(jnp.bfloat16)
    grad_output = jnp.einsum(
        "tc,td->cd", mixture_low, grad_branch, preferred_element_type=jnp.float32
    )
    grad_mixture = jnp.einsum(
        "td,cd->tc", grad_branch, output_full, preferred_element_type=jnp.float32
    )
    grad_mixture = grad_mixture.astype(jnp.bfloat16).reshape(tok_dev, HQ, HD)
    again_scores = masked_scores()
    again_probs = jnp.exp(again_scores - log_total)
    again_low = again_probs.astype(jnp.bfloat16)
    grad_probs = jnp.einsum(
        "qhd,kd->hqk", grad_mixture, value_rows, preferred_element_type=jnp.float32
    )
    row_dot = jnp.sum(again_probs * grad_probs, axis=-1, keepdims=True)
    grad_scores = (again_probs * (grad_probs - row_dot)).astype(jnp.bfloat16)
    grad_queries = (
        jnp.einsum("hqk,kd->qhd", grad_scores, key_rows, preferred_element_type=jnp.float32)
        * score_scale
    )
    grad_keys = (
        jnp.einsum("hqk,qhd->kd", grad_scores, queries, preferred_element_type=jnp.float32)
        * score_scale
    )
    grad_values = jnp.einsum(
        "hqk,qhd->kd", again_low, grad_mixture, preferred_element_type=jnp.float32
    )
    grad_window = jnp.concatenate([grad_keys, grad_values], axis=1)
    grad_key_value = grad_window[WINDOW:]
    grad_earlier = jnp.concatenate(
        [jnp.zeros((reach * tok_dev - WINDOW, 2 * HD), jnp.float32), grad_window[:WINDOW]], axis=0
    )
    for position in range(reach):
        piece = grad_earlier[position * tok_dev : (position + 1) * tok_dev]
        grad_key_value = grad_key_value + passed_along(
            piece.astype(jnp.bfloat16), ("ctx", "fsdp"), position - reach
        ).astype(piece.dtype)
    grad_projected = jnp.concatenate(
        [grad_queries.reshape(tok_dev, HQ * HD), grad_key_value], axis=1
    ).astype(jnp.bfloat16)
    grad_qkv = jnp.einsum(
        "td,tc->dc", normed_low, grad_projected, preferred_element_type=jnp.float32
    )
    grad_normed = jnp.einsum(
        "tc,dc->td", grad_projected, qkv_full, preferred_element_type=jnp.float32
    )
    grad_norm_one, gain_grad_one = norm_backward(inputs, scale_one, gains_float[0], grad_normed)
    input_grad = grad_middle + grad_norm_one
    grad_gains = jnp.concatenate([gain_grad_one, gain_grad_two], axis=0)
    sum_qkv, sum_output, sum_gains = (
        lax.psum_scatter(grad_qkv, ("ctx", "fsdp"), scatter_dimension=0, tiled=True),
        lax.psum_scatter(grad_output, ("ctx", "fsdp"), scatter_dimension=0, tiled=True),
        lax.psum_scatter(grad_gains, ("ctx", "fsdp"), scatter_dimension=1, tiled=True),
    )
    new_qkv, mean_qkv, square_qkv = adamw_update(
        qkv_weight.astype(jnp.float32), sum_qkv, first_qkv, second_qkv, RATE_MATRIX, WEIGHT_DECAY
    )
    new_output, mean_output, square_output = adamw_update(
        output_weight.astype(jnp.float32),
        sum_output,
        first_output,
        second_output,
        RATE_MATRIX,
        WEIGHT_DECAY,
    )
    new_expand, mean_expand, square_expand = adamw_update(
        expand_weight.astype(jnp.float32),
        sum_expand,
        first_expand,
        second_expand,
        RATE_MATRIX,
        WEIGHT_DECAY,
    )
    new_contract, mean_contract, square_contract = adamw_update(
        contract_weight.astype(jnp.float32),
        sum_contract,
        first_contract,
        second_contract,
        RATE_MATRIX,
        WEIGHT_DECAY,
    )
    new_gains, mean_gains, square_gains = adamw_update(
        norm_gains.astype(jnp.float32), sum_gains, first_gains, second_gains, RATE_GAINS, 0.0
    )
    return (
        block_out,
        input_grad,
        new_qkv,
        new_output,
        new_expand,
        new_contract,
        new_gains,
        mean_qkv,
        mean_output,
        mean_expand,
        mean_contract,
        mean_gains,
        square_qkv,
        square_output,
        square_expand,
        square_contract,
        square_gains,
    )


def shards(*arguments):
    plane_rows = 8 * arguments[4].shape[0]
    return (shards_kernel if plane_rows % 16 == 0 else shards_plain)(*arguments)


def solution(mesh):
    rows, columns = P(("ctx", "fsdp"), None), P(None, ("ctx", "fsdp"))
    in_specs = (rows,) * 6 + (columns,) + ((rows,) * 4 + (columns,)) * 2
    out_specs = (rows,) * 2 + ((rows,) * 4 + (columns,)) * 3
    return jax.shard_map(shards, mesh=mesh, in_specs=in_specs, out_specs=out_specs, check_vma=False)
```

```python
import functools
import math
import types

import jax
import jax.numpy as jnp
from jax import lax
from jax.experimental import pallas as pl
from jax.experimental.pallas import tpu as pltpu
from jax.sharding import PartitionSpec as P

HQ = 4
HD = 256
FF = 6912
WINDOW = 512
STEP = 10

NORM_EPSILON = 1e-06
BETA_FIRST = 0.9
BETA_SECOND = 0.999
RATE_MATRIX = 0.1
RATE_GAINS = 0.5
WEIGHT_DECAY = 0.1
ADAM_EPSILON = 1e-08
MASKED_SCORE = -1e30

F32 = jnp.float32
BF16 = jnp.bfloat16
MESH = pl.DeviceIdType.MESH
VMEM_LIMIT = 65400 * 1024
WIRES = 400
QD = HQ * HD


def position():
    ctx, fsdp = lax.axis_index("ctx"), lax.axis_index("fsdp")
    return ctx // 2, lax.rem(ctx, 2), fsdp // 2, lax.rem(fsdp, 2)


def device(q, y, x, c):
    return (q * 2 + y, x * 2 + c)


def device_at(index):
    return (index // 4, lax.rem(index, 4))


def rows_of(ref, first, count):
    if not isinstance(first, int):
        first = pl.multiple_of(first, 16 if ref.dtype == BF16 else 8)
    return ref.at[pl.ds(first, count)]


def gelu_parts(u):
    k = math.sqrt(2.0 / math.pi)
    square = u * u
    t = jnp.tanh(k * u * (1.0 + 0.044715 * square))
    half = 0.5 * (1.0 + t)
    slope = half + 0.5 * u * (1.0 - t * t) * (k * (1.0 + (3.0 * 0.044715) * square))
    return u * half, slope


def dot_nt(a, b):
    return lax.dot_general(a, b, (((1,), (1,)), ((), ())), preferred_element_type=F32)


def dot_tn(a, b):
    return lax.dot_general(a, b, (((0,), (0,)), ((), ())), preferred_element_type=F32)


def dot_nn(a, b):
    return jnp.dot(a, b, preferred_element_type=F32)


def norm_scale(values):
    return lax.rsqrt(jnp.mean(values * values, axis=-1, keepdims=True) + NORM_EPSILON)


def norm_backward(values, scale, gain_row, grad_normed):
    gain_grad = jnp.sum(grad_normed * values * scale, axis=0, keepdims=True)
    scaled = grad_normed * gain_row
    cubed = scale * scale * scale
    grad_values = scale * scaled - values * cubed * jnp.mean(
        scaled * values, axis=-1, keepdims=True
    )
    return grad_values, gain_grad


class Wires:
    def __init__(self, send_sems, recv_sems):
        self.send_sems, self.recv_sems = send_sems, recv_sems
        self.count = 0
        self.sent = {}
        self.tag = None

    def take(self, number=1):
        first = self.count
        self.count += number
        assert self.count <= WIRES, self.count
        return first

    def copy(self, src, dst, target, index, send_index=None):
        return pltpu.make_async_remote_copy(
            src_ref=src,
            dst_ref=dst,
            send_sem=self.send_sems.at[index if send_index is None else send_index],
            recv_sem=self.recv_sems.at[index],
            device_id=target,
            device_id_type=MESH,
        )

    def send(self, src, dst, target, index, when=None, tag=None, send_index=None):
        def make():
            here, there, other = (v() if callable(v) else v for v in (src, dst, target))
            return self.copy(here, there, other, index, send_index)

        self.run(lambda: make().start(), when)
        self.sent.setdefault(tag, []).append((lambda: make().wait_send(), when))

    def run(self, action, when):
        if when is None:
            action()
        else:
            pl.when(when() if callable(when) else when)(action)

    def wait(self, dst, target, index, when=None):
        copy = self.copy(dst, dst, target, index)
        if when is None:
            copy.wait_recv()
        else:
            pl.when(when)(copy.wait_recv)

    def drain(self, *tags):
        for tag in tags or list(self.sent):
            for action, when in self.sent.pop(tag, ()):
                self.run(action, when)


def greet(n_dp, reach):
    q, y, x, c = position()
    barrier = pltpu.get_barrier_semaphore()
    expected = 0

    def signal(target):
        pl.semaphore_signal(barrier, inc=1, device_id=target, device_id_type=MESH)

    for dy in range(2):
        for dx in range(2):
            for dc in range(2):
                if dy + dx + dc:
                    signal(device(q, (y + dy) % 2, (x + dx) % 2, (c + dc) % 2))
                    expected += 1
    me = (q * 2 + y) * 4 + x * 2 + c
    last = 8 * n_dp - 1
    for distance in range(1, reach + 1):
        for other in (me - distance, me + distance):
            here = (other >= 0) & (other <= last)
            pl.when(here)(functools.partial(signal, device_at(jnp.clip(other, 0, last))))
            expected = expected + here.astype(jnp.int32)
    for step in range(1, n_dp):
        signal(device(lax.rem(q + step, n_dp), y, x, c))
        expected = expected + 1
    pl.semaphore_wait(barrier, expected)


class Plane:
    def __init__(self):
        self.q, self.y, self.x, self.c = q, y, x, c = position()
        self.chips = [y * 2 + x, y * 2 + 1 - x, (1 - y) * 2 + x, (1 - y) * 2 + 1 - x]
        self.chip, self.chip_x, self.chip_y, self.chip_d = self.chips
        self.to_x, self.to_y = device(q, y, 1 - x, c), device(q, 1 - y, x, c)
        self.to_c = device(q, y, x, 1 - c)


class Chain:
    def __init__(self, wires, n_dp, own, place, tag):
        self.wires, self.n_dp, self.own, self.place, self.tag = wires, n_dp, own, place, tag
        self.first = {way: wires.take(n_dp - 1) for way in (1, -1)}

    def valid(self, way, step):
        q = position()[0]
        return (q - 1 - step >= 0) if way == 1 else (q + 1 + step <= self.n_dp - 1)

    def send(self, way, step):
        last = self.n_dp - 1

        def block():
            return jnp.clip(position()[0] - way * step, 0, last)

        def place():
            return self.place(block())

        def target():
            q, y, x, c = position()
            return device(jnp.clip(q + way, 0, last), y, x, c)

        def here():
            q = position()[0]
            origin = q - way * step
            return (origin >= 0) & (origin <= last) & (q + way >= 0) & (q + way <= last)

        src = self.own if step == 0 else place
        self.wires.send(src, place, target, self.first[way] + step, here, self.tag)

    def wait(self, way, step):
        q, y, x, c = position()
        block = jnp.clip(q - way * (step + 1), 0, self.n_dp - 1)
        self.wires.wait(
            self.place(block),
            device(jnp.clip(q + way, 0, self.n_dp - 1), y, x, c),
            self.first[way] + step,
            self.valid(way, step),
        )
        if step + 1 < self.n_dp - 1:
            self.send(way, step + 1)

    def start(self):
        self.send(1, 0)
        self.send(-1, 0)

    def hop(self, step):
        self.wait(1, step)
        self.wait(-1, step)


class PlaneGather(Plane):
    def __init__(self, wires, own, buf, base, rows, tag):
        super().__init__()
        self.wires, self.own, self.buf, self.base, self.rows = wires, own, buf, base, rows
        self.half = rows // 2
        self.tag = tag
        (self.xa, self.xb, self.ya, self.yb, self.co, self.da, self.db) = (
            wires.take() for _ in range(7)
        )
        self.cx, self.cy, self.cd = (wires.take() for _ in range(3))

    def part(self, chip, c, which=None):
        first = self.base + (chip * 2 + c) * self.rows
        if which is None:
            return rows_of(self.buf, first, self.rows)
        return rows_of(self.buf, first + which * self.half, self.half)

    def send(self, src, dst, target, index):
        self.wires.send(src, dst, target, index, None, self.tag)

    def start(self):
        c, half = self.c, self.half
        low, high = self.own.at[pl.ds(0, half)], self.own.at[pl.ds(half, half)]
        self.send(low, self.part(self.chip, c, 0), self.to_x, self.xa)
        self.send(high, self.part(self.chip, c, 1), self.to_y, self.yb)
        self.send(high, self.part(self.chip, c, 1), self.to_x, self.xb)
        self.send(low, self.part(self.chip, c, 0), self.to_y, self.ya)
        self.send(self.own, self.part(self.chip, c), self.to_c, self.co)

    def forward(self, target, index, chip, which=None):
        def part():
            return self.part(chip, self.c, which)

        self.send(part, part, target, index)

    def relay(self):
        c, wires = self.c, self.wires
        wires.wait(self.part(self.chip_x, c, 0), self.to_x, self.xa)
        self.forward(self.to_y, self.da, self.chip_x, 0)
        wires.wait(self.part(self.chip_y, c, 1), self.to_y, self.yb)
        self.forward(self.to_x, self.db, self.chip_y, 1)

    def relay_core(self):
        c, wires = self.c, self.wires
        wires.wait(self.part(self.chip_x, c, 1), self.to_x, self.xb)
        self.forward(self.to_c, self.cx, self.chip_x)
        wires.wait(self.part(self.chip_y, c, 0), self.to_y, self.ya)
        self.forward(self.to_c, self.cy, self.chip_y)

    def relay_last(self):
        c, wires = self.c, self.wires
        wires.wait(self.part(self.chip_d, c, 0), self.to_y, self.da)
        wires.wait(self.part(self.chip_d, c, 1), self.to_x, self.db)
        self.forward(self.to_c, self.cd, self.chip_d)

    def wait_core(self):
        self.wires.wait(self.part(self.chip, 1 - self.c), self.to_c, self.co)

    def wait_core_x(self):
        self.wires.wait(self.part(self.chip_x, 1 - self.c), self.to_c, self.cx)

    def wait_core_y(self):
        self.wires.wait(self.part(self.chip_y, 1 - self.c), self.to_c, self.cy)

    def wait_last(self):
        self.wires.wait(self.part(self.chip_d, 1 - self.c), self.to_c, self.cd)


class SlotGather(Plane):
    def __init__(self, wires, n_dp, own, buf, base, rows, tag):
        super().__init__()
        self.wires, self.n_dp, self.own, self.tag = wires, n_dp, own, tag
        self.buf, self.base, self.rows = buf, base, rows
        self.order = [(0, -1)] + [(way, s) for s in range(n_dp - 1) for way in (1, -1)]
        self.chain = Chain(wires, n_dp, own, lambda j: self.slot(self.c, j, self.chip), tag)
        self.kx, self.ky, self.kd, self.kc = (wires.take(len(self.order)) for _ in range(4))

    def slot(self, c, j, chip, count=1):
        return rows_of(
            self.buf, self.base + ((c * self.n_dp + j) * 4 + chip) * self.rows, count * self.rows
        )

    def each(self, ranks):
        for rank, (way, step) in enumerate(self.order):
            if ranks is not None and rank not in ranks:
                continue
            if way == 0:
                yield rank, way, step, self.q, None
            else:
                block = jnp.clip(self.q - way * (step + 1), 0, self.n_dp - 1)
                yield rank, way, step, block, self.chain.valid(way, step)

    def start(self):
        self.chain.start()

    def spread(self, ranks=None):
        for rank, way, step, j, ok in self.each(ranks):
            if way:
                self.chain.wait(way, step)
            src = self.slot(self.c, j, self.chip) if way else self.own
            dst = self.slot(self.c, j, self.chip)
            self.wires.send(src, dst, self.to_x, self.kx + rank, ok, self.tag)
            self.wires.send(src, dst, self.to_y, self.ky + rank, ok, self.tag)

    def relay(self, ranks=None):
        for rank, way, step, j, ok in self.each(ranks):
            even = lax.rem(j, 2) == 0
            odd = jnp.logical_not(even)
            sx, sy = self.slot(self.c, j, self.chip_x), self.slot(self.c, j, self.chip_y)
            self.wires.wait(sx, self.to_x, self.kx + rank, ok)
            to_y = even if ok is None else ok & even
            self.wires.send(sx, sx, self.to_y, self.kd + rank, to_y, self.tag)
            self.wires.wait(sy, self.to_y, self.ky + rank, ok)
            to_x = odd if ok is None else ok & odd
            self.wires.send(sy, sy, self.to_x, self.kd + rank, to_x, self.tag)

    def core(self, ranks=None):
        for rank, way, step, j, ok in self.each(ranks):
            self.wires.wait(self.slot(self.c, j, self.chip_d), self.to_x, self.kd + rank, ok)
            four = self.slot(self.c, j, 0, 4)
            self.wires.send(four, four, self.to_c, self.kc + rank, ok, self.tag)

    def finish(self, ranks=None):
        for rank, way, step, j, ok in self.each(ranks):
            four = self.slot(1 - self.c, j, 0, 4)
            self.wires.wait(four, self.to_c, self.kc + rank, ok)


def add_into(mine, other):
    mine[...] = (mine[...].astype(F32) + other[...].astype(F32)).astype(mine.dtype)


class ChainSum:
    def __init__(self, wires, n_dp, own, land, tag, stage=None, stage_sem=None, straight=False):
        self.wires, self.n_dp, self.own, self.land, self.tag = wires, n_dp, own, land, tag
        self.stage, self.stage_sem, self.straight = stage, stage_sem, straight
        self.half = n_dp // 2
        self.direct, self.far, self.partial = wires.take(n_dp), wires.take(), wires.take(n_dp)

    def add(self, own, slot):
        if self.stage is None:
            add_into(own, slot)
        else:
            copy = pltpu.make_async_copy(slot, self.stage, self.stage_sem)
            copy.start()
            copy.wait()
            add_into(own, self.stage)

    def level(self, number):
        q, y, x, c = position()
        n_dp, half, wires = self.n_dp, self.half, self.wires
        low = q < half
        here = jnp.where(low, q, n_dp - 1 - q) == number
        inward = jnp.where(low, q + 1, q - 1)
        for j in [] if self.straight else [*range(n_dp - 1, half - 1, -1), *range(half)]:
            active = here & (low if j >= half else jnp.logical_not(low))
            slot = self.land(n_dp + 1 + j)
            if number:
                outward = jnp.clip(jnp.where(low, q - 1, q + 1), 0, n_dp - 1)
                wires.wait(slot, device(outward, y, x, c), self.partial + j, active)
                pl.when(active)(functools.partial(self.add, self.own(j), slot))
            if number < half - 1:
                wires.send(
                    self.own(j), slot, device(inward, y, x, c), self.partial + j, active, self.tag
                )
            else:
                wires.send(
                    self.own(j),
                    self.land(n_dp),
                    device(j, y, x, c),
                    self.far,
                    active,
                    self.tag,
                    self.partial + j,
                )
        if number == 0:
            for j in range(n_dp):
                near = self.near(j)
                wires.send(
                    self.own(j),
                    self.land(q),
                    device(j, y, x, c),
                    self.direct + q,
                    near,
                    self.tag,
                    self.direct + j,
                )

    def near(self, j):
        q = position()[0]
        low = q < self.half
        if self.straight:
            return j != q
        return (j != q) & (low if j < self.half else jnp.logical_not(low))

    def collect(self):
        q, y, x, c = position()
        low = q < self.half
        for j in range(self.n_dp):
            near = self.near(j)
            self.wires.wait(self.land(j), device(j, y, x, c), self.direct + j, near)
            pl.when(near)(functools.partial(self.add, self.own(q), self.land(j)))
        if self.straight:
            return
        center = jnp.where(low, self.half, self.half - 1)
        self.wires.wait(self.land(self.n_dp), device(center, y, x, c), self.far)
        self.add(self.own(q), self.land(self.n_dp))


class PlaneSum(Plane):
    def __init__(self, wires, buf, base, rows, cores, diag, sides, tag):
        super().__init__()
        self.wires, self.buf, self.base, self.rows, self.tag = wires, buf, base, rows, tag
        self.half = rows // 2
        self.cores, self.diag, self.sides = cores, diag, sides
        self.kc = wires.take(4)
        self.kdx, self.kdy = wires.take(), wires.take()
        self.kxa, self.kxb, self.kya, self.kyb = (wires.take() for _ in range(4))

    part = PlaneGather.part
    send = PlaneGather.send

    def send_core(self, k):
        def part():
            return self.part(self.chips[k], 1 - self.c)

        self.send(part, lambda: self.cores.at[k], self.to_c, self.kc + k)

    def fetch_core(self, k, stage, sem):
        self.wires.wait(self.cores.at[k], self.to_c, self.kc + k)
        copy = pltpu.make_async_copy(self.cores.at[k], stage, sem)
        copy.start()
        return copy

    def add_core(self, k, stage):
        add_into(self.part(self.chips[k], self.c), stage)

    def side(self, which, half):
        return self.sides.at[which, pl.ds(half * self.half, self.half)]

    def send_half(self, chip, half, dst, target, index):
        def part():
            return self.part(chip, self.c, half)

        self.send(part, dst, target, index)

    def send_diag(self):
        self.send_half(self.chip_d, 0, lambda: self.diag.at[0], self.to_x, self.kdx)
        self.send_half(self.chip_d, 1, lambda: self.diag.at[1], self.to_y, self.kdy)

    def send_x(self):
        self.send_half(self.chip_x, 0, lambda: self.side(0, 0), self.to_x, self.kxa)

    def send_y(self):
        self.send_half(self.chip_y, 1, lambda: self.side(1, 1), self.to_y, self.kyb)

    def send_second(self):
        self.wires.wait(self.diag.at[0], self.to_x, self.kdx)
        mine = self.part(self.chip_y, self.c, 0)
        add_into(mine, self.diag.at[0])
        self.send(mine, self.side(1, 0), self.to_y, self.kya)
        self.wires.wait(self.diag.at[1], self.to_y, self.kdy)
        mine = self.part(self.chip_x, self.c, 1)
        add_into(mine, self.diag.at[1])
        self.send(mine, self.side(0, 1), self.to_x, self.kxb)

    def total(self):
        self.wires.wait(self.side(0, 0), self.to_x, self.kxa)
        self.wires.wait(self.side(1, 1), self.to_y, self.kyb)
        self.wires.wait(self.side(1, 0), self.to_y, self.kya)
        self.wires.wait(self.side(0, 1), self.to_x, self.kxb)
        mine = self.part(self.chip, self.c)
        return mine[...].astype(F32) + self.sides[0].astype(F32) + self.sides[1].astype(F32)


class SlotSum(Plane):
    def __init__(
        self, wires, n_dp, buf, base, rows, cores, diag, sides, landing, tag, stage=None, sem=None
    ):
        super().__init__()
        self.wires, self.n_dp, self.tag = wires, n_dp, tag
        self.buf, self.base, self.rows = buf, base, rows
        self.cores, self.diag, self.sides = cores, diag, sides
        self.stage, self.sem = stage, sem
        self.low = n_dp // 2
        self.high = n_dp - self.low
        self.kc = wires.take(4)
        self.kdx, self.kdy, self.kx0, self.kx1, self.ky0, self.ky1 = (
            wires.take() for _ in range(6)
        )
        self.chain = ChainSum(
            wires,
            n_dp,
            lambda j: self.at(self.c, self.chip, j, 1),
            lambda j: rows_of(landing, j * rows, rows),
            tag,
            straight=True,
        )

    def at(self, c, chip, j, count):
        first = self.base + ((c * 4 + chip) * self.n_dp + j) * self.rows
        return rows_of(self.buf, first, count * self.rows)

    def four(self, ref, k):
        return ref.at[pl.ds(k * self.n_dp * self.rows, self.n_dp * self.rows)]

    def lows(self, ref, which=0):
        return ref.at[pl.ds(which * self.n_dp * self.rows, self.low * self.rows)]

    def highs(self, ref, which=0):
        first = (which * self.n_dp + self.low) * self.rows
        return ref.at[pl.ds(first, self.high * self.rows)]

    def send(self, src, dst, target, index):
        self.wires.send(src, dst, target, index, None, self.tag)

    def send_core(self):
        for k in (3, 1, 2, 0):
            src = self.at(1 - self.c, self.chips[k], 0, self.n_dp)
            self.send(src, self.four(self.cores, k), self.to_c, self.kc + k)

    def add_core(self, k):
        other = self.four(self.cores, k)
        self.wires.wait(other, self.to_c, self.kc + k)
        if self.stage is not None:
            copy = pltpu.make_async_copy(other, self.stage, self.sem)
            copy.start()
            copy.wait()
            other = self.stage
        add_into(self.at(self.c, self.chips[k], 0, self.n_dp), other)

    def send_first(self):
        low, c = self.low, self.c
        self.add_core(3)
        self.send(self.at(c, self.chip_d, 0, low), self.lows(self.diag), self.to_x, self.kdx)
        self.send(self.at(c, self.chip_d, low, self.high), self.highs(self.diag), self.to_y, self.kdy)
        self.add_core(1)
        self.send(self.at(c, self.chip_x, 0, low), self.lows(self.sides), self.to_x, self.kx0)
        self.add_core(2)
        self.send(self.at(c, self.chip_y, low, self.high), self.highs(self.sides, 1), self.to_y, self.ky1)
        self.add_core(0)

    def send_second(self):
        low, c, wires = self.low, self.c, self.wires
        wires.wait(self.lows(self.diag), self.to_x, self.kdx)
        mine = self.at(c, self.chip_y, 0, low)
        add_into(mine, self.lows(self.diag))
        self.send(mine, self.lows(self.sides, 1), self.to_y, self.ky0)
        wires.wait(self.highs(self.diag), self.to_y, self.kdy)
        mine = self.at(c, self.chip_x, low, self.high)
        add_into(mine, self.highs(self.diag))
        self.send(mine, self.highs(self.sides), self.to_x, self.kx1)

    def add_sides(self):
        wires = self.wires
        wires.wait(self.lows(self.sides), self.to_x, self.kx0)
        wires.wait(self.highs(self.sides, 1), self.to_y, self.ky1)
        wires.wait(self.lows(self.sides, 1), self.to_y, self.ky0)
        wires.wait(self.highs(self.sides), self.to_x, self.kx1)
        mine = self.at(self.c, self.chip, 0, self.n_dp)
        mine[...] = (
            mine[...].astype(F32)
            + self.four(self.sides, 0)[...].astype(F32)
            + self.four(self.sides, 1)[...].astype(F32)
        ).astype(mine.dtype)


class Exchange(Plane):
    def __init__(self, wires, pieces_out, pieces_in, local_sem, tag):
        super().__init__()
        self.wires, self.out, self.into, self.tag = wires, pieces_out, pieces_in, tag
        self.index = wires.take(7)
        self.me = self.chip * 2 + self.c
        self.copy = pltpu.make_async_copy(
            pieces_out.at[self.me], pieces_in.at[self.me], local_sem
        )

    def others(self):
        number = 0
        for dc in (0, 1):
            for dy, dx in ((1, 1), (0, 1), (1, 0), (0, 0)):
                if dy + dx + dc == 0:
                    continue
                ty, tx, tc = (self.y + dy) % 2, (self.x + dx) % 2, (self.c + dc) % 2
                yield (ty * 2 + tx) * 2 + tc, device(self.q, ty, tx, tc), self.index + number
                number += 1

    def start(self):
        for other, target, index in self.others():
            self.wires.send(
                self.out.at[other], self.into.at[self.me], target, index, None, self.tag
            )
        self.copy.start()

    def finish(self):
        for other, target, index in self.others():
            self.wires.wait(self.into.at[other], target, index)
        self.copy.wait()


def hidden_layout(n_dp, ff_block):
    unit = max(16, 128 // n_dp)
    units = -(-ff_block // unit)
    cuts = [0, -(-units * 3 // 7), -(-units * 5 // 7), units]
    chunks = [(unit * a, unit * (b - a), n_dp * unit * (b - a)) for a, b in zip(cuts, cuts[1:])]
    pieces = []
    for group in range(8):
        for part in range(2):
            for q in range(n_dp):
                source = part * FF + ff_block * (q * 8 + group)
                for number, (first, count, size) in enumerate(chunks):
                    used = min(first + count, ff_block) - first
                    place = part * size + q * count
                    pieces.append((group, source + first, used, number, place))
    return unit * units, n_dp * unit * units, chunks, pieces


INPUTS = ("tokens", "cotangent", "qkv", "output", "gains", "expand", "contract")
OUTPUTS = (
    "block_out",
    "input_grad",
    "sum_qkv",
    "sum_output",
    "sum_gains",
    "sum_expand",
    "sum_contract",
)


def fold(dst, first, src, row, share):
    wide, features = src.shape[1], dst.shape[1]
    third = share // 3
    extra = wide - features
    dst[first : first + share, :] = src[row : row + share, :features]
    for k in range(3):
        dst[first + share : first + share + third, k * extra : (k + 1) * extra] = src[
            row + third * k : row + third * (k + 1), features:
        ]


def unfold(dst, row, share, src, first):
    wide, features = dst.shape[1], src.shape[1]
    third = share // 3
    extra = wide - features
    dst[row : row + share, :features] = src[first : first + share, :].astype(dst.dtype)
    for k in range(3):
        dst[row + third * k : row + third * (k + 1), features:] = src[
            first + share : first + share + third, k * extra : (k + 1) * extra
        ].astype(dst.dtype)


def block_kernel(n_dp, names, *refs):
    r = types.SimpleNamespace(**dict(zip(names, refs, strict=True)))
    wires = Wires(r.send_sems, r.recv_sems)
    plane = Plane()
    q, y, x, c, chip = plane.q, plane.y, plane.x, plane.c, plane.chip
    me = (q * 4 + chip) * 2 + c
    n_all = 8 * n_dp
    hops = n_dp - 1
    rows, features = r.tokens.shape
    share, wide = r.qkv.shape
    share_out = r.output.shape[0]
    ff_block = r.contract.shape[0]
    plane_rows = 8 * share
    folded = share + share // 3
    padded, width, chunks, pieces = hidden_layout(n_dp, ff_block)
    experts = [r.expand_0, r.expand_1, r.expand_2]
    inners = [r.contract_0, r.contract_1, r.contract_2]
    all_rows = 8 * rows
    x_base, cot_base, branch_base, back_base = (all_rows * i for i in range(4))
    qkv_base, output_base = branch_base, branch_base + n_all * folded
    output_full, output_again = output_base + n_all * share_out, n_all * (share_out + folded)
    reach = WINDOW // rows
    scale = 1.0 / math.sqrt(HD)
    arena = r.arena
    blocks = [((j * 4 + k) * 2 + e, j, k, e) for j in range(n_dp) for k in range(4) for e in range(2)]

    def load(src, dst, number):
        copy = pltpu.make_async_copy(src, dst, r.local_sems.at[number])
        copy.start()
        return copy

    get_expand = load(r.expand, r.sum_expand, 0)
    get_contract = load(r.contract, r.sum_contract, 5)
    starts = [2 * sum(size for _, _, size in chunks[:number]) for number in range(len(chunks))]
    fold(r.own_qkv, 0, r.qkv, 0, share)
    r.pieces_out[...] = jnp.zeros_like(r.pieces_out)
    get_expand.wait()
    for group, source, size, number, place in pieces:
        at = starts[number] + place
        r.pieces_out[group, :, at : at + size] = r.sum_expand[:, source : source + size]
    get_contract.wait()

    def contract_place(number):
        count = chunks[number][1]
        return lambda j: rows_of(inners[number], j * count, count)

    def expand_place(number):
        return lambda j: rows_of(experts[number], j * plane_rows, plane_rows)

    for number, (first, count, _) in enumerate(chunks):
        used = min(first + count, ff_block) - first
        r.stage[0:used, 0:features] = r.sum_contract[first : first + used, :]
        if used < count:
            r.stage[used:count, 0:features] = jnp.zeros((count - used, features), BF16)
        contract_place(number)(q)[...] = r.stage[0:count, 0:features]
    greet(n_dp, reach)
    gains_gather = SlotGather(wires, n_dp, r.gains, r.gain_slots, 0, 8, "weights")
    qkv_gather = SlotGather(wires, n_dp, r.own_qkv, arena, qkv_base, folded, "weights")
    output_gather = SlotGather(wires, n_dp, r.output, arena, output_base, share_out, "weights")
    gathers = (gains_gather, qkv_gather, output_gather)
    firsts = (gains_gather, qkv_gather)
    ranks = len(gains_gather.order)
    for gather in firsts:
        gather.start()
        gather.spread((0,))

    def columns(number):
        return pl.ds(starts[number], 2 * chunks[number][2])

    def exchange(number, tag):
        out, into = (ref.at[:, :, columns(number)] for ref in (r.pieces_out, r.pieces_in))
        moved = Exchange(wires, out, into, r.local_sems.at[8 + number], tag)
        moved.start()
        return moved

    exchanges = [exchange(0, "pieces")]
    output_gather.start()
    own_slots = [load(g.own, g.slot(c, q, chip), 1 + i) for i, g in enumerate(gathers)]
    for gather in firsts:
        gather.spread((1, 2))
    for gather in firsts:
        gather.relay((0,))
    output_gather.spread((0,))
    for gather in firsts:
        gather.spread(range(3, ranks))

    class Chunk:
        def __init__(self, number):
            size = 2 * chunks[number][2]
            exchanges[number].finish()
            for group in range(8):
                r.stage[share * group : share * (group + 1), 0:size] = r.pieces_in[
                    group, :, starts[number] : starts[number] + size
                ]
            self.tag = "chunk_%d" % number
            self.chains = []
            for place in (expand_place(number), contract_place(number)):
                self.chains.append(Chain(wires, n_dp, place(q), place, self.tag))
            expand_place(number)(q)[...] = r.stage[0:plane_rows, 0:size]

        def start(self):
            for chain in self.chains:
                chain.start()

        def hop(self, *steps):
            for step in steps:
                for chain in self.chains:
                    chain.hop(step)

    weights = [Chunk(0)]
    weights[0].start()
    for copy in own_slots:
        copy.wait()
    for gather in firsts:
        gather.relay(range(1, ranks))
    output_gather.spread(range(1, ranks))
    exchanges.append(exchange(1, "pieces"))
    for gather in firsts:
        gather.core()
    for gather in firsts:
        gather.finish()
    for d, j, k, e in blocks:
        slot = (e * n_dp + j) * 4 + k
        unfold(r.qkv_full, share * d, share, arena, qkv_base + slot * folded)
        r.gains_full[0:2, share * d : share * (d + 1)] = r.gain_slots[
            8 * slot : 8 * slot + 2, 0:share
        ]
    inputs = r.tokens[...].astype(F32)
    r.normed[...] = (inputs * norm_scale(inputs) * r.gains_full[0:1, :]).astype(BF16)
    for first in (QD, *range(0, QD, 512)):
        part = dot_nn(r.normed[...], r.qkv_full[:, first : first + 512]).astype(BF16)
        if first < QD:
            r.queries[:, first : first + 512] = part
            continue
        r.window[WINDOW : WINDOW + rows, :] = part
        mine = r.window.at[pl.ds(WINDOW, rows)]
        kv_index = wires.take(2 * reach)
        earlier = []
        for distance in range(1, reach + 1):
            place = r.window.at[pl.ds(WINDOW - distance * rows, rows)]
            after, before = me + distance, me - distance
            index = kv_index + distance - 1
            target = device_at(jnp.clip(after, 0, n_all - 1))
            wires.send(mine, place, target, index, after <= n_all - 1, "window")

            @pl.when(before < 0)
            def _(place=place):
                place[...] = jnp.zeros_like(place)

            earlier.append((place, device_at(jnp.clip(before, 0, n_all - 1)), index, before >= 0))
    output_gather.relay()
    cotangent_gather = PlaneGather(wires, r.cotangent, arena, cot_base, rows, "cotangent")
    cotangent_gather.start()
    own_cotangent = load(r.cotangent, cotangent_gather.part(chip, c), 1)
    exchanges.append(exchange(2, "pieces"))
    output_gather.core()
    weights[0].hop(0)
    weights.append(Chunk(1))
    weights[1].start()
    output_gather.finish()
    for d, j, k, e in blocks:
        first = output_base + ((e * n_dp + j) * 4 + k) * share_out
        there = output_full + share_out * d
        arena[there : there + share_out, :] = arena[first : first + share_out, :]
    put_output = load(arena.at[pl.ds(output_full, QD)], r.output_kept, 2)
    for arrival in earlier:
        wires.wait(*arrival)
    cotangent_gather.relay()
    keys = WINDOW + rows

    def visible():
        row = lax.broadcasted_iota(jnp.int32, (rows, keys), 0)
        col = lax.broadcasted_iota(jnp.int32, (rows, keys), 1)
        return (col > row) & (col <= row + WINDOW) & (col + me * rows >= WINDOW)

    def scores_of(h):
        mine = pl.ds(pl.multiple_of(h * HD, HD), HD)
        raw = dot_nt(r.queries[:, mine], r.window[:, 0:HD]) * scale
        return jnp.where(visible(), raw, MASKED_SCORE)

    def head(h, carry):
        scores = scores_of(h)
        top = jnp.max(scores, axis=-1, keepdims=True)
        log_total = top + jnp.log(jnp.sum(jnp.exp(scores - top), axis=-1, keepdims=True))
        r.log_totals[h] = log_total
        low = jnp.exp(scores - log_total).astype(BF16)
        mine = pl.ds(pl.multiple_of(h * HD, HD), HD)
        r.mixture[:, mine] = dot_nn(low, r.window[:, HD : 2 * HD]).astype(BF16)
        return carry

    lax.fori_loop(0, HQ, head, 0)
    middle = r.tokens[...].astype(F32) + dot_nn(
        r.mixture[...], arena[output_full : output_full + QD, :]
    )
    r.middle[...] = middle
    tokens_gather = PlaneGather(wires, None, arena, x_base, rows, "tokens")
    own = tokens_gather.part(chip, c)
    tokens_gather.own = own
    own[...] = (middle * norm_scale(middle) * r.gains_full[1:2, :]).astype(BF16)
    tokens_gather.start()
    wires.drain("weights")
    own_cotangent.wait()
    put_output.wait()
    weights[0].hop(1)
    weights.append(Chunk(2))
    cotangent_gather.relay_core()
    tokens_gather.relay()
    weights[1].hop(0)
    weights[2].start()
    cotangent_gather.relay_last()
    tokens_gather.relay_core()
    for gather in (cotangent_gather, tokens_gather):
        gather.wait_core()
    for step in range(2, hops):
        weights[0].hop(step)
    chips = plane.chips

    def chunk(number, order, events):
        expand, inner = experts[number], inners[number]
        size = chunks[number][2]

        def tile(index, carry):
            for when, event in events.items():
                pl.when(index == when)(event)
            pair = index // 2
            place = chips[order[3]]
            for k in range(3):
                place = jnp.where(pair == k, chips[order[k]], place)
            offset = (place * 2 + lax.rem(index, 2)) * rows
            here = pl.ds(pl.multiple_of(offset, rows), rows)

            def at(base):
                return pl.ds(pl.multiple_of(base + offset, rows), rows)

            gate_up = dot_nn(arena[at(x_base), :], expand[...])
            grad_hidden = dot_nt(arena[at(cot_base), :], inner[...])
            gate, up = gate_up[:, :size], gate_up[:, size:]
            activated, slope = gelu_parts(gate)
            low = (activated * up).astype(BF16)
            r.hidden[here, :size] = low
            r.grad_gate_up[here, :size] = (grad_hidden * up * slope).astype(BF16)
            r.grad_gate_up[here, size : 2 * size] = (grad_hidden * activated).astype(BF16)
            out = dot_nn(low, inner[...])
            if number:
                out = out + arena[at(branch_base), :].astype(F32)
            arena[at(branch_base), :] = out.astype(BF16)
            back = dot_nt(r.grad_gate_up[here, : 2 * size], expand[...])
            if number:
                back = back + arena[at(back_base), :].astype(F32)
            arena[at(back_base), :] = back.astype(BF16)
            return carry

        lax.fori_loop(0, 8, tile, 0)

    third = features // 3

    def weight_grads(number):
        size = chunks[number][2]
        wires.drain("chunk_%d" % number)

        def contract_tile(index, carry):
            here = pl.ds(pl.multiple_of(index * 128, 128), 128)
            for first in range(0, features, third):
                cot = arena[cot_base : cot_base + all_rows, first : first + third]
                out = dot_tn(r.hidden[:, here], cot).astype(BF16)
                inners[number][here, first : first + third] = out
            return carry

        lax.fori_loop(0, size // 128, contract_tile, 0)

        def expand_tile(index, carry):
            here = pl.ds(pl.multiple_of(index * third, third), third)
            lhs = arena[x_base : x_base + all_rows, here]
            experts[number][here, :] = dot_tn(lhs, r.grad_gate_up[:, : 2 * size]).astype(BF16)
            return carry

        lax.fori_loop(0, 3, expand_tile, 0)

    chain_sums = []
    for number, (_, count, size) in enumerate(chunks):
        pair = []
        for place, land, stage in (
            (
                expand_place(number),
                (r.land_0, r.land_1, r.land_2)[number],
                r.stage.at[pl.ds(0, plane_rows), pl.ds(0, 2 * size)],
            ),
            (
                contract_place(number),
                (r.land_c0, r.land_c1, r.land_c2)[number],
                r.stage.at[pl.ds(0, count), pl.ds(0, features)],
            ),
        ):
            get = functools.partial(lambda ref, j: ref.at[j], land)
            pair.append(
                ChainSum(
                    wires,
                    n_dp,
                    place,
                    get,
                    "sums_%d" % number,
                    stage,
                    r.local_sems.at[5],
                    straight=number == len(chunks) - 1,
                )
            )
        chain_sums.append(pair)

    def level(number, *steps):
        for step in steps:
            for one in chain_sums[number]:
                one.level(step)

    inner_steps = range(1, n_dp // 2)

    def diagonal():
        tokens_gather.relay_last()
        cotangent_gather.wait_last()
        tokens_gather.wait_last()

    def near_x():
        for gather in (cotangent_gather, tokens_gather):
            gather.wait_core_x()

    def near_y():
        for gather in (cotangent_gather, tokens_gather):
            gather.wait_core_y()

    def near_y_and_hop():
        near_y()
        weights[1].hop(1)

    chunk(0, (0, 1, 2, 3), {2: near_x, 4: near_y_and_hop, 6: diagonal})
    weight_grads(0)
    level(0, 0)
    weights[1].hop(*range(2, hops))
    weights[2].hop(0)
    chunk(1, (0, 1, 2, 3), {6: lambda: weights[2].hop(1)})
    weight_grads(1)
    level(1, 0)
    weights[2].hop(*range(2, hops))
    wires.drain("pieces")
    branch_sum, back_sum = (
        PlaneSum(wires, arena, base, rows, r.cores.at[i], r.diag.at[i], r.sides.at[i], "plane")
        for i, base in enumerate((branch_base, back_base))
    )

    def add_core(one, k):
        stage = r.core_stage.at[0, pl.ds(0, rows)]
        one.fetch_core(k, stage, r.local_sems.at[6]).wait()
        one.add_core(k, stage)

    def send_core(k):
        back_sum.send_core(k)
        branch_sum.send_core(k)

    def after_diagonal():
        send_core(3)

    def after_x():
        send_core(1)
        add_core(back_sum, 3)
        back_sum.send_diag()

    def after_y():
        send_core(2)
        add_core(back_sum, 1)
        back_sum.send_x()

    chunk(2, (3, 1, 2, 0), {2: after_diagonal, 4: after_x, 6: after_y})
    send_core(0)
    add_core(back_sum, 2)
    back_sum.send_y()
    add_core(back_sum, 0)
    wires.drain("tokens", "cotangent")
    weight_grads(2)
    get_output = load(r.output_kept, arena.at[pl.ds(output_again, QD)], 2)
    get_cotangent = load(r.cotangent, r.branch_low, 3)
    level(2, 0)
    back_sum.send_second()
    level(0, *inner_steps)
    add_core(branch_sum, 3)
    branch_sum.send_diag()
    add_core(branch_sum, 1)
    branch_sum.send_x()
    add_core(branch_sum, 2)
    branch_sum.send_y()
    add_core(branch_sum, 0)
    grad_normed = back_sum.total()
    middle = r.middle[...]
    grad_middle, gain_two = norm_backward(
        middle, norm_scale(middle), r.gains_full[1:2, :], grad_normed
    )
    get_cotangent.wait()
    r.grad_middle[...] = grad_middle + r.branch_low[...].astype(F32)
    r.branch_low[...] = r.grad_middle[...].astype(BF16)
    output_sum, qkv_sum = (
        SlotSum(
            wires,
            n_dp,
            arena,
            base,
            size,
            cores,
            diag,
            sides,
            land,
            tag,
            r.core_stage.at[1, pl.ds(0, n_dp * size)],
            r.local_sems.at[7],
        )
        for base, size, cores, diag, sides, land, tag in (
            (0, share_out, r.output_cores, r.output_diag, r.output_sides, r.output_land, "output"),
            (n_all * share_out, folded, r.qkv_cores, r.qkv_diag, r.qkv_sides, r.qkv_land, "qkv"),
        )
    )
    gains_sum = SlotSum(
        wires, n_dp, r.gain_slots, 0, 8, r.gain_cores, r.gain_diag, r.gain_sides, r.gain_land, "gains"
    )
    for j in range(n_dp):
        first = 8 * share_out * j
        part = dot_tn(r.mixture[:, first : first + 8 * share_out], r.branch_low[...]).astype(BF16)
        for k in range(4):
            for e in range(2):
                slot = ((e * 4 + k) * n_dp + j) * share_out
                inner = (k * 2 + e) * share_out
                arena[slot : slot + share_out, :] = part[inner : inner + share_out, :]
    output_sum.send_core()
    get_output.wait()
    r.grad_mixture[...] = dot_nt(
        r.branch_low[...], arena[output_again : output_again + QD, :]
    ).astype(BF16)
    r.grad_window[...] = jnp.zeros_like(r.grad_window)

    def head_back(h, carry):
        mine = pl.ds(pl.multiple_of(h * HD, HD), HD)
        probs = jnp.exp(scores_of(h) - r.log_totals[h])
        grad_mixture = r.grad_mixture[:, mine]
        grad_probs = dot_nt(grad_mixture, r.window[:, HD : 2 * HD])
        row_dot = jnp.sum(probs * grad_probs, axis=-1, keepdims=True)
        grad_scores = (probs * (grad_probs - row_dot)).astype(BF16)
        grad_queries = dot_nn(grad_scores, r.window[:, 0:HD]) * scale
        r.grad_projected[:, mine] = grad_queries.astype(BF16)
        r.grad_window[:, 0:HD] += dot_tn(grad_scores, r.queries[:, mine]) * scale
        r.grad_window[:, HD : 2 * HD] += dot_tn(probs.astype(BF16), grad_mixture)
        return carry

    lax.fori_loop(0, HQ, head_back, 0)
    r.window_out[...] = r.grad_window[0:WINDOW, :].astype(BF16)
    later = []
    for distance in range(1, reach + 1):
        after, before = me + distance, me - distance
        index = kv_index + reach + distance - 1
        first = WINDOW - distance * rows
        wires.send(
            r.window_out.at[pl.ds(first, rows)],
            r.window_in.at[distance - 1],
            device_at(jnp.clip(before, 0, n_all - 1)),
            index,
            before >= 0,
            "window",
        )
        source = device_at(jnp.clip(after, 0, n_all - 1))
        later.append((r.window_in.at[distance - 1], source, index, after <= n_all - 1))
    output_sum.send_first()
    branch_sum.send_second()

    def qkv_grads(first, count):
        def tile(index, carry):
            here = pl.ds(pl.multiple_of(index * 128, 128), 128)
            there = slice(first, first + count)
            out = dot_tn(r.normed[:, here], r.grad_projected[:, there]).astype(BF16)
            r.qkv_full[here, there] = out
            return carry

        lax.fori_loop(0, features // 128, tile, 0)

    r.grad_normed[...] = dot_nt(r.grad_projected[:, 0:QD], r.qkv_full[:, 0:QD])
    qkv_grads(0, QD)
    for arrival in later:
        wires.wait(*arrival)

        @pl.when(arrival[3])
        def _(arrival=arrival):
            r.grad_window[WINDOW:, :] += arrival[0][...].astype(F32)

    r.grad_projected[:, QD:] = r.grad_window[WINDOW:, :].astype(BF16)
    grad_normed = r.grad_normed[...] + dot_nt(r.grad_projected[:, QD:], r.qkv_full[:, QD:])
    r.grad_normed[...] = grad_normed
    qkv_grads(QD, wide - QD)
    for d, j, k, e in blocks:
        slot = n_all * share_out + ((e * 4 + k) * n_dp + j) * folded
        fold(arena, slot, r.qkv_full, share * d, share)
    qkv_sum.send_core()
    inputs = r.tokens[...].astype(F32)
    grad_inputs, gain_one = norm_backward(
        inputs, norm_scale(inputs), r.gains_full[0:1, :], r.grad_normed[...]
    )
    r.grad_middle[...] = r.grad_middle[...] + grad_inputs
    put_input_grad = load(r.grad_middle, r.input_grad, 0)
    r.gain_slots[...] = jnp.zeros_like(r.gain_slots)
    for d, j, k, e in blocks:
        slot = ((e * 4 + k) * n_dp + j) * 8
        for row, gain in enumerate((gain_one, gain_two)):
            r.gain_slots[slot + row : slot + row + 1, 0:share] = gain[:, share * d : share * (d + 1)]
    gains_sum.send_core()
    output_sum.send_second()
    qkv_sum.send_first()
    gains_sum.send_first()
    level(1, *inner_steps)

    def give_back(number):
        for one in chain_sums[number]:
            one.collect()
        size = 2 * chunks[number][2]
        r.stage[0:plane_rows, 0:size] = expand_place(number)(q)[...]
        for group in range(8):
            r.pieces_out[group, :, columns(number)] = r.stage[
                share * group : share * (group + 1), 0:size
            ]
        back = exchange(number, "give_back")
        first, count, _ = chunks[number]
        used = min(first + count, ff_block) - first
        r.sum_contract[first : first + used, :] = contract_place(number)(q)[...][0:used, :]
        return back

    def take_back(chosen):
        backs[chosen].finish()
        for group, source, size, number, place in pieces:
            if number == chosen:
                at = starts[number] + place
                r.sum_expand[:, source : source + size] = r.pieces_in[group, :, at : at + size]

    qkv_sum.send_second()
    gains_sum.send_second()
    output_sum.add_sides()
    output_sum.chain.level(0)
    backs = [give_back(0)]
    r.block_out[...] = (r.middle[...] + branch_sum.total()).astype(BF16)
    for one in (qkv_sum, gains_sum):
        one.add_sides()
        one.chain.level(0)
    backs.append(give_back(1))
    take_back(0)
    output_sum.chain.collect()
    r.sum_output[...] = output_sum.chain.own(q)[...].astype(F32)
    backs.append(give_back(2))
    take_back(1)
    for one in (qkv_sum, gains_sum):
        one.chain.collect()
    r.own_qkv[...] = qkv_sum.chain.own(q)[...]
    unfold(r.sum_qkv, 0, share, r.own_qkv, 0)
    r.sum_gains[...] = gains_sum.chain.own(q)[...]
    take_back(2)
    put_input_grad.wait()
    wires.drain()


def run_block(n_dp, tokens, cotangent, qkv, output, gains, expand, contract):
    n_all = 8 * n_dp
    rows, features = tokens.shape
    share, wide = qkv.shape
    share_out = output.shape[0]
    ff_block = contract.shape[0]
    plane_rows = 8 * share
    folded = share + share // 3
    padded, width, chunks, pieces = hidden_layout(n_dp, ff_block)
    largest = max(size for _, _, size in chunks)
    hbm, vmem = pl.BlockSpec(memory_space=pl.ANY), pl.BlockSpec(memory_space=pltpu.VMEM)
    outs = {
        "block_out": ((rows, features), BF16),
        "input_grad": ((rows, features), F32),
        "sum_qkv": ((share, wide), F32),
        "sum_output": ((share_out, features), F32),
        "sum_gains": ((8, 128), F32),
        "sum_expand": (expand.shape, BF16),
        "sum_contract": ((ff_block, features), BF16),
    }
    lands = {
        "land_%d" % i: ((2 * n_dp + 1, plane_rows, 2 * size), BF16)
        for i, (_, _, size) in enumerate(chunks)
    }
    for i, (_, count, _) in enumerate(chunks):
        lands["land_c%d" % i] = ((2 * n_dp + 1, count, features), BF16)
    lands["cores"] = ((2, 4, rows, features), BF16)
    lands["output_kept"] = ((QD, features), BF16)
    lands["output_cores"] = ((4 * n_dp * share_out, features), BF16)
    lands["qkv_cores"] = ((4 * n_dp * folded, features), BF16)

    def sums(name, size, columns, dtype):
        return {
            name + "_diag": ((n_dp * size, columns), dtype),
            name + "_sides": ((2 * n_dp * size, columns), dtype),
            name + "_land": (((2 * n_dp + 1) * size, columns), dtype),
        }

    scratch = {
        "arena": ((32 * rows, features), BF16),
        **{"expand_%d" % i: ((features, 2 * size), BF16) for i, (_, _, size) in enumerate(chunks)},
        **{"contract_%d" % i: ((size, features), BF16) for i, (_, _, size) in enumerate(chunks)},
        "hidden": ((8 * rows, largest), BF16),
        "grad_gate_up": ((8 * rows, 2 * largest), BF16),
        "stage": ((plane_rows, max(features, 2 * largest)), BF16),
        "core_stage": ((2, max(rows, n_dp * folded), features), BF16),
        "diag": ((2, 2, rows // 2, features), BF16),
        "sides": ((2, 2, rows, features), BF16),
        "pieces_out": ((8, share, 2 * width), BF16),
        "pieces_in": ((8, share, 2 * width), BF16),
        "grad_middle": ((rows, features), F32),
        "grad_normed": ((rows, features), F32),
        "own_qkv": ((folded, features), BF16),
        "gain_slots": ((n_all * 8, 128), F32),
        "gains_full": ((8, features), F32),
        "qkv_full": ((features, wide), BF16),
        "normed": ((rows, features), BF16),
        "queries": ((rows, QD), BF16),
        "window": ((WINDOW + rows, 2 * HD), BF16),
        "log_totals": ((HQ, rows, 1), F32),
        "mixture": ((rows, QD), BF16),
        "middle": ((rows, features), F32),
        "branch_low": ((rows, features), BF16),
        "grad_mixture": ((rows, QD), BF16),
        "grad_window": ((WINDOW + rows, 2 * HD), F32),
        "window_out": ((WINDOW, 2 * HD), BF16),
        "window_in": ((WINDOW // rows, rows, 2 * HD), BF16),
        "grad_projected": ((rows, wide), BF16),
        **sums("output", share_out, features, BF16),
        **sums("qkv", folded, features, BF16),
        **sums("gain", 8, 128, F32),
        "gain_cores": ((4 * n_dp * 8, 128), F32),
    }
    names = (*INPUTS, *outs, *lands, *scratch, "local_sems", "send_sems", "recv_sems")
    results = pl.pallas_call(
        functools.partial(block_kernel, n_dp, names),
        out_shape=[jax.ShapeDtypeStruct(*s) for s in (*outs.values(), *lands.values())],
        in_specs=[vmem, hbm, vmem, vmem, vmem, hbm, hbm],
        out_specs=[hbm if name == "input_grad" else vmem for name in outs] + [hbm] * len(lands),
        scratch_shapes=[pltpu.VMEM(*s) for s in scratch.values()]
        + [
            pltpu.SemaphoreType.DMA((11,)),
            pltpu.SemaphoreType.DMA((WIRES,)),
            pltpu.SemaphoreType.DMA((WIRES,)),
        ],
        compiler_params=pltpu.CompilerParams(
            collective_id=0, has_side_effects=True, vmem_limit_bytes=VMEM_LIMIT
        ),
        name="transformer_block",
    )(tokens, cotangent, qkv, output, gains, expand, contract)
    return results[: len(outs)]


def adamw_update(weight, gradient, first, second, rate, decay_rate):
    mean_new = BETA_FIRST * first + (1.0 - BETA_FIRST) * gradient
    square_new = BETA_SECOND * second + (1.0 - BETA_SECOND) * gradient * gradient
    mean_hat = mean_new / (1.0 - BETA_FIRST**STEP)
    square_hat = square_new / (1.0 - BETA_SECOND**STEP)
    updated = weight - rate * (
        mean_hat / (jnp.sqrt(square_hat) + ADAM_EPSILON) + decay_rate * weight
    )
    return (updated, mean_new, square_new)


def shards_kernel(tokens, cotangent, *arguments):
    weights, firsts, seconds = arguments[:5], arguments[5:10], arguments[10:15]
    qkv, output, expand, contract, gains = weights
    share = gains.shape[1]
    gains_tile = jnp.pad(gains.astype(F32), ((0, 6), (0, 128 - share)))
    block_out, input_grad, *sums = run_block(
        lax.axis_size("ctx") // 2, tokens, cotangent, qkv, output, gains_tile, expand, contract
    )
    sum_qkv, sum_output, sum_gains, sum_expand, sum_contract = sums
    gradients = (sum_qkv, sum_output, sum_expand, sum_contract, sum_gains[:2, :share])
    rates = (RATE_MATRIX,) * 4 + (RATE_GAINS,)
    decays = (WEIGHT_DECAY,) * 4 + (0.0,)
    updates = [
        adamw_update(weight.astype(F32), gradient.astype(F32), first, second, rate, decay)
        for weight, gradient, first, second, rate, decay in zip(
            weights, gradients, firsts, seconds, rates, decays
        )
    ]
    return (
        block_out,
        input_grad,
        *(new for new, _, _ in updates),
        *(mean for _, mean, _ in updates),
        *(square for _, _, square in updates),
    )


def passed_along(block, axis, distance):
    devices = range(lax.axis_size(axis))
    route = [(i - distance, i) for i in devices if i - distance in devices]
    return lax.ppermute(block, axis, route)


def norm_forward(values, gain_row):
    scale = norm_scale(values)
    return (values * scale * gain_row, scale)


def shards_plain(
    tokens,
    cotangent,
    qkv_weight,
    output_weight,
    expand_weight,
    contract_weight,
    norm_gains,
    first_qkv,
    first_output,
    first_expand,
    first_contract,
    first_gains,
    second_qkv,
    second_output,
    second_expand,
    second_contract,
    second_gains,
):
    tok_dev = tokens.shape[0]
    n_fsdp = lax.axis_size("fsdp")
    n_ctx = lax.axis_size("ctx")
    ff_block = FF // (n_ctx * n_fsdp)
    score_scale = 1.0 / math.sqrt(HD)
    fsdp_index = lax.axis_index("fsdp")
    ctx_index = lax.axis_index("ctx")
    qkv_full, output_full, gains_full = (
        lax.all_gather(qkv_weight, ("ctx", "fsdp"), axis=0, tiled=True),
        lax.all_gather(output_weight, ("ctx", "fsdp"), axis=0, tiled=True),
        lax.all_gather(norm_gains, ("ctx", "fsdp"), axis=1, tiled=True),
    )
    arranged = expand_weight.reshape(expand_weight.shape[0], 2, n_ctx, n_fsdp, ff_block)
    arranged = lax.all_to_all(arranged, "fsdp", split_axis=3, concat_axis=0, tiled=True)
    arranged = arranged.reshape(arranged.shape[0], 2 * n_ctx * ff_block)
    expand_use, contract_use = (
        lax.all_gather(arranged, "ctx", axis=0, tiled=True),
        lax.all_gather(contract_weight, "ctx", axis=0, tiled=True),
    )
    width = n_ctx * ff_block
    gains_float = gains_full.astype(jnp.float32)
    inputs = tokens.astype(jnp.float32)
    normed, scale_one = norm_forward(inputs, gains_float[0])
    normed_low = normed.astype(jnp.bfloat16)
    projected = jnp.dot(normed_low, qkv_full, preferred_element_type=jnp.float32).astype(
        jnp.bfloat16
    )
    queries = projected[:, : HQ * HD].reshape(tok_dev, HQ, HD)
    key_value = projected[:, HQ * HD :]
    reach = (WINDOW + tok_dev - 1) // tok_dev
    earlier_pieces = []
    for distance in range(reach, 0, -1):
        earlier_pieces.append(passed_along(key_value, ("ctx", "fsdp"), distance))
    earlier = jnp.concatenate(earlier_pieces, axis=0)
    window_kv = jnp.concatenate([earlier, key_value], axis=0)
    key_rows = window_kv[:, :HD]
    value_rows = window_kv[:, HD:]
    offset = (ctx_index * n_fsdp + fsdp_index) * tok_dev
    row_index = lax.broadcasted_iota(jnp.int32, (tok_dev, WINDOW + tok_dev), 0)
    col_index = lax.broadcasted_iota(jnp.int32, (tok_dev, WINDOW + tok_dev), 1)
    visible = (
        (col_index > row_index) & (col_index <= row_index + WINDOW) & (col_index + offset >= WINDOW)
    )

    def masked_scores():
        raw_scores = (
            jnp.einsum("qhd,kd->hqk", queries, key_rows, preferred_element_type=jnp.float32)
            * score_scale
        )
        return jnp.where(visible[None], raw_scores, MASKED_SCORE)

    scores = masked_scores()
    log_total = jax.nn.logsumexp(scores, axis=-1, keepdims=True)
    probs_low = jnp.exp(scores - log_total).astype(jnp.bfloat16)
    mixture = jnp.einsum("hqk,kd->qhd", probs_low, value_rows, preferred_element_type=jnp.float32)
    mixture_low = mixture.reshape(tok_dev, HQ * HD).astype(jnp.bfloat16)
    middle = inputs + jnp.dot(mixture_low, output_full, preferred_element_type=jnp.float32)
    normed_two, scale_two = norm_forward(middle, gains_float[1])
    normed_two_low = normed_two.astype(jnp.bfloat16)
    ffn_input, ffn_cotangent = (
        lax.all_gather(normed_two_low, "fsdp", axis=0, tiled=True),
        lax.all_gather(cotangent, "fsdp", axis=0, tiled=True),
    )
    gate_up = jnp.dot(ffn_input, expand_use, preferred_element_type=jnp.float32)
    gate_part = gate_up[:, :width]
    up_part = gate_up[:, width:]
    activated, gelu_back = jax.vjp(functools.partial(jax.nn.gelu, approximate=True), gate_part)
    hidden_low = (activated * up_part).astype(jnp.bfloat16)
    branch_two = jnp.dot(hidden_low, contract_use, preferred_element_type=jnp.float32)
    branch_two = lax.psum_scatter(
        branch_two.astype(jnp.bfloat16), "fsdp", scatter_dimension=0, tiled=True
    ).astype(jnp.float32)
    result = middle + branch_two
    block_out = result.astype(jnp.bfloat16)
    grad_result = cotangent.astype(jnp.float32)
    grad_contract = jnp.einsum(
        "tf,td->fd", hidden_low, ffn_cotangent, preferred_element_type=jnp.float32
    )
    grad_hidden = jnp.einsum(
        "td,fd->tf", ffn_cotangent, contract_use, preferred_element_type=jnp.float32
    )
    (grad_gate,) = gelu_back(grad_hidden * up_part)
    grad_gate_up = jnp.concatenate([grad_gate, grad_hidden * activated], axis=1).astype(
        jnp.bfloat16
    )
    grad_expand = jnp.einsum(
        "td,tf->df", ffn_input, grad_gate_up, preferred_element_type=jnp.float32
    )
    grad_normed_two = jnp.einsum(
        "tf,df->td", grad_gate_up, expand_use, preferred_element_type=jnp.float32
    )
    grad_normed_two = lax.psum_scatter(grad_normed_two, "fsdp", scatter_dimension=0, tiled=True)
    part_expand, sum_contract = (
        lax.psum_scatter(
            grad_expand.astype(jnp.bfloat16), "ctx", scatter_dimension=0, tiled=True
        ).astype(jnp.float32),
        lax.psum_scatter(
            grad_contract.astype(jnp.bfloat16), "ctx", scatter_dimension=0, tiled=True
        ).astype(jnp.float32),
    )
    part_expand = part_expand.reshape(part_expand.shape[0], 2, n_ctx, 1, ff_block)
    sum_expand = lax.all_to_all(part_expand, "fsdp", split_axis=0, concat_axis=3, tiled=True)
    sum_expand = sum_expand.reshape(sum_expand.shape[0], 2 * FF)
    grad_norm_two, gain_grad_two = norm_backward(middle, scale_two, gains_float[1], grad_normed_two)
    grad_middle = grad_result + grad_norm_two
    grad_branch = grad_middle.astype(jnp.bfloat16)
    grad_output = jnp.einsum(
        "tc,td->cd", mixture_low, grad_branch, preferred_element_type=jnp.float32
    )
    grad_mixture = jnp.einsum(
        "td,cd->tc", grad_branch, output_full, preferred_element_type=jnp.float32
    )
    grad_mixture = grad_mixture.astype(jnp.bfloat16).reshape(tok_dev, HQ, HD)
    again_scores = masked_scores()
    again_probs = jnp.exp(again_scores - log_total)
    again_low = again_probs.astype(jnp.bfloat16)
    grad_probs = jnp.einsum(
        "qhd,kd->hqk", grad_mixture, value_rows, preferred_element_type=jnp.float32
    )
    row_dot = jnp.sum(again_probs * grad_probs, axis=-1, keepdims=True)
    grad_scores = (again_probs * (grad_probs - row_dot)).astype(jnp.bfloat16)
    grad_queries = (
        jnp.einsum("hqk,kd->qhd", grad_scores, key_rows, preferred_element_type=jnp.float32)
        * score_scale
    )
    grad_keys = (
        jnp.einsum("hqk,qhd->kd", grad_scores, queries, preferred_element_type=jnp.float32)
        * score_scale
    )
    grad_values = jnp.einsum(
        "hqk,qhd->kd", again_low, grad_mixture, preferred_element_type=jnp.float32
    )
    grad_window = jnp.concatenate([grad_keys, grad_values], axis=1)
    grad_key_value = grad_window[WINDOW:]
    grad_earlier = jnp.concatenate(
        [jnp.zeros((reach * tok_dev - WINDOW, 2 * HD), jnp.float32), grad_window[:WINDOW]], axis=0
    )
    for position in range(reach):
        piece = grad_earlier[position * tok_dev : (position + 1) * tok_dev]
        grad_key_value = grad_key_value + passed_along(
            piece.astype(jnp.bfloat16), ("ctx", "fsdp"), position - reach
        ).astype(piece.dtype)
    grad_projected = jnp.concatenate(
        [grad_queries.reshape(tok_dev, HQ * HD), grad_key_value], axis=1
    ).astype(jnp.bfloat16)
    grad_qkv = jnp.einsum(
        "td,tc->dc", normed_low, grad_projected, preferred_element_type=jnp.float32
    )
    grad_normed = jnp.einsum(
        "tc,dc->td", grad_projected, qkv_full, preferred_element_type=jnp.float32
    )
    grad_norm_one, gain_grad_one = norm_backward(inputs, scale_one, gains_float[0], grad_normed)
    input_grad = grad_middle + grad_norm_one
    grad_gains = jnp.concatenate([gain_grad_one, gain_grad_two], axis=0)
    sum_qkv, sum_output, sum_gains = (
        lax.psum_scatter(grad_qkv, ("ctx", "fsdp"), scatter_dimension=0, tiled=True),
        lax.psum_scatter(grad_output, ("ctx", "fsdp"), scatter_dimension=0, tiled=True),
        lax.psum_scatter(grad_gains, ("ctx", "fsdp"), scatter_dimension=1, tiled=True),
    )
    new_qkv, mean_qkv, square_qkv = adamw_update(
        qkv_weight.astype(jnp.float32), sum_qkv, first_qkv, second_qkv, RATE_MATRIX, WEIGHT_DECAY
    )
    new_output, mean_output, square_output = adamw_update(
        output_weight.astype(jnp.float32),
        sum_output,
        first_output,
        second_output,
        RATE_MATRIX,
        WEIGHT_DECAY,
    )
    new_expand, mean_expand, square_expand = adamw_update(
        expand_weight.astype(jnp.float32),
        sum_expand,
        first_expand,
        second_expand,
        RATE_MATRIX,
        WEIGHT_DECAY,
    )
    new_contract, mean_contract, square_contract = adamw_update(
        contract_weight.astype(jnp.float32),
        sum_contract,
        first_contract,
        second_contract,
        RATE_MATRIX,
        WEIGHT_DECAY,
    )
    new_gains, mean_gains, square_gains = adamw_update(
        norm_gains.astype(jnp.float32), sum_gains, first_gains, second_gains, RATE_GAINS, 0.0
    )
    return (
        block_out,
        input_grad,
        new_qkv,
        new_output,
        new_expand,
        new_contract,
        new_gains,
        mean_qkv,
        mean_output,
        mean_expand,
        mean_contract,
        mean_gains,
        square_qkv,
        square_output,
        square_expand,
        square_contract,
        square_gains,
    )


def shards(*arguments):
    plane_rows = 8 * arguments[4].shape[0]
    return (shards_kernel if plane_rows % 16 == 0 else shards_plain)(*arguments)


def solution(mesh):
    rows, columns = P(("ctx", "fsdp"), None), P(None, ("ctx", "fsdp"))
    in_specs = (rows,) * 6 + (columns,) + ((rows,) * 4 + (columns,)) * 2
    out_specs = (rows,) * 2 + ((rows,) * 4 + (columns,)) * 3
    return jax.shard_map(shards, mesh=mesh, in_specs=in_specs, out_specs=out_specs, check_vma=False)
```

```python
import functools
import math
import types

import jax
import jax.numpy as jnp
from jax import lax
from jax.experimental import pallas as pl
from jax.experimental.pallas import tpu as pltpu
from jax.sharding import PartitionSpec as P

HQ = 4
HD = 256
FF = 6912
WINDOW = 512
STEP = 10

NORM_EPSILON = 1e-06
BETA_FIRST = 0.9
BETA_SECOND = 0.999
RATE_MATRIX = 0.1
RATE_GAINS = 0.5
WEIGHT_DECAY = 0.1
ADAM_EPSILON = 1e-08
MASKED_SCORE = -1e30

F32 = jnp.float32
BF16 = jnp.bfloat16
MESH = pl.DeviceIdType.MESH
VMEM_LIMIT = 65400 * 1024
WIRES = 400
QD = HQ * HD


def position():
    ctx, fsdp = lax.axis_index("ctx"), lax.axis_index("fsdp")
    return ctx // 2, lax.rem(ctx, 2), fsdp // 2, lax.rem(fsdp, 2)


def device(q, y, x, c):
    return (q * 2 + y, x * 2 + c)


def device_at(index):
    return (index // 4, lax.rem(index, 4))


def rows_of(ref, first, count):
    if not isinstance(first, int):
        first = pl.multiple_of(first, 16 if ref.dtype == BF16 else 8)
    return ref.at[pl.ds(first, count)]


def gelu_parts(u):
    k = math.sqrt(2.0 / math.pi)
    square = u * u
    t = jnp.tanh(k * u * (1.0 + 0.044715 * square))
    half = 0.5 * (1.0 + t)
    slope = half + 0.5 * u * (1.0 - t * t) * (k * (1.0 + (3.0 * 0.044715) * square))
    return u * half, slope


def dot_nt(a, b):
    return lax.dot_general(a, b, (((1,), (1,)), ((), ())), preferred_element_type=F32)


def dot_tn(a, b):
    return lax.dot_general(a, b, (((0,), (0,)), ((), ())), preferred_element_type=F32)


def dot_nn(a, b):
    return jnp.dot(a, b, preferred_element_type=F32)


def norm_scale(values):
    return lax.rsqrt(jnp.mean(values * values, axis=-1, keepdims=True) + NORM_EPSILON)


def norm_backward(values, scale, gain_row, grad_normed):
    gain_grad = jnp.sum(grad_normed * values * scale, axis=0, keepdims=True)
    scaled = grad_normed * gain_row
    cubed = scale * scale * scale
    grad_values = scale * scaled - values * cubed * jnp.mean(
        scaled * values, axis=-1, keepdims=True
    )
    return grad_values, gain_grad


class Wires:
    def __init__(self, send_sems, recv_sems):
        self.send_sems, self.recv_sems = send_sems, recv_sems
        self.count = 0
        self.sent = {}
        self.tag = None

    def take(self, number=1):
        first = self.count
        self.count += number
        assert self.count <= WIRES, self.count
        return first

    def copy(self, src, dst, target, index, send_index=None):
        return pltpu.make_async_remote_copy(
            src_ref=src,
            dst_ref=dst,
            send_sem=self.send_sems.at[index if send_index is None else send_index],
            recv_sem=self.recv_sems.at[index],
            device_id=target,
            device_id_type=MESH,
        )

    def send(self, src, dst, target, index, when=None, tag=None, send_index=None):
        def make():
            here, there, other = (v() if callable(v) else v for v in (src, dst, target))
            return self.copy(here, there, other, index, send_index)

        self.run(lambda: make().start(), when)
        self.sent.setdefault(tag, []).append((lambda: make().wait_send(), when))

    def run(self, action, when):
        if when is None:
            action()
        else:
            pl.when(when() if callable(when) else when)(action)

    def wait(self, dst, target, index, when=None):
        copy = self.copy(dst, dst, target, index)
        if when is None:
            copy.wait_recv()
        else:
            pl.when(when)(copy.wait_recv)

    def drain(self, *tags):
        for tag in tags or list(self.sent):
            for action, when in self.sent.pop(tag, ()):
                self.run(action, when)


def greet(n_dp, reach):
    q, y, x, c = position()
    barrier = pltpu.get_barrier_semaphore()
    expected = 0

    def signal(target):
        pl.semaphore_signal(barrier, inc=1, device_id=target, device_id_type=MESH)

    for dy in range(2):
        for dx in range(2):
            for dc in range(2):
                if dy + dx + dc:
                    signal(device(q, (y + dy) % 2, (x + dx) % 2, (c + dc) % 2))
                    expected += 1
    me = (q * 2 + y) * 4 + x * 2 + c
    last = 8 * n_dp - 1
    for distance in range(1, reach + 1):
        for other in (me - distance, me + distance):
            here = (other >= 0) & (other <= last)
            pl.when(here)(functools.partial(signal, device_at(jnp.clip(other, 0, last))))
            expected = expected + here.astype(jnp.int32)
    for step in range(1, n_dp):
        signal(device(lax.rem(q + step, n_dp), y, x, c))
        expected = expected + 1
    pl.semaphore_wait(barrier, expected)


class Plane:
    def __init__(self):
        self.q, self.y, self.x, self.c = q, y, x, c = position()
        self.chips = [y * 2 + x, y * 2 + 1 - x, (1 - y) * 2 + x, (1 - y) * 2 + 1 - x]
        self.chip, self.chip_x, self.chip_y, self.chip_d = self.chips
        self.to_x, self.to_y = device(q, y, 1 - x, c), device(q, 1 - y, x, c)
        self.to_c = device(q, y, x, 1 - c)


class Chain:
    def __init__(self, wires, n_dp, own, place, tag):
        self.wires, self.n_dp, self.own, self.place, self.tag = wires, n_dp, own, place, tag
        self.first = {way: wires.take(n_dp - 1) for way in (1, -1)}

    def valid(self, way, step):
        q = position()[0]
        return (q - 1 - step >= 0) if way == 1 else (q + 1 + step <= self.n_dp - 1)

    def send(self, way, step):
        last = self.n_dp - 1

        def block():
            return jnp.clip(position()[0] - way * step, 0, last)

        def place():
            return self.place(block())

        def target():
            q, y, x, c = position()
            return device(jnp.clip(q + way, 0, last), y, x, c)

        def here():
            q = position()[0]
            origin = q - way * step
            return (origin >= 0) & (origin <= last) & (q + way >= 0) & (q + way <= last)

        src = self.own if step == 0 else place
        self.wires.send(src, place, target, self.first[way] + step, here, self.tag)

    def wait(self, way, step):
        q, y, x, c = position()
        block = jnp.clip(q - way * (step + 1), 0, self.n_dp - 1)
        self.wires.wait(
            self.place(block),
            device(jnp.clip(q + way, 0, self.n_dp - 1), y, x, c),
            self.first[way] + step,
            self.valid(way, step),
        )
        if step + 1 < self.n_dp - 1:
            self.send(way, step + 1)

    def start(self):
        self.send(1, 0)
        self.send(-1, 0)

    def hop(self, step):
        self.wait(1, step)
        self.wait(-1, step)


class PlaneGather(Plane):
    def __init__(self, wires, own, buf, base, rows, tag):
        super().__init__()
        self.wires, self.own, self.buf, self.base, self.rows = wires, own, buf, base, rows
        self.half = rows // 2
        self.tag = tag
        (self.xa, self.xb, self.ya, self.yb, self.co, self.da, self.db) = (
            wires.take() for _ in range(7)
        )
        self.cx, self.cy, self.cd = (wires.take() for _ in range(3))

    def part(self, chip, c, which=None):
        first = self.base + (chip * 2 + c) * self.rows
        if which is None:
            return rows_of(self.buf, first, self.rows)
        return rows_of(self.buf, first + which * self.half, self.half)

    def send(self, src, dst, target, index):
        self.wires.send(src, dst, target, index, None, self.tag)

    def start(self):
        c, half = self.c, self.half
        low, high = self.own.at[pl.ds(0, half)], self.own.at[pl.ds(half, half)]
        self.send(low, self.part(self.chip, c, 0), self.to_x, self.xa)
        self.send(high, self.part(self.chip, c, 1), self.to_y, self.yb)
        self.send(high, self.part(self.chip, c, 1), self.to_x, self.xb)
        self.send(low, self.part(self.chip, c, 0), self.to_y, self.ya)
        self.send(self.own, self.part(self.chip, c), self.to_c, self.co)

    def forward(self, target, index, chip, which=None):
        def part():
            return self.part(chip, self.c, which)

        self.send(part, part, target, index)

    def relay(self):
        c, wires = self.c, self.wires
        wires.wait(self.part(self.chip_x, c, 0), self.to_x, self.xa)
        self.forward(self.to_y, self.da, self.chip_x, 0)
        wires.wait(self.part(self.chip_y, c, 1), self.to_y, self.yb)
        self.forward(self.to_x, self.db, self.chip_y, 1)

    def relay_core(self):
        c, wires = self.c, self.wires
        wires.wait(self.part(self.chip_x, c, 1), self.to_x, self.xb)
        self.forward(self.to_c, self.cx, self.chip_x)
        wires.wait(self.part(self.chip_y, c, 0), self.to_y, self.ya)
        self.forward(self.to_c, self.cy, self.chip_y)

    def relay_last(self):
        c, wires = self.c, self.wires
        wires.wait(self.part(self.chip_d, c, 0), self.to_y, self.da)
        wires.wait(self.part(self.chip_d, c, 1), self.to_x, self.db)
        self.forward(self.to_c, self.cd, self.chip_d)

    def wait_core(self):
        self.wires.wait(self.part(self.chip, 1 - self.c), self.to_c, self.co)

    def wait_core_x(self):
        self.wires.wait(self.part(self.chip_x, 1 - self.c), self.to_c, self.cx)

    def wait_core_y(self):
        self.wires.wait(self.part(self.chip_y, 1 - self.c), self.to_c, self.cy)

    def wait_last(self):
        self.wires.wait(self.part(self.chip_d, 1 - self.c), self.to_c, self.cd)


class SlotGather(Plane):
    def __init__(self, wires, n_dp, own, buf, base, rows, tag):
        super().__init__()
        self.wires, self.n_dp, self.own, self.tag = wires, n_dp, own, tag
        self.buf, self.base, self.rows = buf, base, rows
        self.order = [(0, -1)] + [(way, s) for s in range(n_dp - 1) for way in (1, -1)]
        self.chain = Chain(wires, n_dp, own, lambda j: self.slot(self.c, j, self.chip), tag)
        self.kx, self.ky, self.kd, self.kc = (wires.take(len(self.order)) for _ in range(4))

    def slot(self, c, j, chip, count=1):
        return rows_of(
            self.buf, self.base + ((c * self.n_dp + j) * 4 + chip) * self.rows, count * self.rows
        )

    def each(self, ranks):
        for rank, (way, step) in enumerate(self.order):
            if ranks is not None and rank not in ranks:
                continue
            if way == 0:
                yield rank, way, step, self.q, None
            else:
                block = jnp.clip(self.q - way * (step + 1), 0, self.n_dp - 1)
                yield rank, way, step, block, self.chain.valid(way, step)

    def start(self):
        self.chain.start()

    def spread(self, ranks=None):
        for rank, way, step, j, ok in self.each(ranks):
            if way:
                self.chain.wait(way, step)
            src = self.slot(self.c, j, self.chip) if way else self.own
            dst = self.slot(self.c, j, self.chip)
            self.wires.send(src, dst, self.to_x, self.kx + rank, ok, self.tag)
            self.wires.send(src, dst, self.to_y, self.ky + rank, ok, self.tag)

    def relay(self, ranks=None):
        for rank, way, step, j, ok in self.each(ranks):
            even = lax.rem(j, 2) == 0
            odd = jnp.logical_not(even)
            sx, sy = self.slot(self.c, j, self.chip_x), self.slot(self.c, j, self.chip_y)
            self.wires.wait(sx, self.to_x, self.kx + rank, ok)
            to_y = even if ok is None else ok & even
            self.wires.send(sx, sx, self.to_y, self.kd + rank, to_y, self.tag)
            self.wires.wait(sy, self.to_y, self.ky + rank, ok)
            to_x = odd if ok is None else ok & odd
            self.wires.send(sy, sy, self.to_x, self.kd + rank, to_x, self.tag)

    def core(self, ranks=None):
        for rank, way, step, j, ok in self.each(ranks):
            self.wires.wait(self.slot(self.c, j, self.chip_d), self.to_x, self.kd + rank, ok)
            four = self.slot(self.c, j, 0, 4)
            self.wires.send(four, four, self.to_c, self.kc + rank, ok, self.tag)

    def finish(self, ranks=None):
        for rank, way, step, j, ok in self.each(ranks):
            four = self.slot(1 - self.c, j, 0, 4)
            self.wires.wait(four, self.to_c, self.kc + rank, ok)


def add_into(mine, other):
    mine[...] = (mine[...].astype(F32) + other[...].astype(F32)).astype(mine.dtype)


class ChainSum:
    def __init__(self, wires, n_dp, own, land, tag, stages=None, sems=None, straight=False):
        self.wires, self.n_dp, self.own, self.land, self.tag = wires, n_dp, own, land, tag
        self.stages, self.sems, self.straight = stages, sems, straight
        self.half = n_dp // 2
        self.direct, self.far, self.partial = wires.take(n_dp), wires.take(), wires.take(n_dp)

    def fetch(self, slot, index):
        return pltpu.make_async_copy(slot, self.stages[index], self.sems[index])

    def begin(self, slot, index, when):
        if self.stages is not None:
            self.wires.run(lambda: self.fetch(slot, index).start(), when)

    def finish(self, own, slot, index, when):
        def add():
            if self.stages is None:
                add_into(own, slot)
            else:
                self.fetch(slot, index).wait()
                add_into(own, self.stages[index])

        self.wires.run(add, when)

    def passing(self, number):
        q = position()[0]
        low = q < self.half
        here = jnp.where(low, q, self.n_dp - 1 - q) == number
        for j in [*range(self.n_dp - 1, self.half - 1, -1), *range(self.half)]:
            active = here & (low if j >= self.half else jnp.logical_not(low))
            yield j, j % self.half, self.land(self.n_dp + 1 + j), active

    def arrive(self, number):
        q, y, x, c = position()
        outward = jnp.clip(jnp.where(q < self.half, q - 1, q + 1), 0, self.n_dp - 1)
        for j, index, slot, active in self.passing(number):
            self.wires.wait(slot, device(outward, y, x, c), self.partial + j, active)
            self.begin(slot, index, active)

    def level(self, number):
        q, y, x, c = position()
        inward = jnp.where(q < self.half, q + 1, q - 1)
        for j, index, slot, active in self.passing(number):
            own = self.own(j)
            if number:
                self.finish(own, slot, index, active)
            if number < self.half - 1:
                dst, target, receive = slot, device(inward, y, x, c), self.partial + j
            else:
                dst, target, receive = self.land(self.n_dp), device(j, y, x, c), self.far
            self.wires.send(own, dst, target, receive, active, self.tag, self.partial + j)

    def near(self, j):
        q = position()[0]
        low = q < self.half
        if self.straight:
            return j != q
        return (j != q) & (low if j < self.half else jnp.logical_not(low))

    def send_near(self):
        q, y, x, c = position()
        for j in range(self.n_dp):
            self.wires.send(
                self.own(j),
                self.land(q),
                device(j, y, x, c),
                self.direct + q,
                self.near(j),
                self.tag,
                self.direct + j,
            )

    def arrivals(self):
        q, y, x, c = position()
        for j in range(self.n_dp):
            yield self.land(j), device(j, y, x, c), self.direct + j, j % self.half, self.near(j)
        if not self.straight:
            center = jnp.where(q < self.half, self.half, self.half - 1)
            yield self.land(self.n_dp), device(center, y, x, c), self.far, self.half, None

    def receive(self):
        for slot, source, number, index, when in self.arrivals():
            self.wires.wait(slot, source, number, when)
            self.begin(slot, index, when)

    def collect(self):
        for slot, source, number, index, when in self.arrivals():
            self.finish(self.own(position()[0]), slot, index, when)


class PlaneSum(Plane):
    def __init__(self, wires, buf, base, rows, cores, diag, sides, tag):
        super().__init__()
        self.wires, self.buf, self.base, self.rows, self.tag = wires, buf, base, rows, tag
        self.half = rows // 2
        self.cores, self.diag, self.sides = cores, diag, sides
        self.kc = wires.take(4)
        self.kdx, self.kdy = wires.take(), wires.take()
        self.kxa, self.kxb, self.kya, self.kyb = (wires.take() for _ in range(4))

    part = PlaneGather.part
    send = PlaneGather.send

    def send_core(self, k):
        def part():
            return self.part(self.chips[k], 1 - self.c)

        self.send(part, lambda: self.cores.at[k], self.to_c, self.kc + k)

    def fetch_core(self, k, stage, sem):
        self.wires.wait(self.cores.at[k], self.to_c, self.kc + k)
        copy = pltpu.make_async_copy(self.cores.at[k], stage, sem)
        copy.start()
        return copy

    def add_core(self, k, stage):
        add_into(self.part(self.chips[k], self.c), stage)

    def side(self, which, half):
        return self.sides.at[which, pl.ds(half * self.half, self.half)]

    def send_half(self, chip, half, dst, target, index):
        def part():
            return self.part(chip, self.c, half)

        self.send(part, dst, target, index)

    def send_diag(self):
        self.send_half(self.chip_d, 0, lambda: self.diag.at[0], self.to_x, self.kdx)
        self.send_half(self.chip_d, 1, lambda: self.diag.at[1], self.to_y, self.kdy)

    def send_x(self):
        self.send_half(self.chip_x, 0, lambda: self.side(0, 0), self.to_x, self.kxa)

    def send_y(self):
        self.send_half(self.chip_y, 1, lambda: self.side(1, 1), self.to_y, self.kyb)

    def send_second(self):
        self.wires.wait(self.diag.at[0], self.to_x, self.kdx)
        mine = self.part(self.chip_y, self.c, 0)
        add_into(mine, self.diag.at[0])
        self.send(mine, self.side(1, 0), self.to_y, self.kya)
        self.wires.wait(self.diag.at[1], self.to_y, self.kdy)
        mine = self.part(self.chip_x, self.c, 1)
        add_into(mine, self.diag.at[1])
        self.send(mine, self.side(0, 1), self.to_x, self.kxb)

    def total(self):
        self.wires.wait(self.side(0, 0), self.to_x, self.kxa)
        self.wires.wait(self.side(1, 1), self.to_y, self.kyb)
        self.wires.wait(self.side(1, 0), self.to_y, self.kya)
        self.wires.wait(self.side(0, 1), self.to_x, self.kxb)
        mine = self.part(self.chip, self.c)
        return mine[...].astype(F32) + self.sides[0].astype(F32) + self.sides[1].astype(F32)


class SlotSum(Plane):
    def __init__(
        self, wires, n_dp, buf, base, rows, cores, diag, sides, landing, tag, stages=None, sems=None
    ):
        super().__init__()
        self.wires, self.n_dp, self.tag = wires, n_dp, tag
        self.buf, self.base, self.rows = buf, base, rows
        self.cores, self.diag, self.sides = cores, diag, sides
        self.stages, self.sems = stages, sems
        self.low = n_dp // 2
        self.high = n_dp - self.low
        self.kc = wires.take(4)
        self.kdx, self.kdy, self.kx0, self.kx1, self.ky0, self.ky1 = (
            wires.take() for _ in range(6)
        )
        self.chain = ChainSum(
            wires,
            n_dp,
            lambda j: self.at(self.c, self.chip, j, 1),
            lambda j: rows_of(landing, j * rows, rows),
            tag,
            straight=True,
        )

    def at(self, c, chip, j, count):
        first = self.base + ((c * 4 + chip) * self.n_dp + j) * self.rows
        return rows_of(self.buf, first, count * self.rows)

    def four(self, ref, k):
        return ref.at[pl.ds(k * self.n_dp * self.rows, self.n_dp * self.rows)]

    def lows(self, ref, which=0):
        return ref.at[pl.ds(which * self.n_dp * self.rows, self.low * self.rows)]

    def highs(self, ref, which=0):
        first = (which * self.n_dp + self.low) * self.rows
        return ref.at[pl.ds(first, self.high * self.rows)]

    def send(self, src, dst, target, index):
        self.wires.send(src, dst, target, index, None, self.tag)

    def send_core(self):
        for k in (3, 2, 1, 0):
            src = self.at(1 - self.c, self.chips[k], 0, self.n_dp)
            self.send(src, self.four(self.cores, k), self.to_c, self.kc + k)

    def core_copy(self, k):
        return pltpu.make_async_copy(
            self.four(self.cores, k), self.stages[k % 2], self.sems[k % 2]
        )

    def wait_core(self, k):
        self.wires.wait(self.four(self.cores, k), self.to_c, self.kc + k)
        if self.stages is not None:
            self.core_copy(k).start()

    def add_core(self, k):
        other = self.four(self.cores, k)
        if self.stages is not None:
            self.core_copy(k).wait()
            other = self.stages[k % 2]
        add_into(self.at(self.c, self.chips[k], 0, self.n_dp), other)

    def send_first(self):
        low, c = self.low, self.c
        self.wait_core(3)
        self.wait_core(2)
        self.add_core(3)
        self.wait_core(1)
        self.send(self.at(c, self.chip_d, 0, low), self.lows(self.diag), self.to_x, self.kdx)
        self.send(self.at(c, self.chip_d, low, self.high), self.highs(self.diag), self.to_y, self.kdy)
        self.add_core(2)
        self.wait_core(0)
        self.send(self.at(c, self.chip_y, low, self.high), self.highs(self.sides, 1), self.to_y, self.ky1)
        self.add_core(1)
        self.send(self.at(c, self.chip_x, 0, low), self.lows(self.sides), self.to_x, self.kx0)
        self.add_core(0)

    def send_second(self):
        low, c, wires = self.low, self.c, self.wires
        wires.wait(self.lows(self.diag), self.to_x, self.kdx)
        mine = self.at(c, self.chip_y, 0, low)
        add_into(mine, self.lows(self.diag))
        self.send(mine, self.lows(self.sides, 1), self.to_y, self.ky0)
        wires.wait(self.highs(self.diag), self.to_y, self.kdy)
        mine = self.at(c, self.chip_x, low, self.high)
        add_into(mine, self.highs(self.diag))
        self.send(mine, self.highs(self.sides), self.to_x, self.kx1)

    def add_sides(self):
        wires = self.wires
        wires.wait(self.lows(self.sides), self.to_x, self.kx0)
        wires.wait(self.highs(self.sides, 1), self.to_y, self.ky1)
        wires.wait(self.lows(self.sides, 1), self.to_y, self.ky0)
        wires.wait(self.highs(self.sides), self.to_x, self.kx1)
        mine = self.at(self.c, self.chip, 0, self.n_dp)
        mine[...] = (
            mine[...].astype(F32)
            + self.four(self.sides, 0)[...].astype(F32)
            + self.four(self.sides, 1)[...].astype(F32)
        ).astype(mine.dtype)


class Exchange(Plane):
    def __init__(self, wires, pieces_out, pieces_in, local_sem, tag):
        super().__init__()
        self.wires, self.out, self.into, self.tag = wires, pieces_out, pieces_in, tag
        self.index = wires.take(7)
        self.me = self.chip * 2 + self.c
        self.copy = pltpu.make_async_copy(
            pieces_out.at[self.me], pieces_in.at[self.me], local_sem
        )

    def others(self):
        number = 0
        for dc in (0, 1):
            for dy, dx in ((1, 1), (0, 1), (1, 0), (0, 0)):
                if dy + dx + dc == 0:
                    continue
                ty, tx, tc = (self.y + dy) % 2, (self.x + dx) % 2, (self.c + dc) % 2
                yield (ty * 2 + tx) * 2 + tc, device(self.q, ty, tx, tc), self.index + number
                number += 1

    def start(self):
        for other, target, index in self.others():
            self.wires.send(
                self.out.at[other], self.into.at[self.me], target, index, None, self.tag
            )
        self.copy.start()

    def finish(self):
        for other, target, index in self.others():
            self.wires.wait(self.into.at[other], target, index)
        self.copy.wait()


def hidden_layout(n_dp, ff_block):
    unit = max(16, 128 // n_dp)
    units = -(-ff_block // unit)
    cuts = [0, -(-units * 3 // 7), -(-units * 5 // 7), units]
    chunks = [(unit * a, unit * (b - a), n_dp * unit * (b - a)) for a, b in zip(cuts, cuts[1:])]
    pieces = []
    for group in range(8):
        for part in range(2):
            for q in range(n_dp):
                source = part * FF + ff_block * (q * 8 + group)
                for number, (first, count, size) in enumerate(chunks):
                    used = min(first + count, ff_block) - first
                    place = part * size + q * count
                    pieces.append((group, source + first, used, number, place))
    return unit * units, n_dp * unit * units, chunks, pieces


INPUTS = ("tokens", "cotangent", "qkv", "output", "gains", "expand", "contract")
OUTPUTS = (
    "block_out",
    "input_grad",
    "sum_qkv",
    "sum_output",
    "sum_gains",
    "sum_expand",
    "sum_contract",
)


def fold(dst, first, src, row, share):
    wide, features = src.shape[1], dst.shape[1]
    third = share // 3
    extra = wide - features
    dst[first : first + share, :] = src[row : row + share, :features]
    for k in range(3):
        dst[first + share : first + share + third, k * extra : (k + 1) * extra] = src[
            row + third * k : row + third * (k + 1), features:
        ]


def unfold(dst, row, share, src, first):
    wide, features = dst.shape[1], src.shape[1]
    third = share // 3
    extra = wide - features
    dst[row : row + share, :features] = src[first : first + share, :].astype(dst.dtype)
    for k in range(3):
        dst[row + third * k : row + third * (k + 1), features:] = src[
            first + share : first + share + third, k * extra : (k + 1) * extra
        ].astype(dst.dtype)


def block_kernel(n_dp, names, *refs):
    r = types.SimpleNamespace(**dict(zip(names, refs, strict=True)))
    wires = Wires(r.send_sems, r.recv_sems)
    plane = Plane()
    q, y, x, c, chip = plane.q, plane.y, plane.x, plane.c, plane.chip
    me = (q * 4 + chip) * 2 + c
    n_all = 8 * n_dp
    hops = n_dp - 1
    rows, features = r.tokens.shape
    share, wide = r.qkv.shape
    share_out = r.output.shape[0]
    ff_block = r.contract.shape[0]
    plane_rows = 8 * share
    folded = share + share // 3
    padded, width, chunks, pieces = hidden_layout(n_dp, ff_block)
    experts = [r.expand_0, r.expand_1, r.expand_2]
    inners = [r.contract_0, r.contract_1, r.contract_2]
    all_rows = 8 * rows
    x_base, cot_base, branch_base, back_base = (all_rows * i for i in range(4))
    qkv_base, output_base = branch_base, branch_base + n_all * folded
    output_full, output_again = output_base + n_all * share_out, n_all * (share_out + folded)
    reach = WINDOW // rows
    scale = 1.0 / math.sqrt(HD)
    arena = r.arena
    blocks = [((j * 4 + k) * 2 + e, j, k, e) for j in range(n_dp) for k in range(4) for e in range(2)]

    def load(src, dst, number):
        copy = pltpu.make_async_copy(src, dst, r.local_sems.at[number])
        copy.start()
        return copy

    get_expand = load(r.expand, r.sum_expand, 0)
    get_contract = load(r.contract, r.sum_contract, 5)
    starts = [2 * sum(size for _, _, size in chunks[:number]) for number in range(len(chunks))]
    fold(r.own_qkv, 0, r.qkv, 0, share)
    r.pieces_out[...] = jnp.zeros_like(r.pieces_out)
    get_expand.wait()
    for group, source, size, number, place in pieces:
        at = starts[number] + place
        r.pieces_out[group, :, at : at + size] = r.sum_expand[:, source : source + size]
    get_contract.wait()

    def contract_place(number):
        count = chunks[number][1]
        return lambda j: rows_of(inners[number], j * count, count)

    def expand_place(number):
        return lambda j: rows_of(experts[number], j * plane_rows, plane_rows)

    for number, (first, count, _) in enumerate(chunks):
        used = min(first + count, ff_block) - first
        r.stage[0:used, 0:features] = r.sum_contract[first : first + used, :]
        if used < count:
            r.stage[used:count, 0:features] = jnp.zeros((count - used, features), BF16)
        contract_place(number)(q)[...] = r.stage[0:count, 0:features]
    greet(n_dp, reach)
    gains_gather = SlotGather(wires, n_dp, r.gains, r.gain_slots, 0, 8, "weights")
    qkv_gather = SlotGather(wires, n_dp, r.own_qkv, arena, qkv_base, folded, "weights")
    output_gather = SlotGather(wires, n_dp, r.output, arena, output_base, share_out, "weights")
    gathers = (gains_gather, qkv_gather, output_gather)
    firsts = (gains_gather, qkv_gather)
    ranks = len(gains_gather.order)
    for gather in firsts:
        gather.start()
        gather.spread((0,))

    def columns(number):
        return pl.ds(starts[number], 2 * chunks[number][2])

    def exchange(number, tag):
        out, into = (ref.at[:, :, columns(number)] for ref in (r.pieces_out, r.pieces_in))
        moved = Exchange(wires, out, into, r.local_sems.at[8 + number], tag)
        moved.start()
        return moved

    exchanges = [exchange(0, "pieces")]
    output_gather.start()
    own_slots = [load(g.own, g.slot(c, q, chip), 1 + i) for i, g in enumerate(gathers)]
    for gather in firsts:
        gather.spread((1, 2))
    for gather in firsts:
        gather.relay((0,))
    output_gather.spread((0,))
    for gather in firsts:
        gather.spread(range(3, ranks))

    class Chunk:
        def __init__(self, number):
            size = 2 * chunks[number][2]
            exchanges[number].finish()
            for group in range(8):
                r.stage[share * group : share * (group + 1), 0:size] = r.pieces_in[
                    group, :, starts[number] : starts[number] + size
                ]
            self.tag = "chunk_%d" % number
            self.chains = []
            for place in (expand_place(number), contract_place(number)):
                self.chains.append(Chain(wires, n_dp, place(q), place, self.tag))
            expand_place(number)(q)[...] = r.stage[0:plane_rows, 0:size]

        def start(self):
            for chain in self.chains:
                chain.start()

        def hop(self, *steps):
            for step in steps:
                for chain in self.chains:
                    chain.hop(step)

    weights = [Chunk(0)]
    weights[0].start()
    for copy in own_slots:
        copy.wait()
    for gather in firsts:
        gather.relay(range(1, ranks))
    output_gather.spread(range(1, ranks))
    exchanges.append(exchange(1, "pieces"))
    for gather in firsts:
        gather.core()
    for gather in firsts:
        gather.finish()
    for d, j, k, e in blocks:
        slot = (e * n_dp + j) * 4 + k
        unfold(r.qkv_full, share * d, share, arena, qkv_base + slot * folded)
        r.gains_full[0:2, share * d : share * (d + 1)] = r.gain_slots[
            8 * slot : 8 * slot + 2, 0:share
        ]
    inputs = r.tokens[...].astype(F32)
    r.normed[...] = (inputs * norm_scale(inputs) * r.gains_full[0:1, :]).astype(BF16)
    for first in (QD, *range(0, QD, 512)):
        part = dot_nn(r.normed[...], r.qkv_full[:, first : first + 512]).astype(BF16)
        if first < QD:
            r.queries[:, first : first + 512] = part
            continue
        r.window[WINDOW : WINDOW + rows, :] = part
        mine = r.window.at[pl.ds(WINDOW, rows)]
        kv_index = wires.take(2 * reach)
        earlier = []
        for distance in range(1, reach + 1):
            place = r.window.at[pl.ds(WINDOW - distance * rows, rows)]
            after, before = me + distance, me - distance
            index = kv_index + distance - 1
            target = device_at(jnp.clip(after, 0, n_all - 1))
            wires.send(mine, place, target, index, after <= n_all - 1, "window")

            @pl.when(before < 0)
            def _(place=place):
                place[...] = jnp.zeros_like(place)

            earlier.append((place, device_at(jnp.clip(before, 0, n_all - 1)), index, before >= 0))
    output_gather.relay()
    cotangent_gather = PlaneGather(wires, r.cotangent, arena, cot_base, rows, "cotangent")
    cotangent_gather.start()
    own_cotangent = load(r.cotangent, cotangent_gather.part(chip, c), 1)
    exchanges.append(exchange(2, "pieces"))
    output_gather.core()
    weights[0].hop(0)
    weights.append(Chunk(1))
    weights[1].start()
    output_gather.finish()
    for d, j, k, e in blocks:
        first = output_base + ((e * n_dp + j) * 4 + k) * share_out
        there = output_full + share_out * d
        arena[there : there + share_out, :] = arena[first : first + share_out, :]
    put_output = load(arena.at[pl.ds(output_full, QD)], r.output_kept, 2)
    for arrival in earlier:
        wires.wait(*arrival)
    keys = WINDOW + rows

    def visible():
        row = lax.broadcasted_iota(jnp.int32, (rows, keys), 0)
        col = lax.broadcasted_iota(jnp.int32, (rows, keys), 1)
        return (col > row) & (col <= row + WINDOW) & (col + me * rows >= WINDOW)

    def scores_of(h):
        mine = pl.ds(pl.multiple_of(h * HD, HD), HD)
        raw = dot_nt(r.queries[:, mine], r.window[:, 0:HD]) * scale
        return jnp.where(visible(), raw, MASKED_SCORE)

    def head(h, carry):
        scores = scores_of(h)
        top = jnp.max(scores, axis=-1, keepdims=True)
        log_total = top + jnp.log(jnp.sum(jnp.exp(scores - top), axis=-1, keepdims=True))
        r.log_totals[h] = log_total
        low = jnp.exp(scores - log_total).astype(BF16)
        mine = pl.ds(pl.multiple_of(h * HD, HD), HD)
        r.mixture[:, mine] = dot_nn(low, r.window[:, HD : 2 * HD]).astype(BF16)
        return carry

    lax.fori_loop(0, HQ, head, 0)
    cotangent_gather.relay()
    middle = r.tokens[...].astype(F32) + dot_nn(
        r.mixture[...], arena[output_full : output_full + QD, :]
    )
    r.middle[...] = middle
    tokens_gather = PlaneGather(wires, None, arena, x_base, rows, "tokens")
    own = tokens_gather.part(chip, c)
    tokens_gather.own = own
    own[...] = (middle * norm_scale(middle) * r.gains_full[1:2, :]).astype(BF16)
    tokens_gather.start()
    wires.drain("weights")
    own_cotangent.wait()
    put_output.wait()
    weights[0].hop(1)
    weights.append(Chunk(2))
    cotangent_gather.relay_core()
    tokens_gather.relay()
    weights[1].hop(0)
    weights[2].start()
    cotangent_gather.relay_last()
    tokens_gather.relay_core()
    for gather in (cotangent_gather, tokens_gather):
        gather.wait_core()
    for step in range(2, hops):
        weights[0].hop(step)
    chips = plane.chips

    def chunk(number, order, events):
        expand, inner = experts[number], inners[number]
        size = chunks[number][2]

        def tile(index, carry):
            for when, event in events.items():
                pl.when(index == when)(event)
            pair = index // 2
            place = chips[order[3]]
            for k in range(3):
                place = jnp.where(pair == k, chips[order[k]], place)
            offset = (place * 2 + lax.rem(index, 2)) * rows
            here = pl.ds(pl.multiple_of(offset, rows), rows)

            def at(base):
                return pl.ds(pl.multiple_of(base + offset, rows), rows)

            gate_up = dot_nn(arena[at(x_base), :], expand[...])
            grad_hidden = dot_nt(arena[at(cot_base), :], inner[...])
            gate, up = gate_up[:, :size], gate_up[:, size:]
            activated, slope = gelu_parts(gate)
            low = (activated * up).astype(BF16)
            r.hidden[here, :size] = low
            r.grad_gate_up[here, :size] = (grad_hidden * up * slope).astype(BF16)
            r.grad_gate_up[here, size : 2 * size] = (grad_hidden * activated).astype(BF16)
            out = dot_nn(low, inner[...])
            if number:
                out = out + arena[at(branch_base), :].astype(F32)
            arena[at(branch_base), :] = out.astype(BF16)
            back = dot_nt(r.grad_gate_up[here, : 2 * size], expand[...])
            if number:
                back = back + arena[at(back_base), :].astype(F32)
            arena[at(back_base), :] = back.astype(BF16)
            return carry

        lax.fori_loop(0, 8, tile, 0)

    third = features // 3

    def weight_grads(number):
        size = chunks[number][2]
        wires.drain("chunk_%d" % number)

        def contract_tile(index, carry):
            here = pl.ds(pl.multiple_of(index * 128, 128), 128)
            for first in range(0, features, third):
                cot = arena[cot_base : cot_base + all_rows, first : first + third]
                out = dot_tn(r.hidden[:, here], cot).astype(BF16)
                inners[number][here, first : first + third] = out
            return carry

        lax.fori_loop(0, size // 128, contract_tile, 0)

        def expand_tile(index, carry):
            here = pl.ds(pl.multiple_of(index * third, third), third)
            lhs = arena[x_base : x_base + all_rows, here]
            experts[number][here, :] = dot_tn(lhs, r.grad_gate_up[:, : 2 * size]).astype(BF16)
            return carry

        lax.fori_loop(0, 3, expand_tile, 0)

    chain_sums = []
    stages = n_dp // 2 + 1
    free_rows = output_again + QD
    assert 2 * stages * plane_rows <= all_rows
    assert free_rows + stages * (chunks[0][1] + chunks[1][1]) <= branch_base
    for number, (_, count, size) in enumerate(chunks):
        pair = []
        for place, land, rooms, kind in (
            (
                expand_place(number),
                (r.land_0, r.land_1, r.land_2)[number],
                [
                    r.grad_gate_up.at[
                        pl.ds(((number % 2) * stages + k) * plane_rows, plane_rows), pl.ds(0, 2 * size)
                    ]
                    for k in range(stages)
                ],
                0,
            ),
            (
                contract_place(number),
                (r.land_c0, r.land_c1, r.land_c2)[number],
                [
                    rows_of(arena, free_rows + (number % 2) * stages * chunks[0][1] + k * count, count)
                    for k in range(stages)
                ],
                1,
            ),
        ):
            get = functools.partial(lambda ref, j: ref.at[j], land)
            pair.append(
                ChainSum(
                    wires,
                    n_dp,
                    place,
                    get,
                    "sums_%d" % number,
                    rooms,
                    [
                        r.local_sems.at[11 + ((number % 2) * 2 + kind) * stages + k]
                        for k in range(stages)
                    ],
                )
            )
        chain_sums.append(pair)

    def level(number, *steps):
        for step in steps:
            if step:
                for one in chain_sums[number]:
                    one.arrive(step)
            for one in chain_sums[number]:
                one.level(step)

    inner_steps = range(1, n_dp // 2)

    def diagonal():
        tokens_gather.relay_last()
        cotangent_gather.wait_last()
        tokens_gather.wait_last()

    def near_x():
        for gather in (cotangent_gather, tokens_gather):
            gather.wait_core_x()

    def near_y():
        for gather in (cotangent_gather, tokens_gather):
            gather.wait_core_y()

    def near_y_and_hop():
        near_y()
        weights[1].hop(1)

    chunk(0, (0, 1, 2, 3), {2: near_x, 4: near_y_and_hop, 6: diagonal})
    weight_grads(0)
    level(0, 0)
    weights[1].hop(*range(2, hops))
    weights[2].hop(0)
    chunk(1, (0, 1, 2, 3), {6: lambda: weights[2].hop(1)})
    weight_grads(1)
    level(1, 0)
    weights[2].hop(*range(2, hops))
    wires.drain("pieces")
    branch_sum, back_sum = (
        PlaneSum(wires, arena, base, rows, r.cores.at[i], r.diag.at[i], r.sides.at[i], "plane")
        for i, base in enumerate((branch_base, back_base))
    )

    def add_core(one, k):
        stage = r.core_stage.at[0, pl.ds(0, rows)]
        one.fetch_core(k, stage, r.local_sems.at[6]).wait()
        one.add_core(k, stage)

    def send_core(k):
        back_sum.send_core(k)
        branch_sum.send_core(k)

    def after_diagonal():
        send_core(3)

    def after_x():
        send_core(1)
        add_core(back_sum, 3)
        back_sum.send_diag()

    def after_y():
        send_core(2)
        add_core(back_sum, 1)
        back_sum.send_x()

    chunk(2, (3, 1, 2, 0), {2: after_diagonal, 4: after_x, 6: after_y})
    send_core(0)
    add_core(back_sum, 2)
    back_sum.send_y()
    add_core(back_sum, 0)
    wires.drain("tokens", "cotangent")
    weight_grads(2)
    get_output = load(r.output_kept, arena.at[pl.ds(output_again, QD)], 2)
    get_cotangent = load(r.cotangent, r.branch_low, 3)
    level(2, 0)
    for pair in chain_sums:
        for one in pair:
            one.send_near()
    back_sum.send_second()
    level(0, *inner_steps)
    add_core(branch_sum, 3)
    branch_sum.send_diag()
    add_core(branch_sum, 1)
    branch_sum.send_x()
    add_core(branch_sum, 2)
    branch_sum.send_y()
    add_core(branch_sum, 0)
    grad_normed = back_sum.total()
    middle = r.middle[...]
    grad_middle, gain_two = norm_backward(
        middle, norm_scale(middle), r.gains_full[1:2, :], grad_normed
    )
    get_cotangent.wait()
    r.grad_middle[...] = grad_middle + r.branch_low[...].astype(F32)
    r.branch_low[...] = r.grad_middle[...].astype(BF16)
    output_sum, qkv_sum = (
        SlotSum(
            wires,
            n_dp,
            arena,
            base,
            size,
            cores,
            diag,
            sides,
            land,
            tag,
            [r.core_stage.at[k, pl.ds(0, n_dp * size)] for k in range(2)],
            [r.local_sems.at[6 + k] for k in range(2)],
        )
        for base, size, cores, diag, sides, land, tag in (
            (0, share_out, r.output_cores, r.output_diag, r.output_sides, r.output_land, "output"),
            (n_all * share_out, folded, r.qkv_cores, r.qkv_diag, r.qkv_sides, r.qkv_land, "qkv"),
        )
    )
    gains_sum = SlotSum(
        wires, n_dp, r.gain_slots, 0, 8, r.gain_cores, r.gain_diag, r.gain_sides, r.gain_land, "gains"
    )
    for j in range(n_dp):
        first = 8 * share_out * j
        part = dot_tn(r.mixture[:, first : first + 8 * share_out], r.branch_low[...]).astype(BF16)
        for k in range(4):
            for e in range(2):
                slot = ((e * 4 + k) * n_dp + j) * share_out
                inner = (k * 2 + e) * share_out
                arena[slot : slot + share_out, :] = part[inner : inner + share_out, :]
    output_sum.send_core()
    level(1, *inner_steps)
    get_output.wait()
    r.grad_mixture[...] = dot_nt(
        r.branch_low[...], arena[output_again : output_again + QD, :]
    ).astype(BF16)
    r.grad_window[...] = jnp.zeros_like(r.grad_window)

    def head_back(h, carry):
        mine = pl.ds(pl.multiple_of(h * HD, HD), HD)
        probs = jnp.exp(scores_of(h) - r.log_totals[h])
        grad_mixture = r.grad_mixture[:, mine]
        grad_probs = dot_nt(grad_mixture, r.window[:, HD : 2 * HD])
        row_dot = jnp.sum(probs * grad_probs, axis=-1, keepdims=True)
        grad_scores = (probs * (grad_probs - row_dot)).astype(BF16)
        grad_queries = dot_nn(grad_scores, r.window[:, 0:HD]) * scale
        r.grad_projected[:, mine] = grad_queries.astype(BF16)
        r.grad_window[:, 0:HD] += dot_tn(grad_scores, r.queries[:, mine]) * scale
        r.grad_window[:, HD : 2 * HD] += dot_tn(probs.astype(BF16), grad_mixture)
        return carry

    lax.fori_loop(0, HQ, head_back, 0)
    r.window_out[...] = r.grad_window[0:WINDOW, :].astype(BF16)
    later = []
    for distance in range(1, reach + 1):
        after, before = me + distance, me - distance
        index = kv_index + reach + distance - 1
        first = WINDOW - distance * rows
        wires.send(
            r.window_out.at[pl.ds(first, rows)],
            r.window_in.at[distance - 1],
            device_at(jnp.clip(before, 0, n_all - 1)),
            index,
            before >= 0,
            "window",
        )
        source = device_at(jnp.clip(after, 0, n_all - 1))
        later.append((r.window_in.at[distance - 1], source, index, after <= n_all - 1))
    output_sum.send_first()
    branch_sum.send_second()

    def qkv_grads(first, count):
        def tile(index, carry):
            here = pl.ds(pl.multiple_of(index * 128, 128), 128)
            there = slice(first, first + count)
            out = dot_tn(r.normed[:, here], r.grad_projected[:, there]).astype(BF16)
            r.qkv_full[here, there] = out
            return carry

        lax.fori_loop(0, features // 128, tile, 0)

    r.grad_normed[...] = dot_nt(r.grad_projected[:, 0:QD], r.qkv_full[:, 0:QD])
    qkv_grads(0, QD)
    for arrival in later:
        wires.wait(*arrival)

        @pl.when(arrival[3])
        def _(arrival=arrival):
            r.grad_window[WINDOW:, :] += arrival[0][...].astype(F32)

    r.grad_projected[:, QD:] = r.grad_window[WINDOW:, :].astype(BF16)
    grad_normed = r.grad_normed[...] + dot_nt(r.grad_projected[:, QD:], r.qkv_full[:, QD:])
    r.grad_normed[...] = grad_normed
    qkv_grads(QD, wide - QD)
    for d, j, k, e in blocks:
        slot = n_all * share_out + ((e * 4 + k) * n_dp + j) * folded
        fold(arena, slot, r.qkv_full, share * d, share)
    qkv_sum.send_core()
    output_sum.send_second()
    inputs = r.tokens[...].astype(F32)
    grad_inputs, gain_one = norm_backward(
        inputs, norm_scale(inputs), r.gains_full[0:1, :], r.grad_normed[...]
    )
    r.grad_middle[...] = r.grad_middle[...] + grad_inputs
    put_input_grad = load(r.grad_middle, r.input_grad, 0)
    qkv_sum.send_first()
    r.gain_slots[...] = jnp.zeros_like(r.gain_slots)
    for d, j, k, e in blocks:
        slot = ((e * 4 + k) * n_dp + j) * 8
        for row, gain in enumerate((gain_one, gain_two)):
            r.gain_slots[slot + row : slot + row + 1, 0:share] = gain[:, share * d : share * (d + 1)]
    gains_sum.send_core()
    level(2, *inner_steps)

    def give_back(number):
        for one in chain_sums[number]:
            one.receive()
        for one in chain_sums[number]:
            one.collect()
        size = 2 * chunks[number][2]
        r.stage[0:plane_rows, 0:size] = expand_place(number)(q)[...]
        for group in range(8):
            r.pieces_out[group, :, columns(number)] = r.stage[
                share * group : share * (group + 1), 0:size
            ]
        back = exchange(number, "give_back")
        first, count, _ = chunks[number]
        used = min(first + count, ff_block) - first
        r.sum_contract[first : first + used, :] = contract_place(number)(q)[...][0:used, :]
        return back

    def take_back(chosen):
        backs[chosen].finish()
        for group, source, size, number, place in pieces:
            if number == chosen:
                at = starts[number] + place
                r.sum_expand[:, source : source + size] = r.pieces_in[group, :, at : at + size]

    gains_sum.send_first()
    qkv_sum.send_second()
    output_sum.add_sides()
    output_sum.chain.send_near()
    backs = [give_back(0)]
    gains_sum.send_second()
    r.block_out[...] = (r.middle[...] + branch_sum.total()).astype(BF16)
    for one in (qkv_sum, gains_sum):
        one.add_sides()
        one.chain.send_near()
    backs.append(give_back(1))
    take_back(0)
    output_sum.chain.receive()
    output_sum.chain.collect()
    r.sum_output[...] = output_sum.chain.own(q)[...].astype(F32)
    backs.append(give_back(2))
    take_back(1)
    for one in (qkv_sum, gains_sum):
        one.chain.receive()
        one.chain.collect()
    r.own_qkv[...] = qkv_sum.chain.own(q)[...]
    unfold(r.sum_qkv, 0, share, r.own_qkv, 0)
    r.sum_gains[...] = gains_sum.chain.own(q)[...]
    take_back(2)
    put_input_grad.wait()
    wires.drain()


def run_block(n_dp, tokens, cotangent, qkv, output, gains, expand, contract):
    n_all = 8 * n_dp
    rows, features = tokens.shape
    share, wide = qkv.shape
    share_out = output.shape[0]
    ff_block = contract.shape[0]
    plane_rows = 8 * share
    folded = share + share // 3
    padded, width, chunks, pieces = hidden_layout(n_dp, ff_block)
    largest = max(size for _, _, size in chunks)
    hbm, vmem = pl.BlockSpec(memory_space=pl.ANY), pl.BlockSpec(memory_space=pltpu.VMEM)
    outs = {
        "block_out": ((rows, features), BF16),
        "input_grad": ((rows, features), F32),
        "sum_qkv": ((share, wide), F32),
        "sum_output": ((share_out, features), F32),
        "sum_gains": ((8, 128), F32),
        "sum_expand": (expand.shape, BF16),
        "sum_contract": ((ff_block, features), BF16),
    }
    lands = {
        "land_%d" % i: ((2 * n_dp + 1, plane_rows, 2 * size), BF16)
        for i, (_, _, size) in enumerate(chunks)
    }
    for i, (_, count, _) in enumerate(chunks):
        lands["land_c%d" % i] = ((2 * n_dp + 1, count, features), BF16)
    lands["cores"] = ((2, 4, rows, features), BF16)
    lands["output_kept"] = ((QD, features), BF16)
    lands["output_cores"] = ((4 * n_dp * share_out, features), BF16)
    lands["qkv_cores"] = ((4 * n_dp * folded, features), BF16)

    def sums(name, size, columns, dtype):
        return {
            name + "_diag": ((n_dp * size, columns), dtype),
            name + "_sides": ((2 * n_dp * size, columns), dtype),
            name + "_land": (((2 * n_dp + 1) * size, columns), dtype),
        }

    scratch = {
        "arena": ((32 * rows, features), BF16),
        **{"expand_%d" % i: ((features, 2 * size), BF16) for i, (_, _, size) in enumerate(chunks)},
        **{"contract_%d" % i: ((size, features), BF16) for i, (_, _, size) in enumerate(chunks)},
        "hidden": ((8 * rows, largest), BF16),
        "grad_gate_up": ((8 * rows, 2 * largest), BF16),
        "stage": ((plane_rows, max(features, 2 * largest)), BF16),
        "core_stage": ((2, max(rows, n_dp * folded), features), BF16),
        "diag": ((2, 2, rows // 2, features), BF16),
        "sides": ((2, 2, rows, features), BF16),
        "pieces_out": ((8, share, 2 * width), BF16),
        "pieces_in": ((8, share, 2 * width), BF16),
        "grad_middle": ((rows, features), F32),
        "grad_normed": ((rows, features), F32),
        "own_qkv": ((folded, features), BF16),
        "gain_slots": ((n_all * 8, 128), F32),
        "gains_full": ((8, features), F32),
        "qkv_full": ((features, wide), BF16),
        "normed": ((rows, features), BF16),
        "queries": ((rows, QD), BF16),
        "window": ((WINDOW + rows, 2 * HD), BF16),
        "log_totals": ((HQ, rows, 1), F32),
        "mixture": ((rows, QD), BF16),
        "middle": ((rows, features), F32),
        "branch_low": ((rows, features), BF16),
        "grad_mixture": ((rows, QD), BF16),
        "grad_window": ((WINDOW + rows, 2 * HD), F32),
        "window_out": ((WINDOW, 2 * HD), BF16),
        "window_in": ((WINDOW // rows, rows, 2 * HD), BF16),
        "grad_projected": ((rows, wide), BF16),
        **sums("output", share_out, features, BF16),
        **sums("qkv", folded, features, BF16),
        **sums("gain", 8, 128, F32),
        "gain_cores": ((4 * n_dp * 8, 128), F32),
    }
    names = (*INPUTS, *outs, *lands, *scratch, "local_sems", "send_sems", "recv_sems")
    results = pl.pallas_call(
        functools.partial(block_kernel, n_dp, names),
        out_shape=[jax.ShapeDtypeStruct(*s) for s in (*outs.values(), *lands.values())],
        in_specs=[vmem, hbm, vmem, vmem, vmem, hbm, hbm],
        out_specs=[hbm if name == "input_grad" else vmem for name in outs] + [hbm] * len(lands),
        scratch_shapes=[pltpu.VMEM(*s) for s in scratch.values()]
        + [
            pltpu.SemaphoreType.DMA((11 + 4 * (n_dp // 2 + 1),)),
            pltpu.SemaphoreType.DMA((WIRES,)),
            pltpu.SemaphoreType.DMA((WIRES,)),
        ],
        compiler_params=pltpu.CompilerParams(
            collective_id=0, has_side_effects=True, vmem_limit_bytes=VMEM_LIMIT
        ),
        name="transformer_block",
    )(tokens, cotangent, qkv, output, gains, expand, contract)
    return results[: len(outs)]


def adamw_update(weight, gradient, first, second, rate, decay_rate):
    mean_new = BETA_FIRST * first + (1.0 - BETA_FIRST) * gradient
    square_new = BETA_SECOND * second + (1.0 - BETA_SECOND) * gradient * gradient
    mean_hat = mean_new / (1.0 - BETA_FIRST**STEP)
    square_hat = square_new / (1.0 - BETA_SECOND**STEP)
    updated = weight - rate * (
        mean_hat / (jnp.sqrt(square_hat) + ADAM_EPSILON) + decay_rate * weight
    )
    return (updated, mean_new, square_new)


def shards_kernel(tokens, cotangent, *arguments):
    weights, firsts, seconds = arguments[:5], arguments[5:10], arguments[10:15]
    qkv, output, expand, contract, gains = weights
    share = gains.shape[1]
    gains_tile = jnp.pad(gains.astype(F32), ((0, 6), (0, 128 - share)))
    block_out, input_grad, *sums = run_block(
        lax.axis_size("ctx") // 2, tokens, cotangent, qkv, output, gains_tile, expand, contract
    )
    sum_qkv, sum_output, sum_gains, sum_expand, sum_contract = sums
    gradients = (sum_qkv, sum_output, sum_expand, sum_contract, sum_gains[:2, :share])
    rates = (RATE_MATRIX,) * 4 + (RATE_GAINS,)
    decays = (WEIGHT_DECAY,) * 4 + (0.0,)
    updates = [
        adamw_update(weight.astype(F32), gradient.astype(F32), first, second, rate, decay)
        for weight, gradient, first, second, rate, decay in zip(
            weights, gradients, firsts, seconds, rates, decays
        )
    ]
    return (
        block_out,
        input_grad,
        *(new for new, _, _ in updates),
        *(mean for _, mean, _ in updates),
        *(square for _, _, square in updates),
    )


def passed_along(block, axis, distance):
    devices = range(lax.axis_size(axis))
    route = [(i - distance, i) for i in devices if i - distance in devices]
    return lax.ppermute(block, axis, route)


def norm_forward(values, gain_row):
    scale = norm_scale(values)
    return (values * scale * gain_row, scale)


def shards_plain(
    tokens,
    cotangent,
    qkv_weight,
    output_weight,
    expand_weight,
    contract_weight,
    norm_gains,
    first_qkv,
    first_output,
    first_expand,
    first_contract,
    first_gains,
    second_qkv,
    second_output,
    second_expand,
    second_contract,
    second_gains,
):
    tok_dev = tokens.shape[0]
    n_fsdp = lax.axis_size("fsdp")
    n_ctx = lax.axis_size("ctx")
    ff_block = FF // (n_ctx * n_fsdp)
    score_scale = 1.0 / math.sqrt(HD)
    fsdp_index = lax.axis_index("fsdp")
    ctx_index = lax.axis_index("ctx")
    qkv_full, output_full, gains_full = (
        lax.all_gather(qkv_weight, ("ctx", "fsdp"), axis=0, tiled=True),
        lax.all_gather(output_weight, ("ctx", "fsdp"), axis=0, tiled=True),
        lax.all_gather(norm_gains, ("ctx", "fsdp"), axis=1, tiled=True),
    )
    arranged = expand_weight.reshape(expand_weight.shape[0], 2, n_ctx, n_fsdp, ff_block)
    arranged = lax.all_to_all(arranged, "fsdp", split_axis=3, concat_axis=0, tiled=True)
    arranged = arranged.reshape(arranged.shape[0], 2 * n_ctx * ff_block)
    expand_use, contract_use = (
        lax.all_gather(arranged, "ctx", axis=0, tiled=True),
        lax.all_gather(contract_weight, "ctx", axis=0, tiled=True),
    )
    width = n_ctx * ff_block
    gains_float = gains_full.astype(jnp.float32)
    inputs = tokens.astype(jnp.float32)
    normed, scale_one = norm_forward(inputs, gains_float[0])
    normed_low = normed.astype(jnp.bfloat16)
    projected = jnp.dot(normed_low, qkv_full, preferred_element_type=jnp.float32).astype(
        jnp.bfloat16
    )
    queries = projected[:, : HQ * HD].reshape(tok_dev, HQ, HD)
    key_value = projected[:, HQ * HD :]
    reach = (WINDOW + tok_dev - 1) // tok_dev
    earlier_pieces = []
    for distance in range(reach, 0, -1):
        earlier_pieces.append(passed_along(key_value, ("ctx", "fsdp"), distance))
    earlier = jnp.concatenate(earlier_pieces, axis=0)
    window_kv = jnp.concatenate([earlier, key_value], axis=0)
    key_rows = window_kv[:, :HD]
    value_rows = window_kv[:, HD:]
    offset = (ctx_index * n_fsdp + fsdp_index) * tok_dev
    row_index = lax.broadcasted_iota(jnp.int32, (tok_dev, WINDOW + tok_dev), 0)
    col_index = lax.broadcasted_iota(jnp.int32, (tok_dev, WINDOW + tok_dev), 1)
    visible = (
        (col_index > row_index) & (col_index <= row_index + WINDOW) & (col_index + offset >= WINDOW)
    )

    def masked_scores():
        raw_scores = (
            jnp.einsum("qhd,kd->hqk", queries, key_rows, preferred_element_type=jnp.float32)
            * score_scale
        )
        return jnp.where(visible[None], raw_scores, MASKED_SCORE)

    scores = masked_scores()
    log_total = jax.nn.logsumexp(scores, axis=-1, keepdims=True)
    probs_low = jnp.exp(scores - log_total).astype(jnp.bfloat16)
    mixture = jnp.einsum("hqk,kd->qhd", probs_low, value_rows, preferred_element_type=jnp.float32)
    mixture_low = mixture.reshape(tok_dev, HQ * HD).astype(jnp.bfloat16)
    middle = inputs + jnp.dot(mixture_low, output_full, preferred_element_type=jnp.float32)
    normed_two, scale_two = norm_forward(middle, gains_float[1])
    normed_two_low = normed_two.astype(jnp.bfloat16)
    ffn_input, ffn_cotangent = (
        lax.all_gather(normed_two_low, "fsdp", axis=0, tiled=True),
        lax.all_gather(cotangent, "fsdp", axis=0, tiled=True),
    )
    gate_up = jnp.dot(ffn_input, expand_use, preferred_element_type=jnp.float32)
    gate_part = gate_up[:, :width]
    up_part = gate_up[:, width:]
    activated, gelu_back = jax.vjp(functools.partial(jax.nn.gelu, approximate=True), gate_part)
    hidden_low = (activated * up_part).astype(jnp.bfloat16)
    branch_two = jnp.dot(hidden_low, contract_use, preferred_element_type=jnp.float32)
    branch_two = lax.psum_scatter(
        branch_two.astype(jnp.bfloat16), "fsdp", scatter_dimension=0, tiled=True
    ).astype(jnp.float32)
    result = middle + branch_two
    block_out = result.astype(jnp.bfloat16)
    grad_result = cotangent.astype(jnp.float32)
    grad_contract = jnp.einsum(
        "tf,td->fd", hidden_low, ffn_cotangent, preferred_element_type=jnp.float32
    )
    grad_hidden = jnp.einsum(
        "td,fd->tf", ffn_cotangent, contract_use, preferred_element_type=jnp.float32
    )
    (grad_gate,) = gelu_back(grad_hidden * up_part)
    grad_gate_up = jnp.concatenate([grad_gate, grad_hidden * activated], axis=1).astype(
        jnp.bfloat16
    )
    grad_expand = jnp.einsum(
        "td,tf->df", ffn_input, grad_gate_up, preferred_element_type=jnp.float32
    )
    grad_normed_two = jnp.einsum(
        "tf,df->td", grad_gate_up, expand_use, preferred_element_type=jnp.float32
    )
    grad_normed_two = lax.psum_scatter(grad_normed_two, "fsdp", scatter_dimension=0, tiled=True)
    part_expand, sum_contract = (
        lax.psum_scatter(
            grad_expand.astype(jnp.bfloat16), "ctx", scatter_dimension=0, tiled=True
        ).astype(jnp.float32),
        lax.psum_scatter(
            grad_contract.astype(jnp.bfloat16), "ctx", scatter_dimension=0, tiled=True
        ).astype(jnp.float32),
    )
    part_expand = part_expand.reshape(part_expand.shape[0], 2, n_ctx, 1, ff_block)
    sum_expand = lax.all_to_all(part_expand, "fsdp", split_axis=0, concat_axis=3, tiled=True)
    sum_expand = sum_expand.reshape(sum_expand.shape[0], 2 * FF)
    grad_norm_two, gain_grad_two = norm_backward(middle, scale_two, gains_float[1], grad_normed_two)
    grad_middle = grad_result + grad_norm_two
    grad_branch = grad_middle.astype(jnp.bfloat16)
    grad_output = jnp.einsum(
        "tc,td->cd", mixture_low, grad_branch, preferred_element_type=jnp.float32
    )
    grad_mixture = jnp.einsum(
        "td,cd->tc", grad_branch, output_full, preferred_element_type=jnp.float32
    )
    grad_mixture = grad_mixture.astype(jnp.bfloat16).reshape(tok_dev, HQ, HD)
    again_scores = masked_scores()
    again_probs = jnp.exp(again_scores - log_total)
    again_low = again_probs.astype(jnp.bfloat16)
    grad_probs = jnp.einsum(
        "qhd,kd->hqk", grad_mixture, value_rows, preferred_element_type=jnp.float32
    )
    row_dot = jnp.sum(again_probs * grad_probs, axis=-1, keepdims=True)
    grad_scores = (again_probs * (grad_probs - row_dot)).astype(jnp.bfloat16)
    grad_queries = (
        jnp.einsum("hqk,kd->qhd", grad_scores, key_rows, preferred_element_type=jnp.float32)
        * score_scale
    )
    grad_keys = (
        jnp.einsum("hqk,qhd->kd", grad_scores, queries, preferred_element_type=jnp.float32)
        * score_scale
    )
    grad_values = jnp.einsum(
        "hqk,qhd->kd", again_low, grad_mixture, preferred_element_type=jnp.float32
    )
    grad_window = jnp.concatenate([grad_keys, grad_values], axis=1)
    grad_key_value = grad_window[WINDOW:]
    grad_earlier = jnp.concatenate(
        [jnp.zeros((reach * tok_dev - WINDOW, 2 * HD), jnp.float32), grad_window[:WINDOW]], axis=0
    )
    for position in range(reach):
        piece = grad_earlier[position * tok_dev : (position + 1) * tok_dev]
        grad_key_value = grad_key_value + passed_along(
            piece.astype(jnp.bfloat16), ("ctx", "fsdp"), position - reach
        ).astype(piece.dtype)
    grad_projected = jnp.concatenate(
        [grad_queries.reshape(tok_dev, HQ * HD), grad_key_value], axis=1
    ).astype(jnp.bfloat16)
    grad_qkv = jnp.einsum(
        "td,tc->dc", normed_low, grad_projected, preferred_element_type=jnp.float32
    )
    grad_normed = jnp.einsum(
        "tc,dc->td", grad_projected, qkv_full, preferred_element_type=jnp.float32
    )
    grad_norm_one, gain_grad_one = norm_backward(inputs, scale_one, gains_float[0], grad_normed)
    input_grad = grad_middle + grad_norm_one
    grad_gains = jnp.concatenate([gain_grad_one, gain_grad_two], axis=0)
    sum_qkv, sum_output, sum_gains = (
        lax.psum_scatter(grad_qkv, ("ctx", "fsdp"), scatter_dimension=0, tiled=True),
        lax.psum_scatter(grad_output, ("ctx", "fsdp"), scatter_dimension=0, tiled=True),
        lax.psum_scatter(grad_gains, ("ctx", "fsdp"), scatter_dimension=1, tiled=True),
    )
    new_qkv, mean_qkv, square_qkv = adamw_update(
        qkv_weight.astype(jnp.float32), sum_qkv, first_qkv, second_qkv, RATE_MATRIX, WEIGHT_DECAY
    )
    new_output, mean_output, square_output = adamw_update(
        output_weight.astype(jnp.float32),
        sum_output,
        first_output,
        second_output,
        RATE_MATRIX,
        WEIGHT_DECAY,
    )
    new_expand, mean_expand, square_expand = adamw_update(
        expand_weight.astype(jnp.float32),
        sum_expand,
        first_expand,
        second_expand,
        RATE_MATRIX,
        WEIGHT_DECAY,
    )
    new_contract, mean_contract, square_contract = adamw_update(
        contract_weight.astype(jnp.float32),
        sum_contract,
        first_contract,
        second_contract,
        RATE_MATRIX,
        WEIGHT_DECAY,
    )
    new_gains, mean_gains, square_gains = adamw_update(
        norm_gains.astype(jnp.float32), sum_gains, first_gains, second_gains, RATE_GAINS, 0.0
    )
    return (
        block_out,
        input_grad,
        new_qkv,
        new_output,
        new_expand,
        new_contract,
        new_gains,
        mean_qkv,
        mean_output,
        mean_expand,
        mean_contract,
        mean_gains,
        square_qkv,
        square_output,
        square_expand,
        square_contract,
        square_gains,
    )


def shards(*arguments):
    plane_rows = 8 * arguments[4].shape[0]
    return (shards_kernel if plane_rows % 16 == 0 else shards_plain)(*arguments)


def solution(mesh):
    rows, columns = P(("ctx", "fsdp"), None), P(None, ("ctx", "fsdp"))
    in_specs = (rows,) * 6 + (columns,) + ((rows,) * 4 + (columns,)) * 2
    out_specs = (rows,) * 2 + ((rows,) * 4 + (columns,)) * 3
    return jax.shard_map(shards, mesh=mesh, in_specs=in_specs, out_specs=out_specs, check_vma=False)
```

```python
import functools
import math
import types

import jax
import jax.numpy as jnp
from jax import lax
from jax.experimental import pallas as pl
from jax.experimental.pallas import tpu as pltpu
from jax.sharding import PartitionSpec as P

HQ = 4
HD = 256
FF = 6912
WINDOW = 512
STEP = 10

NORM_EPSILON = 1e-06
BETA_FIRST = 0.9
BETA_SECOND = 0.999
RATE_MATRIX = 0.1
RATE_GAINS = 0.5
WEIGHT_DECAY = 0.1
ADAM_EPSILON = 1e-08
MASKED_SCORE = -1e30

F32 = jnp.float32
BF16 = jnp.bfloat16
MESH = pl.DeviceIdType.MESH
VMEM_LIMIT = 65400 * 1024
WIRES = 400
QD = HQ * HD


def position():
    ctx, fsdp = lax.axis_index("ctx"), lax.axis_index("fsdp")
    return ctx // 2, lax.rem(ctx, 2), fsdp // 2, lax.rem(fsdp, 2)


def device(q, y, x, c):
    return (q * 2 + y, x * 2 + c)


def device_at(index):
    return (index // 4, lax.rem(index, 4))


def rows_of(ref, first, count):
    if not isinstance(first, int):
        first = pl.multiple_of(first, 16 if ref.dtype == BF16 else 8)
    return ref.at[pl.ds(first, count)]


def gelu_parts(u):
    k = math.sqrt(2.0 / math.pi)
    square = u * u
    t = jnp.tanh(k * u * (1.0 + 0.044715 * square))
    half = 0.5 * (1.0 + t)
    slope = half + 0.5 * u * (1.0 - t * t) * (k * (1.0 + (3.0 * 0.044715) * square))
    return u * half, slope


def dot_nt(a, b):
    return lax.dot_general(a, b, (((1,), (1,)), ((), ())), preferred_element_type=F32)


def dot_tn(a, b):
    return lax.dot_general(a, b, (((0,), (0,)), ((), ())), preferred_element_type=F32)


def dot_nn(a, b):
    return jnp.dot(a, b, preferred_element_type=F32)


def norm_scale(values):
    return lax.rsqrt(jnp.mean(values * values, axis=-1, keepdims=True) + NORM_EPSILON)


def norm_backward(values, scale, gain_row, grad_normed):
    gain_grad = jnp.sum(grad_normed * values * scale, axis=0, keepdims=True)
    scaled = grad_normed * gain_row
    cubed = scale * scale * scale
    grad_values = scale * scaled - values * cubed * jnp.mean(
        scaled * values, axis=-1, keepdims=True
    )
    return grad_values, gain_grad


class Wires:
    def __init__(self, send_sems, recv_sems):
        self.send_sems, self.recv_sems = send_sems, recv_sems
        self.count = 0
        self.sent = {}
        self.tag = None

    def take(self, number=1):
        first = self.count
        self.count += number
        assert self.count <= WIRES, self.count
        return first

    def copy(self, src, dst, target, index, send_index=None):
        return pltpu.make_async_remote_copy(
            src_ref=src,
            dst_ref=dst,
            send_sem=self.send_sems.at[index if send_index is None else send_index],
            recv_sem=self.recv_sems.at[index],
            device_id=target,
            device_id_type=MESH,
        )

    def send(self, src, dst, target, index, when=None, tag=None, send_index=None):
        def make():
            here, there, other = (v() if callable(v) else v for v in (src, dst, target))
            return self.copy(here, there, other, index, send_index)

        self.run(lambda: make().start(), when)
        self.sent.setdefault(tag, []).append((lambda: make().wait_send(), when))

    def run(self, action, when):
        if when is None:
            action()
        else:
            pl.when(when() if callable(when) else when)(action)

    def wait(self, dst, target, index, when=None):
        copy = self.copy(dst, dst, target, index)
        if when is None:
            copy.wait_recv()
        else:
            pl.when(when)(copy.wait_recv)

    def drain(self, *tags):
        for tag in tags or list(self.sent):
            for action, when in self.sent.pop(tag, ()):
                self.run(action, when)


def greet(n_dp, reach):
    q, y, x, c = position()
    barrier = pltpu.get_barrier_semaphore()
    expected = 0

    def signal(target):
        pl.semaphore_signal(barrier, inc=1, device_id=target, device_id_type=MESH)

    for dy in range(2):
        for dx in range(2):
            for dc in range(2):
                if dy + dx + dc:
                    signal(device(q, (y + dy) % 2, (x + dx) % 2, (c + dc) % 2))
                    expected += 1
    me = (q * 2 + y) * 4 + x * 2 + c
    last = 8 * n_dp - 1
    for distance in range(1, reach + 1):
        for other in (me - distance, me + distance):
            here = (other >= 0) & (other <= last)
            pl.when(here)(functools.partial(signal, device_at(jnp.clip(other, 0, last))))
            expected = expected + here.astype(jnp.int32)
    for step in range(1, n_dp):
        signal(device(lax.rem(q + step, n_dp), y, x, c))
        expected = expected + 1
    pl.semaphore_wait(barrier, expected)


class Plane:
    def __init__(self):
        self.q, self.y, self.x, self.c = q, y, x, c = position()
        self.chips = [y * 2 + x, y * 2 + 1 - x, (1 - y) * 2 + x, (1 - y) * 2 + 1 - x]
        self.chip, self.chip_x, self.chip_y, self.chip_d = self.chips
        self.to_x, self.to_y = device(q, y, 1 - x, c), device(q, 1 - y, x, c)
        self.to_c = device(q, y, x, 1 - c)


class Chain:
    def __init__(self, wires, n_dp, own, place, tag):
        self.wires, self.n_dp, self.own, self.place, self.tag = wires, n_dp, own, place, tag
        self.first = {way: wires.take(n_dp - 1) for way in (1, -1)}

    def valid(self, way, step):
        q = position()[0]
        return (q - 1 - step >= 0) if way == 1 else (q + 1 + step <= self.n_dp - 1)

    def send(self, way, step):
        last = self.n_dp - 1

        def block():
            return jnp.clip(position()[0] - way * step, 0, last)

        def place():
            return self.place(block())

        def target():
            q, y, x, c = position()
            return device(jnp.clip(q + way, 0, last), y, x, c)

        def here():
            q = position()[0]
            origin = q - way * step
            return (origin >= 0) & (origin <= last) & (q + way >= 0) & (q + way <= last)

        src = self.own if step == 0 else place
        self.wires.send(src, place, target, self.first[way] + step, here, self.tag)

    def wait(self, way, step):
        q, y, x, c = position()
        block = jnp.clip(q - way * (step + 1), 0, self.n_dp - 1)
        self.wires.wait(
            self.place(block),
            device(jnp.clip(q + way, 0, self.n_dp - 1), y, x, c),
            self.first[way] + step,
            self.valid(way, step),
        )
        if step + 1 < self.n_dp - 1:
            self.send(way, step + 1)

    def start(self):
        self.send(1, 0)
        self.send(-1, 0)

    def hop(self, step):
        self.wait(1, step)
        self.wait(-1, step)


class PlaneGather(Plane):
    def __init__(self, wires, own, buf, base, rows, tag):
        super().__init__()
        self.wires, self.own, self.buf, self.base, self.rows = wires, own, buf, base, rows
        self.half = rows // 2
        self.tag = tag
        (self.xa, self.xb, self.ya, self.yb, self.co, self.da, self.db) = (
            wires.take() for _ in range(7)
        )
        self.cx, self.cy, self.cd = (wires.take() for _ in range(3))

    def part(self, chip, c, which=None):
        first = self.base + (chip * 2 + c) * self.rows
        if which is None:
            return rows_of(self.buf, first, self.rows)
        return rows_of(self.buf, first + which * self.half, self.half)

    def send(self, src, dst, target, index):
        self.wires.send(src, dst, target, index, None, self.tag)

    def start(self):
        c, half = self.c, self.half
        low, high = self.own.at[pl.ds(0, half)], self.own.at[pl.ds(half, half)]
        self.send(low, self.part(self.chip, c, 0), self.to_x, self.xa)
        self.send(high, self.part(self.chip, c, 1), self.to_y, self.yb)
        self.send(high, self.part(self.chip, c, 1), self.to_x, self.xb)
        self.send(low, self.part(self.chip, c, 0), self.to_y, self.ya)
        self.send(self.own, self.part(self.chip, c), self.to_c, self.co)

    def forward(self, target, index, chip, which=None):
        def part():
            return self.part(chip, self.c, which)

        self.send(part, part, target, index)

    def relay(self):
        c, wires = self.c, self.wires
        wires.wait(self.part(self.chip_x, c, 0), self.to_x, self.xa)
        self.forward(self.to_y, self.da, self.chip_x, 0)
        wires.wait(self.part(self.chip_y, c, 1), self.to_y, self.yb)
        self.forward(self.to_x, self.db, self.chip_y, 1)

    def relay_core(self):
        c, wires = self.c, self.wires
        wires.wait(self.part(self.chip_x, c, 1), self.to_x, self.xb)
        self.forward(self.to_c, self.cx, self.chip_x)
        wires.wait(self.part(self.chip_y, c, 0), self.to_y, self.ya)
        self.forward(self.to_c, self.cy, self.chip_y)

    def relay_last(self):
        c, wires = self.c, self.wires
        wires.wait(self.part(self.chip_d, c, 0), self.to_y, self.da)
        wires.wait(self.part(self.chip_d, c, 1), self.to_x, self.db)
        self.forward(self.to_c, self.cd, self.chip_d)

    def wait_core(self):
        self.wires.wait(self.part(self.chip, 1 - self.c), self.to_c, self.co)

    def wait_core_x(self):
        self.wires.wait(self.part(self.chip_x, 1 - self.c), self.to_c, self.cx)

    def wait_core_y(self):
        self.wires.wait(self.part(self.chip_y, 1 - self.c), self.to_c, self.cy)

    def wait_last(self):
        self.wires.wait(self.part(self.chip_d, 1 - self.c), self.to_c, self.cd)


class SlotGather(Plane):
    def __init__(self, wires, n_dp, own, buf, base, rows, tag):
        super().__init__()
        self.wires, self.n_dp, self.own, self.tag = wires, n_dp, own, tag
        self.buf, self.base, self.rows = buf, base, rows
        self.order = [(0, -1)] + [(way, s) for s in range(n_dp - 1) for way in (1, -1)]
        self.chain = Chain(wires, n_dp, own, lambda j: self.slot(self.c, j, self.chip), tag)
        self.kx, self.ky, self.kd, self.kc = (wires.take(len(self.order)) for _ in range(4))

    def slot(self, c, j, chip, count=1):
        return rows_of(
            self.buf, self.base + ((c * self.n_dp + j) * 4 + chip) * self.rows, count * self.rows
        )

    def each(self, ranks):
        for rank, (way, step) in enumerate(self.order):
            if ranks is not None and rank not in ranks:
                continue
            if way == 0:
                yield rank, way, step, self.q, None
            else:
                block = jnp.clip(self.q - way * (step + 1), 0, self.n_dp - 1)
                yield rank, way, step, block, self.chain.valid(way, step)

    def start(self):
        self.chain.start()

    def spread(self, ranks=None):
        for rank, way, step, j, ok in self.each(ranks):
            if way:
                self.chain.wait(way, step)
            src = self.slot(self.c, j, self.chip) if way else self.own
            dst = self.slot(self.c, j, self.chip)
            self.wires.send(src, dst, self.to_x, self.kx + rank, ok, self.tag)
            self.wires.send(src, dst, self.to_y, self.ky + rank, ok, self.tag)

    def relay(self, ranks=None):
        for rank, way, step, j, ok in self.each(ranks):
            even = lax.rem(j, 2) == 0
            odd = jnp.logical_not(even)
            sx, sy = self.slot(self.c, j, self.chip_x), self.slot(self.c, j, self.chip_y)
            self.wires.wait(sx, self.to_x, self.kx + rank, ok)
            to_y = even if ok is None else ok & even
            self.wires.send(sx, sx, self.to_y, self.kd + rank, to_y, self.tag)
            self.wires.wait(sy, self.to_y, self.ky + rank, ok)
            to_x = odd if ok is None else ok & odd
            self.wires.send(sy, sy, self.to_x, self.kd + rank, to_x, self.tag)

    def core(self, ranks=None):
        for rank, way, step, j, ok in self.each(ranks):
            self.wires.wait(self.slot(self.c, j, self.chip_d), self.to_x, self.kd + rank, ok)
            four = self.slot(self.c, j, 0, 4)
            self.wires.send(four, four, self.to_c, self.kc + rank, ok, self.tag)

    def finish(self, ranks=None):
        for rank, way, step, j, ok in self.each(ranks):
            four = self.slot(1 - self.c, j, 0, 4)
            self.wires.wait(four, self.to_c, self.kc + rank, ok)


def add_into(mine, other):
    mine[...] = (mine[...].astype(F32) + other[...].astype(F32)).astype(mine.dtype)


class ChainSum:
    def __init__(self, wires, n_dp, own, land, tag, stages=None, sems=None, straight=False):
        self.wires, self.n_dp, self.own, self.land, self.tag = wires, n_dp, own, land, tag
        self.stages, self.sems, self.straight = stages, sems, straight
        self.half = n_dp // 2
        self.direct, self.far, self.partial = wires.take(n_dp), wires.take(), wires.take(n_dp)

    def fetch(self, slot, index):
        return pltpu.make_async_copy(slot, self.stages[index], self.sems[index])

    def begin(self, slot, index, when):
        if self.stages is not None:
            self.wires.run(lambda: self.fetch(slot, index).start(), when)

    def finish(self, own, slot, index, when):
        def add():
            if self.stages is None:
                add_into(own, slot)
            else:
                self.fetch(slot, index).wait()
                add_into(own, self.stages[index])

        self.wires.run(add, when)

    def passing(self, number):
        q = position()[0]
        low = q < self.half
        here = jnp.where(low, q, self.n_dp - 1 - q) == number
        for j in [*range(self.n_dp - 1, self.half - 1, -1), *range(self.half)]:
            active = here & (low if j >= self.half else jnp.logical_not(low))
            yield j, j % self.half, self.land(self.n_dp + 1 + j), active

    def arrive(self, number):
        q, y, x, c = position()
        outward = jnp.clip(jnp.where(q < self.half, q - 1, q + 1), 0, self.n_dp - 1)
        for j, index, slot, active in self.passing(number):
            self.wires.wait(slot, device(outward, y, x, c), self.partial + j, active)
            self.begin(slot, index, active)

    def level(self, number):
        q, y, x, c = position()
        inward = jnp.where(q < self.half, q + 1, q - 1)
        for j, index, slot, active in self.passing(number):
            own = self.own(j)
            if number:
                self.finish(own, slot, index, active)
            if number < self.half - 1:
                dst, target, receive = slot, device(inward, y, x, c), self.partial + j
            else:
                dst, target, receive = self.land(self.n_dp), device(j, y, x, c), self.far
            self.wires.send(own, dst, target, receive, active, self.tag, self.partial + j)

    def near(self, j):
        q = position()[0]
        low = q < self.half
        if self.straight:
            return j != q
        return (j != q) & (low if j < self.half else jnp.logical_not(low))

    def send_near(self):
        q, y, x, c = position()
        for j in range(self.n_dp):
            self.wires.send(
                self.own(j),
                self.land(q),
                device(j, y, x, c),
                self.direct + q,
                self.near(j),
                self.tag,
                self.direct + j,
            )

    def arrivals(self):
        q, y, x, c = position()
        for j in range(self.n_dp):
            yield self.land(j), device(j, y, x, c), self.direct + j, j % self.half, self.near(j)
        if not self.straight:
            center = jnp.where(q < self.half, self.half, self.half - 1)
            yield self.land(self.n_dp), device(center, y, x, c), self.far, self.half, None

    def receive(self):
        for slot, source, number, index, when in self.arrivals():
            self.wires.wait(slot, source, number, when)
            self.begin(slot, index, when)

    def collect(self):
        for slot, source, number, index, when in self.arrivals():
            self.finish(self.own(position()[0]), slot, index, when)


class PlaneSum(Plane):
    def __init__(self, wires, buf, base, rows, cores, diag, sides, tag):
        super().__init__()
        self.wires, self.buf, self.base, self.rows, self.tag = wires, buf, base, rows, tag
        self.half = rows // 2
        self.cores, self.diag, self.sides = cores, diag, sides
        self.kc = wires.take(4)
        self.kdx, self.kdy = wires.take(), wires.take()
        self.kxa, self.kxb, self.kya, self.kyb = (wires.take() for _ in range(4))

    part = PlaneGather.part
    send = PlaneGather.send

    def send_core(self, k):
        def part():
            return self.part(self.chips[k], 1 - self.c)

        self.send(part, lambda: self.cores.at[k], self.to_c, self.kc + k)

    def fetch_core(self, k, stage, sem):
        self.wires.wait(self.cores.at[k], self.to_c, self.kc + k)
        copy = pltpu.make_async_copy(self.cores.at[k], stage, sem)
        copy.start()
        return copy

    def add_core(self, k, stage):
        add_into(self.part(self.chips[k], self.c), stage)

    def side(self, which, half):
        return self.sides.at[which, pl.ds(half * self.half, self.half)]

    def send_half(self, chip, half, dst, target, index):
        def part():
            return self.part(chip, self.c, half)

        self.send(part, dst, target, index)

    def send_diag(self):
        self.send_half(self.chip_d, 0, lambda: self.diag.at[0], self.to_x, self.kdx)
        self.send_half(self.chip_d, 1, lambda: self.diag.at[1], self.to_y, self.kdy)

    def send_x(self):
        self.send_half(self.chip_x, 0, lambda: self.side(0, 0), self.to_x, self.kxa)

    def send_y(self):
        self.send_half(self.chip_y, 1, lambda: self.side(1, 1), self.to_y, self.kyb)

    def send_second(self):
        self.wires.wait(self.diag.at[0], self.to_x, self.kdx)
        mine = self.part(self.chip_y, self.c, 0)
        add_into(mine, self.diag.at[0])
        self.send(mine, self.side(1, 0), self.to_y, self.kya)
        self.wires.wait(self.diag.at[1], self.to_y, self.kdy)
        mine = self.part(self.chip_x, self.c, 1)
        add_into(mine, self.diag.at[1])
        self.send(mine, self.side(0, 1), self.to_x, self.kxb)

    def total(self):
        self.wires.wait(self.side(0, 0), self.to_x, self.kxa)
        self.wires.wait(self.side(1, 1), self.to_y, self.kyb)
        self.wires.wait(self.side(1, 0), self.to_y, self.kya)
        self.wires.wait(self.side(0, 1), self.to_x, self.kxb)
        mine = self.part(self.chip, self.c)
        return mine[...].astype(F32) + self.sides[0].astype(F32) + self.sides[1].astype(F32)


class SlotSum(Plane):
    def __init__(
        self, wires, n_dp, buf, base, rows, cores, diag, sides, landing, tag, stages=None, sems=None
    ):
        super().__init__()
        self.wires, self.n_dp, self.tag = wires, n_dp, tag
        self.buf, self.base, self.rows = buf, base, rows
        self.cores, self.diag, self.sides = cores, diag, sides
        self.stages, self.sems = stages, sems
        self.low = n_dp // 2
        self.high = n_dp - self.low
        self.kc = wires.take(4)
        self.kdx, self.kdy, self.kx0, self.kx1, self.ky0, self.ky1 = (
            wires.take() for _ in range(6)
        )
        self.chain = ChainSum(
            wires,
            n_dp,
            lambda j: self.at(self.c, self.chip, j, 1),
            lambda j: rows_of(landing, j * rows, rows),
            tag,
            straight=True,
        )

    def at(self, c, chip, j, count):
        first = self.base + ((c * 4 + chip) * self.n_dp + j) * self.rows
        return rows_of(self.buf, first, count * self.rows)

    def four(self, ref, k):
        return ref.at[pl.ds(k * self.n_dp * self.rows, self.n_dp * self.rows)]

    def lows(self, ref, which=0):
        return ref.at[pl.ds(which * self.n_dp * self.rows, self.low * self.rows)]

    def highs(self, ref, which=0):
        first = (which * self.n_dp + self.low) * self.rows
        return ref.at[pl.ds(first, self.high * self.rows)]

    def send(self, src, dst, target, index):
        self.wires.send(src, dst, target, index, None, self.tag)

    def send_core(self):
        for k in (3, 2, 1, 0):
            src = self.at(1 - self.c, self.chips[k], 0, self.n_dp)
            self.send(src, self.four(self.cores, k), self.to_c, self.kc + k)

    def core_copy(self, k):
        return pltpu.make_async_copy(
            self.four(self.cores, k), self.stages[k % 2], self.sems[k % 2]
        )

    def wait_core(self, k):
        self.wires.wait(self.four(self.cores, k), self.to_c, self.kc + k)
        if self.stages is not None:
            self.core_copy(k).start()

    def add_core(self, k):
        other = self.four(self.cores, k)
        if self.stages is not None:
            self.core_copy(k).wait()
            other = self.stages[k % 2]
        add_into(self.at(self.c, self.chips[k], 0, self.n_dp), other)

    def send_first(self):
        low, c = self.low, self.c
        self.wait_core(3)
        self.wait_core(2)
        self.add_core(3)
        self.wait_core(1)
        self.send(self.at(c, self.chip_d, 0, low), self.lows(self.diag), self.to_x, self.kdx)
        self.send(self.at(c, self.chip_d, low, self.high), self.highs(self.diag), self.to_y, self.kdy)
        self.add_core(2)
        self.wait_core(0)
        self.send(self.at(c, self.chip_y, low, self.high), self.highs(self.sides, 1), self.to_y, self.ky1)
        self.add_core(1)
        self.send(self.at(c, self.chip_x, 0, low), self.lows(self.sides), self.to_x, self.kx0)
        self.add_core(0)

    def send_second(self):
        low, c, wires = self.low, self.c, self.wires
        wires.wait(self.lows(self.diag), self.to_x, self.kdx)
        mine = self.at(c, self.chip_y, 0, low)
        add_into(mine, self.lows(self.diag))
        self.send(mine, self.lows(self.sides, 1), self.to_y, self.ky0)
        wires.wait(self.highs(self.diag), self.to_y, self.kdy)
        mine = self.at(c, self.chip_x, low, self.high)
        add_into(mine, self.highs(self.diag))
        self.send(mine, self.highs(self.sides), self.to_x, self.kx1)

    def add_sides(self):
        wires = self.wires
        wires.wait(self.lows(self.sides), self.to_x, self.kx0)
        wires.wait(self.highs(self.sides, 1), self.to_y, self.ky1)
        wires.wait(self.lows(self.sides, 1), self.to_y, self.ky0)
        wires.wait(self.highs(self.sides), self.to_x, self.kx1)
        mine = self.at(self.c, self.chip, 0, self.n_dp)
        mine[...] = (
            mine[...].astype(F32)
            + self.four(self.sides, 0)[...].astype(F32)
            + self.four(self.sides, 1)[...].astype(F32)
        ).astype(mine.dtype)


class Exchange(Plane):
    def __init__(self, wires, pieces_out, pieces_in, local_sem, tag):
        super().__init__()
        self.wires, self.out, self.into, self.tag = wires, pieces_out, pieces_in, tag
        self.index = wires.take(7)
        self.me = self.chip * 2 + self.c
        self.copy = pltpu.make_async_copy(
            pieces_out.at[self.me], pieces_in.at[self.me], local_sem
        )

    def others(self):
        number = 0
        for dc in (0, 1):
            for dy, dx in ((1, 1), (0, 1), (1, 0), (0, 0)):
                if dy + dx + dc == 0:
                    continue
                ty, tx, tc = (self.y + dy) % 2, (self.x + dx) % 2, (self.c + dc) % 2
                yield (ty * 2 + tx) * 2 + tc, device(self.q, ty, tx, tc), self.index + number
                number += 1

    def start(self):
        for other, target, index in self.others():
            self.wires.send(
                self.out.at[other], self.into.at[self.me], target, index, None, self.tag
            )
        self.copy.start()

    def finish(self):
        for other, target, index in self.others():
            self.wires.wait(self.into.at[other], target, index)
        self.copy.wait()


def hidden_layout(n_dp, ff_block):
    unit = max(16, 128 // n_dp)
    units = -(-ff_block // unit)
    cuts = [0, -(-units * 3 // 7), -(-units * 5 // 7), units]
    chunks = [(unit * a, unit * (b - a), n_dp * unit * (b - a)) for a, b in zip(cuts, cuts[1:])]
    pieces = []
    for group in range(8):
        for part in range(2):
            for q in range(n_dp):
                source = part * FF + ff_block * (q * 8 + group)
                for number, (first, count, size) in enumerate(chunks):
                    used = min(first + count, ff_block) - first
                    place = part * size + q * count
                    pieces.append((group, source + first, used, number, place))
    return unit * units, n_dp * unit * units, chunks, pieces


INPUTS = ("tokens", "cotangent", "qkv", "output", "gains", "expand", "contract")
OUTPUTS = (
    "block_out",
    "input_grad",
    "sum_qkv",
    "sum_output",
    "sum_gains",
    "sum_expand",
    "sum_contract",
)


def fold(dst, first, src, row, share):
    wide, features = src.shape[1], dst.shape[1]
    third = share // 3
    extra = wide - features
    dst[first : first + share, :] = src[row : row + share, :features]
    for k in range(3):
        dst[first + share : first + share + third, k * extra : (k + 1) * extra] = src[
            row + third * k : row + third * (k + 1), features:
        ]


def unfold(dst, row, share, src, first):
    wide, features = dst.shape[1], src.shape[1]
    third = share // 3
    extra = wide - features
    dst[row : row + share, :features] = src[first : first + share, :].astype(dst.dtype)
    for k in range(3):
        dst[row + third * k : row + third * (k + 1), features:] = src[
            first + share : first + share + third, k * extra : (k + 1) * extra
        ].astype(dst.dtype)


def block_kernel(n_dp, names, *refs):
    r = types.SimpleNamespace(**dict(zip(names, refs, strict=True)))
    wires = Wires(r.send_sems, r.recv_sems)
    plane = Plane()
    q, y, x, c, chip = plane.q, plane.y, plane.x, plane.c, plane.chip
    me = (q * 4 + chip) * 2 + c
    n_all = 8 * n_dp
    hops = n_dp - 1
    rows, features = r.tokens.shape
    share, wide = r.qkv.shape
    share_out = r.output.shape[0]
    ff_block = r.contract.shape[0]
    plane_rows = 8 * share
    folded = share + share // 3
    padded, width, chunks, pieces = hidden_layout(n_dp, ff_block)
    experts = [r.expand_0, r.expand_1, r.expand_2]
    inners = [r.contract_0, r.contract_1, r.contract_2]
    all_rows = 8 * rows
    x_base, cot_base, branch_base, back_base = (all_rows * i for i in range(4))
    qkv_base, output_base = branch_base, branch_base + n_all * folded
    output_full, output_again = output_base + n_all * share_out, n_all * (share_out + folded)
    reach = WINDOW // rows
    scale = 1.0 / math.sqrt(HD)
    arena = r.arena
    blocks = [((j * 4 + k) * 2 + e, j, k, e) for j in range(n_dp) for k in range(4) for e in range(2)]

    def load(src, dst, number):
        copy = pltpu.make_async_copy(src, dst, r.local_sems.at[number])
        copy.start()
        return copy

    get_expand = load(r.expand, r.sum_expand, 0)
    get_contract = load(r.contract, r.sum_contract, 5)
    starts = [2 * sum(size for _, _, size in chunks[:number]) for number in range(len(chunks))]
    fold(r.own_qkv, 0, r.qkv, 0, share)
    r.pieces_out[...] = jnp.zeros_like(r.pieces_out)
    get_expand.wait()
    for group, source, size, number, place in pieces:
        at = starts[number] + place
        r.pieces_out[group, :, at : at + size] = r.sum_expand[:, source : source + size]
    get_contract.wait()

    def contract_place(number):
        count = chunks[number][1]
        return lambda j: rows_of(inners[number], j * count, count)

    def expand_place(number):
        return lambda j: rows_of(experts[number], j * plane_rows, plane_rows)

    for number, (first, count, _) in enumerate(chunks):
        used = min(first + count, ff_block) - first
        r.stage[0:used, 0:features] = r.sum_contract[first : first + used, :]
        if used < count:
            r.stage[used:count, 0:features] = jnp.zeros((count - used, features), BF16)
        contract_place(number)(q)[...] = r.stage[0:count, 0:features]
    greet(n_dp, reach)
    gains_gather = SlotGather(wires, n_dp, r.gains, r.gain_slots, 0, 8, "weights")
    qkv_gather = SlotGather(wires, n_dp, r.own_qkv, arena, qkv_base, folded, "weights")
    output_gather = SlotGather(wires, n_dp, r.output, arena, output_base, share_out, "weights")
    gathers = (gains_gather, qkv_gather, output_gather)
    firsts = (gains_gather, qkv_gather)
    ranks = len(gains_gather.order)
    for gather in firsts:
        gather.start()
        gather.spread((0,))

    def columns(number):
        return pl.ds(starts[number], 2 * chunks[number][2])

    def exchange(number, tag):
        out, into = (ref.at[:, :, columns(number)] for ref in (r.pieces_out, r.pieces_in))
        moved = Exchange(wires, out, into, r.local_sems.at[8 + number], tag)
        moved.start()
        return moved

    exchanges = [exchange(0, "pieces")]
    output_gather.start()
    own_slots = [load(g.own, g.slot(c, q, chip), 1 + i) for i, g in enumerate(gathers)]
    for gather in firsts:
        gather.spread((1, 2))
    for gather in firsts:
        gather.relay((0,))
    output_gather.spread((0,))
    for gather in firsts:
        gather.spread(range(3, ranks))

    class Chunk:
        def __init__(self, number):
            size = 2 * chunks[number][2]
            exchanges[number].finish()
            for group in range(8):
                r.stage[share * group : share * (group + 1), 0:size] = r.pieces_in[
                    group, :, starts[number] : starts[number] + size
                ]
            self.tag = "chunk_%d" % number
            self.chains = []
            for place in (expand_place(number), contract_place(number)):
                self.chains.append(Chain(wires, n_dp, place(q), place, self.tag))
            expand_place(number)(q)[...] = r.stage[0:plane_rows, 0:size]

        def start(self):
            for chain in self.chains:
                chain.start()

        def hop(self, *steps):
            for step in steps:
                for chain in self.chains:
                    chain.hop(step)

    weights = [Chunk(0)]
    weights[0].start()
    for copy in own_slots:
        copy.wait()
    for gather in firsts:
        gather.relay(range(1, ranks))
    output_gather.spread(range(1, ranks))
    exchanges.append(exchange(1, "pieces"))
    for gather in firsts:
        gather.core()
    for gather in firsts:
        gather.finish()
    for d, j, k, e in blocks:
        slot = (e * n_dp + j) * 4 + k
        unfold(r.qkv_full, share * d, share, arena, qkv_base + slot * folded)
        r.gains_full[0:2, share * d : share * (d + 1)] = r.gain_slots[
            8 * slot : 8 * slot + 2, 0:share
        ]
    inputs = r.tokens[...].astype(F32)
    r.normed[...] = (inputs * norm_scale(inputs) * r.gains_full[0:1, :]).astype(BF16)
    for first in (QD, *range(0, QD, 512)):
        part = dot_nn(r.normed[...], r.qkv_full[:, first : first + 512]).astype(BF16)
        if first < QD:
            r.queries[:, first : first + 512] = part
            continue
        r.window[WINDOW : WINDOW + rows, :] = part
        mine = r.window.at[pl.ds(WINDOW, rows)]
        kv_index = wires.take(2 * reach)
        earlier = []
        for distance in range(1, reach + 1):
            place = r.window.at[pl.ds(WINDOW - distance * rows, rows)]
            after, before = me + distance, me - distance
            index = kv_index + distance - 1
            target = device_at(jnp.clip(after, 0, n_all - 1))
            wires.send(mine, place, target, index, after <= n_all - 1, "window")

            @pl.when(before < 0)
            def _(place=place):
                place[...] = jnp.zeros_like(place)

            earlier.append((place, device_at(jnp.clip(before, 0, n_all - 1)), index, before >= 0))
    output_gather.relay()
    cotangent_gather = PlaneGather(wires, r.cotangent, arena, cot_base, rows, "cotangent")
    cotangent_gather.start()
    own_cotangent = load(r.cotangent, cotangent_gather.part(chip, c), 1)
    exchanges.append(exchange(2, "pieces"))
    output_gather.core()
    weights[0].hop(0)
    weights.append(Chunk(1))
    weights[1].start()
    output_gather.finish()
    for d, j, k, e in blocks:
        first = output_base + ((e * n_dp + j) * 4 + k) * share_out
        there = output_full + share_out * d
        arena[there : there + share_out, :] = arena[first : first + share_out, :]
    put_output = load(arena.at[pl.ds(output_full, QD)], r.output_kept, 2)
    for arrival in earlier:
        wires.wait(*arrival)
    keys = WINDOW + rows

    def visible():
        row = lax.broadcasted_iota(jnp.int32, (rows, keys), 0)
        col = lax.broadcasted_iota(jnp.int32, (rows, keys), 1)
        return (col > row) & (col <= row + WINDOW) & (col + me * rows >= WINDOW)

    def scores_of(h):
        mine = pl.ds(pl.multiple_of(h * HD, HD), HD)
        raw = dot_nt(r.queries[:, mine], r.window[:, 0:HD]) * scale
        return jnp.where(visible(), raw, MASKED_SCORE)

    def head(h, carry):
        scores = scores_of(h)
        top = jnp.max(scores, axis=-1, keepdims=True)
        log_total = top + jnp.log(jnp.sum(jnp.exp(scores - top), axis=-1, keepdims=True))
        r.log_totals[h] = log_total
        low = jnp.exp(scores - log_total).astype(BF16)
        mine = pl.ds(pl.multiple_of(h * HD, HD), HD)
        r.mixture[:, mine] = dot_nn(low, r.window[:, HD : 2 * HD]).astype(BF16)
        return carry

    lax.fori_loop(0, HQ, head, 0)
    cotangent_gather.relay()
    middle = r.tokens[...].astype(F32) + dot_nn(
        r.mixture[...], arena[output_full : output_full + QD, :]
    )
    r.middle[...] = middle
    tokens_gather = PlaneGather(wires, None, arena, x_base, rows, "tokens")
    own = tokens_gather.part(chip, c)
    tokens_gather.own = own
    own[...] = (middle * norm_scale(middle) * r.gains_full[1:2, :]).astype(BF16)
    tokens_gather.start()
    wires.drain("weights")
    own_cotangent.wait()
    put_output.wait()
    weights[0].hop(1)
    weights.append(Chunk(2))
    cotangent_gather.relay_core()
    tokens_gather.relay()
    weights[1].hop(0)
    weights[2].start()
    cotangent_gather.relay_last()
    tokens_gather.relay_core()
    for gather in (cotangent_gather, tokens_gather):
        gather.wait_core()
    for step in range(2, hops):
        weights[0].hop(step)
    chips = plane.chips

    def chunk(number, order, events):
        expand, inner = experts[number], inners[number]
        size = chunks[number][2]

        def tile(index, carry):
            for when, event in events.items():
                pl.when(index == when)(event)
            pair = index // 2
            place = chips[order[3]]
            for k in range(3):
                place = jnp.where(pair == k, chips[order[k]], place)
            offset = (place * 2 + lax.rem(index, 2)) * rows
            here = pl.ds(pl.multiple_of(offset, rows), rows)

            def at(base):
                return pl.ds(pl.multiple_of(base + offset, rows), rows)

            gate_up = dot_nn(arena[at(x_base), :], expand[...])
            grad_hidden = dot_nt(arena[at(cot_base), :], inner[...])
            gate, up = gate_up[:, :size], gate_up[:, size:]
            activated, slope = gelu_parts(gate)
            low = (activated * up).astype(BF16)
            r.hidden[here, :size] = low
            r.grad_gate_up[here, :size] = (grad_hidden * up * slope).astype(BF16)
            r.grad_gate_up[here, size : 2 * size] = (grad_hidden * activated).astype(BF16)
            out = dot_nn(low, inner[...])
            if number:
                out = out + arena[at(branch_base), :].astype(F32)
            arena[at(branch_base), :] = out.astype(BF16)
            back = dot_nt(r.grad_gate_up[here, : 2 * size], expand[...])
            if number:
                back = back + arena[at(back_base), :].astype(F32)
            arena[at(back_base), :] = back.astype(BF16)
            return carry

        lax.fori_loop(0, 8, tile, 0)

    third = features // 3

    def weight_grads(number):
        size = chunks[number][2]
        wires.drain("chunk_%d" % number)

        def contract_tile(index, carry):
            here = pl.ds(pl.multiple_of(index * 128, 128), 128)
            for first in range(0, features, third):
                cot = arena[cot_base : cot_base + all_rows, first : first + third]
                out = dot_tn(r.hidden[:, here], cot).astype(BF16)
                inners[number][here, first : first + third] = out
            return carry

        lax.fori_loop(0, size // 128, contract_tile, 0)

        def expand_tile(index, carry):
            here = pl.ds(pl.multiple_of(index * third, third), third)
            lhs = arena[x_base : x_base + all_rows, here]
            experts[number][here, :] = dot_tn(lhs, r.grad_gate_up[:, : 2 * size]).astype(BF16)
            return carry

        lax.fori_loop(0, 3, expand_tile, 0)

    chain_sums = []
    stages = n_dp // 2 + 1
    free_rows = output_again + QD
    assert 2 * stages * plane_rows <= all_rows
    assert free_rows + stages * (chunks[0][1] + chunks[1][1]) <= branch_base
    for number, (_, count, size) in enumerate(chunks):
        pair = []
        for place, land, rooms, kind in (
            (
                expand_place(number),
                (r.land_0, r.land_1, r.land_2)[number],
                [
                    r.grad_gate_up.at[
                        pl.ds(((number % 2) * stages + k) * plane_rows, plane_rows), pl.ds(0, 2 * size)
                    ]
                    for k in range(stages)
                ],
                0,
            ),
            (
                contract_place(number),
                (r.land_c0, r.land_c1, r.land_c2)[number],
                [
                    rows_of(arena, free_rows + (number % 2) * stages * chunks[0][1] + k * count, count)
                    for k in range(stages)
                ],
                1,
            ),
        ):
            get = functools.partial(lambda ref, j: ref.at[j], land)
            pair.append(
                ChainSum(
                    wires,
                    n_dp,
                    place,
                    get,
                    "sums_%d" % number,
                    rooms,
                    [
                        r.local_sems.at[11 + ((number % 2) * 2 + kind) * stages + k]
                        for k in range(stages)
                    ],
                )
            )
        chain_sums.append(pair)

    def level(number, *steps):
        for step in steps:
            if step:
                for one in chain_sums[number]:
                    one.arrive(step)
            for one in chain_sums[number]:
                one.level(step)

    inner_steps = range(1, n_dp // 2)

    def diagonal():
        tokens_gather.relay_last()
        cotangent_gather.wait_last()
        tokens_gather.wait_last()

    def near_x():
        for gather in (cotangent_gather, tokens_gather):
            gather.wait_core_x()

    def near_y():
        for gather in (cotangent_gather, tokens_gather):
            gather.wait_core_y()

    def near_y_and_hop():
        near_y()
        weights[1].hop(1)

    chunk(0, (0, 1, 2, 3), {2: near_x, 4: near_y_and_hop, 6: diagonal})
    weight_grads(0)
    level(0, 0)
    weights[1].hop(*range(2, hops))
    weights[2].hop(0)
    chunk(1, (0, 1, 2, 3), {6: lambda: weights[2].hop(1)})
    weight_grads(1)
    level(1, 0)
    weights[2].hop(*range(2, hops))
    wires.drain("pieces")
    branch_sum, back_sum = (
        PlaneSum(wires, arena, base, rows, r.cores.at[i], r.diag.at[i], r.sides.at[i], "plane")
        for i, base in enumerate((branch_base, back_base))
    )

    def add_core(one, k):
        stage = r.core_stage.at[0, pl.ds(0, rows)]
        one.fetch_core(k, stage, r.local_sems.at[6]).wait()
        one.add_core(k, stage)

    def send_core(k):
        back_sum.send_core(k)
        branch_sum.send_core(k)

    def after_diagonal():
        send_core(3)

    def after_x():
        send_core(1)
        add_core(back_sum, 3)
        back_sum.send_diag()

    def after_y():
        send_core(2)
        add_core(back_sum, 1)
        back_sum.send_x()

    chunk(2, (3, 1, 2, 0), {2: after_diagonal, 4: after_x, 6: after_y})
    send_core(0)
    add_core(back_sum, 2)
    back_sum.send_y()
    add_core(back_sum, 0)
    wires.drain("tokens", "cotangent")
    weight_grads(2)
    get_output = load(r.output_kept, arena.at[pl.ds(output_again, QD)], 2)
    get_cotangent = load(r.cotangent, r.branch_low, 3)
    level(2, 0)
    back_sum.send_second()
    level(0, *inner_steps)
    add_core(branch_sum, 3)
    branch_sum.send_diag()
    add_core(branch_sum, 1)
    branch_sum.send_x()
    add_core(branch_sum, 2)
    branch_sum.send_y()
    add_core(branch_sum, 0)
    grad_normed = back_sum.total()
    middle = r.middle[...]
    grad_middle, gain_two = norm_backward(
        middle, norm_scale(middle), r.gains_full[1:2, :], grad_normed
    )
    get_cotangent.wait()
    r.grad_middle[...] = grad_middle + r.branch_low[...].astype(F32)
    r.branch_low[...] = r.grad_middle[...].astype(BF16)
    output_sum, qkv_sum = (
        SlotSum(
            wires,
            n_dp,
            arena,
            base,
            size,
            cores,
            diag,
            sides,
            land,
            tag,
            [r.core_stage.at[k, pl.ds(0, n_dp * size)] for k in range(2)],
            [r.local_sems.at[6 + k] for k in range(2)],
        )
        for base, size, cores, diag, sides, land, tag in (
            (0, share_out, r.output_cores, r.output_diag, r.output_sides, r.output_land, "output"),
            (n_all * share_out, folded, r.qkv_cores, r.qkv_diag, r.qkv_sides, r.qkv_land, "qkv"),
        )
    )
    gains_sum = SlotSum(
        wires, n_dp, r.gain_slots, 0, 8, r.gain_cores, r.gain_diag, r.gain_sides, r.gain_land, "gains"
    )
    for j in range(n_dp):
        first = 8 * share_out * j
        part = dot_tn(r.mixture[:, first : first + 8 * share_out], r.branch_low[...]).astype(BF16)
        for k in range(4):
            for e in range(2):
                slot = ((e * 4 + k) * n_dp + j) * share_out
                inner = (k * 2 + e) * share_out
                arena[slot : slot + share_out, :] = part[inner : inner + share_out, :]
    output_sum.send_core()
    level(1, *inner_steps)
    for one in chain_sums[0]:
        one.send_near()
    for one in chain_sums[1]:
        one.send_near()
    get_output.wait()
    r.grad_mixture[...] = dot_nt(
        r.branch_low[...], arena[output_again : output_again + QD, :]
    ).astype(BF16)
    r.grad_window[...] = jnp.zeros_like(r.grad_window)

    def head_back(h, carry):
        mine = pl.ds(pl.multiple_of(h * HD, HD), HD)
        probs = jnp.exp(scores_of(h) - r.log_totals[h])
        grad_mixture = r.grad_mixture[:, mine]
        grad_probs = dot_nt(grad_mixture, r.window[:, HD : 2 * HD])
        row_dot = jnp.sum(probs * grad_probs, axis=-1, keepdims=True)
        grad_scores = (probs * (grad_probs - row_dot)).astype(BF16)
        grad_queries = dot_nn(grad_scores, r.window[:, 0:HD]) * scale
        r.grad_projected[:, mine] = grad_queries.astype(BF16)
        r.grad_window[:, 0:HD] += dot_tn(grad_scores, r.queries[:, mine]) * scale
        r.grad_window[:, HD : 2 * HD] += dot_tn(probs.astype(BF16), grad_mixture)
        return carry

    lax.fori_loop(0, HQ, head_back, 0)
    r.window_out[...] = r.grad_window[0:WINDOW, :].astype(BF16)
    later = []
    for distance in range(1, reach + 1):
        after, before = me + distance, me - distance
        index = kv_index + reach + distance - 1
        first = WINDOW - distance * rows
        wires.send(
            r.window_out.at[pl.ds(first, rows)],
            r.window_in.at[distance - 1],
            device_at(jnp.clip(before, 0, n_all - 1)),
            index,
            before >= 0,
            "window",
        )
        source = device_at(jnp.clip(after, 0, n_all - 1))
        later.append((r.window_in.at[distance - 1], source, index, after <= n_all - 1))
    output_sum.send_first()
    branch_sum.send_second()

    def qkv_grads(first, count):
        def tile(index, carry):
            here = pl.ds(pl.multiple_of(index * 128, 128), 128)
            there = slice(first, first + count)
            out = dot_tn(r.normed[:, here], r.grad_projected[:, there]).astype(BF16)
            r.qkv_full[here, there] = out
            return carry

        lax.fori_loop(0, features // 128, tile, 0)

    r.grad_normed[...] = dot_nt(r.grad_projected[:, 0:QD], r.qkv_full[:, 0:QD])
    qkv_grads(0, QD)
    for arrival in later:
        wires.wait(*arrival)

        @pl.when(arrival[3])
        def _(arrival=arrival):
            r.grad_window[WINDOW:, :] += arrival[0][...].astype(F32)

    r.grad_projected[:, QD:] = r.grad_window[WINDOW:, :].astype(BF16)
    grad_normed = r.grad_normed[...] + dot_nt(r.grad_projected[:, QD:], r.qkv_full[:, QD:])
    r.grad_normed[...] = grad_normed
    qkv_grads(QD, wide - QD)
    for d, j, k, e in blocks:
        slot = n_all * share_out + ((e * 4 + k) * n_dp + j) * folded
        fold(arena, slot, r.qkv_full, share * d, share)
    qkv_sum.send_core()
    output_sum.send_second()
    inputs = r.tokens[...].astype(F32)
    grad_inputs, gain_one = norm_backward(
        inputs, norm_scale(inputs), r.gains_full[0:1, :], r.grad_normed[...]
    )
    r.grad_middle[...] = r.grad_middle[...] + grad_inputs
    put_input_grad = load(r.grad_middle, r.input_grad, 0)
    qkv_sum.send_first()
    r.gain_slots[...] = jnp.zeros_like(r.gain_slots)
    for d, j, k, e in blocks:
        slot = ((e * 4 + k) * n_dp + j) * 8
        for row, gain in enumerate((gain_one, gain_two)):
            r.gain_slots[slot + row : slot + row + 1, 0:share] = gain[:, share * d : share * (d + 1)]
    gains_sum.send_core()
    level(2, *inner_steps)
    for one in chain_sums[2]:
        one.send_near()

    def give_back(number):
        for one in chain_sums[number]:
            one.receive()
        for one in chain_sums[number]:
            one.collect()
        size = 2 * chunks[number][2]
        r.stage[0:plane_rows, 0:size] = expand_place(number)(q)[...]
        for group in range(8):
            r.pieces_out[group, :, columns(number)] = r.stage[
                share * group : share * (group + 1), 0:size
            ]
        back = exchange(number, "give_back")
        first, count, _ = chunks[number]
        used = min(first + count, ff_block) - first
        r.sum_contract[first : first + used, :] = contract_place(number)(q)[...][0:used, :]
        return back

    def take_back(chosen):
        backs[chosen].finish()
        for group, source, size, number, place in pieces:
            if number == chosen:
                at = starts[number] + place
                r.sum_expand[:, source : source + size] = r.pieces_in[group, :, at : at + size]

    gains_sum.send_first()
    qkv_sum.send_second()
    output_sum.add_sides()
    output_sum.chain.send_near()
    backs = [give_back(0)]
    gains_sum.send_second()
    r.block_out[...] = (r.middle[...] + branch_sum.total()).astype(BF16)
    for one in (qkv_sum, gains_sum):
        one.add_sides()
        one.chain.send_near()
    backs.append(give_back(1))
    take_back(0)
    output_sum.chain.receive()
    output_sum.chain.collect()
    r.sum_output[...] = output_sum.chain.own(q)[...].astype(F32)
    backs.append(give_back(2))
    take_back(1)
    for one in (qkv_sum, gains_sum):
        one.chain.receive()
        one.chain.collect()
    r.own_qkv[...] = qkv_sum.chain.own(q)[...]
    unfold(r.sum_qkv, 0, share, r.own_qkv, 0)
    r.sum_gains[...] = gains_sum.chain.own(q)[...]
    take_back(2)
    put_input_grad.wait()
    wires.drain()


def run_block(n_dp, tokens, cotangent, qkv, output, gains, expand, contract):
    n_all = 8 * n_dp
    rows, features = tokens.shape
    share, wide = qkv.shape
    share_out = output.shape[0]
    ff_block = contract.shape[0]
    plane_rows = 8 * share
    folded = share + share // 3
    padded, width, chunks, pieces = hidden_layout(n_dp, ff_block)
    largest = max(size for _, _, size in chunks)
    hbm, vmem = pl.BlockSpec(memory_space=pl.ANY), pl.BlockSpec(memory_space=pltpu.VMEM)
    outs = {
        "block_out": ((rows, features), BF16),
        "input_grad": ((rows, features), F32),
        "sum_qkv": ((share, wide), F32),
        "sum_output": ((share_out, features), F32),
        "sum_gains": ((8, 128), F32),
        "sum_expand": (expand.shape, BF16),
        "sum_contract": ((ff_block, features), BF16),
    }
    lands = {
        "land_%d" % i: ((2 * n_dp + 1, plane_rows, 2 * size), BF16)
        for i, (_, _, size) in enumerate(chunks)
    }
    for i, (_, count, _) in enumerate(chunks):
        lands["land_c%d" % i] = ((2 * n_dp + 1, count, features), BF16)
    lands["cores"] = ((2, 4, rows, features), BF16)
    lands["output_kept"] = ((QD, features), BF16)
    lands["output_cores"] = ((4 * n_dp * share_out, features), BF16)
    lands["qkv_cores"] = ((4 * n_dp * folded, features), BF16)

    def sums(name, size, columns, dtype):
        return {
            name + "_diag": ((n_dp * size, columns), dtype),
            name + "_sides": ((2 * n_dp * size, columns), dtype),
            name + "_land": (((2 * n_dp + 1) * size, columns), dtype),
        }

    scratch = {
        "arena": ((32 * rows, features), BF16),
        **{"expand_%d" % i: ((features, 2 * size), BF16) for i, (_, _, size) in enumerate(chunks)},
        **{"contract_%d" % i: ((size, features), BF16) for i, (_, _, size) in enumerate(chunks)},
        "hidden": ((8 * rows, largest), BF16),
        "grad_gate_up": ((8 * rows, 2 * largest), BF16),
        "stage": ((plane_rows, max(features, 2 * largest)), BF16),
        "core_stage": ((2, max(rows, n_dp * folded), features), BF16),
        "diag": ((2, 2, rows // 2, features), BF16),
        "sides": ((2, 2, rows, features), BF16),
        "pieces_out": ((8, share, 2 * width), BF16),
        "pieces_in": ((8, share, 2 * width), BF16),
        "grad_middle": ((rows, features), F32),
        "grad_normed": ((rows, features), F32),
        "own_qkv": ((folded, features), BF16),
        "gain_slots": ((n_all * 8, 128), F32),
        "gains_full": ((8, features), F32),
        "qkv_full": ((features, wide), BF16),
        "normed": ((rows, features), BF16),
        "queries": ((rows, QD), BF16),
        "window": ((WINDOW + rows, 2 * HD), BF16),
        "log_totals": ((HQ, rows, 1), F32),
        "mixture": ((rows, QD), BF16),
        "middle": ((rows, features), F32),
        "branch_low": ((rows, features), BF16),
        "grad_mixture": ((rows, QD), BF16),
        "grad_window": ((WINDOW + rows, 2 * HD), F32),
        "window_out": ((WINDOW, 2 * HD), BF16),
        "window_in": ((WINDOW // rows, rows, 2 * HD), BF16),
        "grad_projected": ((rows, wide), BF16),
        **sums("output", share_out, features, BF16),
        **sums("qkv", folded, features, BF16),
        **sums("gain", 8, 128, F32),
        "gain_cores": ((4 * n_dp * 8, 128), F32),
    }
    names = (*INPUTS, *outs, *lands, *scratch, "local_sems", "send_sems", "recv_sems")
    results = pl.pallas_call(
        functools.partial(block_kernel, n_dp, names),
        out_shape=[jax.ShapeDtypeStruct(*s) for s in (*outs.values(), *lands.values())],
        in_specs=[vmem, hbm, vmem, vmem, vmem, hbm, hbm],
        out_specs=[hbm if name == "input_grad" else vmem for name in outs] + [hbm] * len(lands),
        scratch_shapes=[pltpu.VMEM(*s) for s in scratch.values()]
        + [
            pltpu.SemaphoreType.DMA((11 + 4 * (n_dp // 2 + 1),)),
            pltpu.SemaphoreType.DMA((WIRES,)),
            pltpu.SemaphoreType.DMA((WIRES,)),
        ],
        compiler_params=pltpu.CompilerParams(
            collective_id=0, has_side_effects=True, vmem_limit_bytes=VMEM_LIMIT
        ),
        name="transformer_block",
    )(tokens, cotangent, qkv, output, gains, expand, contract)
    return results[: len(outs)]


def adamw_update(weight, gradient, first, second, rate, decay_rate):
    mean_new = BETA_FIRST * first + (1.0 - BETA_FIRST) * gradient
    square_new = BETA_SECOND * second + (1.0 - BETA_SECOND) * gradient * gradient
    mean_hat = mean_new / (1.0 - BETA_FIRST**STEP)
    square_hat = square_new / (1.0 - BETA_SECOND**STEP)
    updated = weight - rate * (
        mean_hat / (jnp.sqrt(square_hat) + ADAM_EPSILON) + decay_rate * weight
    )
    return (updated, mean_new, square_new)


def shards_kernel(tokens, cotangent, *arguments):
    weights, firsts, seconds = arguments[:5], arguments[5:10], arguments[10:15]
    qkv, output, expand, contract, gains = weights
    share = gains.shape[1]
    gains_tile = jnp.pad(gains.astype(F32), ((0, 6), (0, 128 - share)))
    block_out, input_grad, *sums = run_block(
        lax.axis_size("ctx") // 2, tokens, cotangent, qkv, output, gains_tile, expand, contract
    )
    sum_qkv, sum_output, sum_gains, sum_expand, sum_contract = sums
    gradients = (sum_qkv, sum_output, sum_expand, sum_contract, sum_gains[:2, :share])
    rates = (RATE_MATRIX,) * 4 + (RATE_GAINS,)
    decays = (WEIGHT_DECAY,) * 4 + (0.0,)
    updates = [
        adamw_update(weight.astype(F32), gradient.astype(F32), first, second, rate, decay)
        for weight, gradient, first, second, rate, decay in zip(
            weights, gradients, firsts, seconds, rates, decays
        )
    ]
    return (
        block_out,
        input_grad,
        *(new for new, _, _ in updates),
        *(mean for _, mean, _ in updates),
        *(square for _, _, square in updates),
    )


def passed_along(block, axis, distance):
    devices = range(lax.axis_size(axis))
    route = [(i - distance, i) for i in devices if i - distance in devices]
    return lax.ppermute(block, axis, route)


def norm_forward(values, gain_row):
    scale = norm_scale(values)
    return (values * scale * gain_row, scale)


def shards_plain(
    tokens,
    cotangent,
    qkv_weight,
    output_weight,
    expand_weight,
    contract_weight,
    norm_gains,
    first_qkv,
    first_output,
    first_expand,
    first_contract,
    first_gains,
    second_qkv,
    second_output,
    second_expand,
    second_contract,
    second_gains,
):
    tok_dev = tokens.shape[0]
    n_fsdp = lax.axis_size("fsdp")
    n_ctx = lax.axis_size("ctx")
    ff_block = FF // (n_ctx * n_fsdp)
    score_scale = 1.0 / math.sqrt(HD)
    fsdp_index = lax.axis_index("fsdp")
    ctx_index = lax.axis_index("ctx")
    qkv_full, output_full, gains_full = (
        lax.all_gather(qkv_weight, ("ctx", "fsdp"), axis=0, tiled=True),
        lax.all_gather(output_weight, ("ctx", "fsdp"), axis=0, tiled=True),
        lax.all_gather(norm_gains, ("ctx", "fsdp"), axis=1, tiled=True),
    )
    arranged = expand_weight.reshape(expand_weight.shape[0], 2, n_ctx, n_fsdp, ff_block)
    arranged = lax.all_to_all(arranged, "fsdp", split_axis=3, concat_axis=0, tiled=True)
    arranged = arranged.reshape(arranged.shape[0], 2 * n_ctx * ff_block)
    expand_use, contract_use = (
        lax.all_gather(arranged, "ctx", axis=0, tiled=True),
        lax.all_gather(contract_weight, "ctx", axis=0, tiled=True),
    )
    width = n_ctx * ff_block
    gains_float = gains_full.astype(jnp.float32)
    inputs = tokens.astype(jnp.float32)
    normed, scale_one = norm_forward(inputs, gains_float[0])
    normed_low = normed.astype(jnp.bfloat16)
    projected = jnp.dot(normed_low, qkv_full, preferred_element_type=jnp.float32).astype(
        jnp.bfloat16
    )
    queries = projected[:, : HQ * HD].reshape(tok_dev, HQ, HD)
    key_value = projected[:, HQ * HD :]
    reach = (WINDOW + tok_dev - 1) // tok_dev
    earlier_pieces = []
    for distance in range(reach, 0, -1):
        earlier_pieces.append(passed_along(key_value, ("ctx", "fsdp"), distance))
    earlier = jnp.concatenate(earlier_pieces, axis=0)
    window_kv = jnp.concatenate([earlier, key_value], axis=0)
    key_rows = window_kv[:, :HD]
    value_rows = window_kv[:, HD:]
    offset = (ctx_index * n_fsdp + fsdp_index) * tok_dev
    row_index = lax.broadcasted_iota(jnp.int32, (tok_dev, WINDOW + tok_dev), 0)
    col_index = lax.broadcasted_iota(jnp.int32, (tok_dev, WINDOW + tok_dev), 1)
    visible = (
        (col_index > row_index) & (col_index <= row_index + WINDOW) & (col_index + offset >= WINDOW)
    )

    def masked_scores():
        raw_scores = (
            jnp.einsum("qhd,kd->hqk", queries, key_rows, preferred_element_type=jnp.float32)
            * score_scale
        )
        return jnp.where(visible[None], raw_scores, MASKED_SCORE)

    scores = masked_scores()
    log_total = jax.nn.logsumexp(scores, axis=-1, keepdims=True)
    probs_low = jnp.exp(scores - log_total).astype(jnp.bfloat16)
    mixture = jnp.einsum("hqk,kd->qhd", probs_low, value_rows, preferred_element_type=jnp.float32)
    mixture_low = mixture.reshape(tok_dev, HQ * HD).astype(jnp.bfloat16)
    middle = inputs + jnp.dot(mixture_low, output_full, preferred_element_type=jnp.float32)
    normed_two, scale_two = norm_forward(middle, gains_float[1])
    normed_two_low = normed_two.astype(jnp.bfloat16)
    ffn_input, ffn_cotangent = (
        lax.all_gather(normed_two_low, "fsdp", axis=0, tiled=True),
        lax.all_gather(cotangent, "fsdp", axis=0, tiled=True),
    )
    gate_up = jnp.dot(ffn_input, expand_use, preferred_element_type=jnp.float32)
    gate_part = gate_up[:, :width]
    up_part = gate_up[:, width:]
    activated, gelu_back = jax.vjp(functools.partial(jax.nn.gelu, approximate=True), gate_part)
    hidden_low = (activated * up_part).astype(jnp.bfloat16)
    branch_two = jnp.dot(hidden_low, contract_use, preferred_element_type=jnp.float32)
    branch_two = lax.psum_scatter(
        branch_two.astype(jnp.bfloat16), "fsdp", scatter_dimension=0, tiled=True
    ).astype(jnp.float32)
    result = middle + branch_two
    block_out = result.astype(jnp.bfloat16)
    grad_result = cotangent.astype(jnp.float32)
    grad_contract = jnp.einsum(
        "tf,td->fd", hidden_low, ffn_cotangent, preferred_element_type=jnp.float32
    )
    grad_hidden = jnp.einsum(
        "td,fd->tf", ffn_cotangent, contract_use, preferred_element_type=jnp.float32
    )
    (grad_gate,) = gelu_back(grad_hidden * up_part)
    grad_gate_up = jnp.concatenate([grad_gate, grad_hidden * activated], axis=1).astype(
        jnp.bfloat16
    )
    grad_expand = jnp.einsum(
        "td,tf->df", ffn_input, grad_gate_up, preferred_element_type=jnp.float32
    )
    grad_normed_two = jnp.einsum(
        "tf,df->td", grad_gate_up, expand_use, preferred_element_type=jnp.float32
    )
    grad_normed_two = lax.psum_scatter(grad_normed_two, "fsdp", scatter_dimension=0, tiled=True)
    part_expand, sum_contract = (
        lax.psum_scatter(
            grad_expand.astype(jnp.bfloat16), "ctx", scatter_dimension=0, tiled=True
        ).astype(jnp.float32),
        lax.psum_scatter(
            grad_contract.astype(jnp.bfloat16), "ctx", scatter_dimension=0, tiled=True
        ).astype(jnp.float32),
    )
    part_expand = part_expand.reshape(part_expand.shape[0], 2, n_ctx, 1, ff_block)
    sum_expand = lax.all_to_all(part_expand, "fsdp", split_axis=0, concat_axis=3, tiled=True)
    sum_expand = sum_expand.reshape(sum_expand.shape[0], 2 * FF)
    grad_norm_two, gain_grad_two = norm_backward(middle, scale_two, gains_float[1], grad_normed_two)
    grad_middle = grad_result + grad_norm_two
    grad_branch = grad_middle.astype(jnp.bfloat16)
    grad_output = jnp.einsum(
        "tc,td->cd", mixture_low, grad_branch, preferred_element_type=jnp.float32
    )
    grad_mixture = jnp.einsum(
        "td,cd->tc", grad_branch, output_full, preferred_element_type=jnp.float32
    )
    grad_mixture = grad_mixture.astype(jnp.bfloat16).reshape(tok_dev, HQ, HD)
    again_scores = masked_scores()
    again_probs = jnp.exp(again_scores - log_total)
    again_low = again_probs.astype(jnp.bfloat16)
    grad_probs = jnp.einsum(
        "qhd,kd->hqk", grad_mixture, value_rows, preferred_element_type=jnp.float32
    )
    row_dot = jnp.sum(again_probs * grad_probs, axis=-1, keepdims=True)
    grad_scores = (again_probs * (grad_probs - row_dot)).astype(jnp.bfloat16)
    grad_queries = (
        jnp.einsum("hqk,kd->qhd", grad_scores, key_rows, preferred_element_type=jnp.float32)
        * score_scale
    )
    grad_keys = (
        jnp.einsum("hqk,qhd->kd", grad_scores, queries, preferred_element_type=jnp.float32)
        * score_scale
    )
    grad_values = jnp.einsum(
        "hqk,qhd->kd", again_low, grad_mixture, preferred_element_type=jnp.float32
    )
    grad_window = jnp.concatenate([grad_keys, grad_values], axis=1)
    grad_key_value = grad_window[WINDOW:]
    grad_earlier = jnp.concatenate(
        [jnp.zeros((reach * tok_dev - WINDOW, 2 * HD), jnp.float32), grad_window[:WINDOW]], axis=0
    )
    for position in range(reach):
        piece = grad_earlier[position * tok_dev : (position + 1) * tok_dev]
        grad_key_value = grad_key_value + passed_along(
            piece.astype(jnp.bfloat16), ("ctx", "fsdp"), position - reach
        ).astype(piece.dtype)
    grad_projected = jnp.concatenate(
        [grad_queries.reshape(tok_dev, HQ * HD), grad_key_value], axis=1
    ).astype(jnp.bfloat16)
    grad_qkv = jnp.einsum(
        "td,tc->dc", normed_low, grad_projected, preferred_element_type=jnp.float32
    )
    grad_normed = jnp.einsum(
        "tc,dc->td", grad_projected, qkv_full, preferred_element_type=jnp.float32
    )
    grad_norm_one, gain_grad_one = norm_backward(inputs, scale_one, gains_float[0], grad_normed)
    input_grad = grad_middle + grad_norm_one
    grad_gains = jnp.concatenate([gain_grad_one, gain_grad_two], axis=0)
    sum_qkv, sum_output, sum_gains = (
        lax.psum_scatter(grad_qkv, ("ctx", "fsdp"), scatter_dimension=0, tiled=True),
        lax.psum_scatter(grad_output, ("ctx", "fsdp"), scatter_dimension=0, tiled=True),
        lax.psum_scatter(grad_gains, ("ctx", "fsdp"), scatter_dimension=1, tiled=True),
    )
    new_qkv, mean_qkv, square_qkv = adamw_update(
        qkv_weight.astype(jnp.float32), sum_qkv, first_qkv, second_qkv, RATE_MATRIX, WEIGHT_DECAY
    )
    new_output, mean_output, square_output = adamw_update(
        output_weight.astype(jnp.float32),
        sum_output,
        first_output,
        second_output,
        RATE_MATRIX,
        WEIGHT_DECAY,
    )
    new_expand, mean_expand, square_expand = adamw_update(
        expand_weight.astype(jnp.float32),
        sum_expand,
        first_expand,
        second_expand,
        RATE_MATRIX,
        WEIGHT_DECAY,
    )
    new_contract, mean_contract, square_contract = adamw_update(
        contract_weight.astype(jnp.float32),
        sum_contract,
        first_contract,
        second_contract,
        RATE_MATRIX,
        WEIGHT_DECAY,
    )
    new_gains, mean_gains, square_gains = adamw_update(
        norm_gains.astype(jnp.float32), sum_gains, first_gains, second_gains, RATE_GAINS, 0.0
    )
    return (
        block_out,
        input_grad,
        new_qkv,
        new_output,
        new_expand,
        new_contract,
        new_gains,
        mean_qkv,
        mean_output,
        mean_expand,
        mean_contract,
        mean_gains,
        square_qkv,
        square_output,
        square_expand,
        square_contract,
        square_gains,
    )


def shards(*arguments):
    plane_rows = 8 * arguments[4].shape[0]
    return (shards_kernel if plane_rows % 16 == 0 else shards_plain)(*arguments)


def solution(mesh):
    rows, columns = P(("ctx", "fsdp"), None), P(None, ("ctx", "fsdp"))
    in_specs = (rows,) * 6 + (columns,) + ((rows,) * 4 + (columns,)) * 2
    out_specs = (rows,) * 2 + ((rows,) * 4 + (columns,)) * 3
    return jax.shard_map(shards, mesh=mesh, in_specs=in_specs, out_specs=out_specs, check_vma=False)
```
